32 devices in a mesh: dp: 8 (over z, x), fsdp: 4 (over y, core).
Axes of the slice: x: 2, y: 2, z: 4, core: 2. Of those that a mesh axis runs over, the one named last changes fastest.
Arguments:
- tokens: bfloat16 [16384, 512], P(('dp', 'fsdp')), may hold values from -6 to 6
- lengths: int32 [32], P(('dp', 'fsdp')), may hold values from 256 to 512, as said below
- norm_gains: bfloat16 [2, 2, 512], P(None, None, ('dp', 'fsdp')), may hold values from 0.5 to 1.5
- norm_shifts: bfloat16 [2, 2, 512], P(None, None, ('dp', 'fsdp')), may hold values from -1.796875 to 1.796875
- w_qkv: bfloat16 [2, 512, 1536], P(None, ('dp', 'fsdp')), may hold values from -0.25 to 0.25
- b_qkv: bfloat16 [2, 1536], P(None, ('dp', 'fsdp')), may hold values from -1.796875 to 1.796875
- w_attn: bfloat16 [2, 512, 512], P(None, ('dp', 'fsdp')), may hold values from -2 to 2
- blend_weights: bfloat16 [2, 3, 512], P(None, None, ('dp', 'fsdp')), may hold values from 0.5 to 1.5
- w_in: bfloat16 [2, 512, 2048], P(None, ('dp', 'fsdp')), may hold values from -0.25 to 0.25
- b_in: bfloat16 [2, 2048], P(None, ('dp', 'fsdp')), may hold values from -1.796875 to 1.796875
- w_out: bfloat16 [2, 2048, 512], P(None, ('dp', 'fsdp')), may hold values from -0.125 to 0.125
- out_bias: bfloat16 [2, 2, 512], P(None, None, ('dp', 'fsdp')), may hold values from -1.796875 to 1.796875
- cotangent: bfloat16 [16384, 512], P(('dp', 'fsdp')), may hold values from -6 to 6
Outputs:
- mixed_out: bfloat16 [16384, 512], P(('dp', 'fsdp'))
- grad_tokens: float32 [16384, 512], P(('dp', 'fsdp'))
- grad_norm_gains: float32 [2, 2, 512], P(None, None, ('dp', 'fsdp'))
- grad_norm_shifts: float32 [2, 2, 512], P(None, None, ('dp', 'fsdp'))
- grad_w_qkv: float32 [2, 512, 1536], P(None, ('dp', 'fsdp'))
- grad_b_qkv: float32 [2, 1536], P(None, ('dp', 'fsdp'))
- grad_w_attn: float32 [2, 512, 512], P(None, ('dp', 'fsdp'))
- grad_blend_weights: float32 [2, 3, 512], P(None, None, ('dp', 'fsdp'))
- grad_w_in: float32 [2, 512, 2048], P(None, ('dp', 'fsdp'))
- grad_b_in: float32 [2, 2048], P(None, ('dp', 'fsdp'))
- grad_w_out: float32 [2, 2048, 512], P(None, ('dp', 'fsdp'))
- grad_out_bias: float32 [2, 2, 512], P(None, None, ('dp', 'fsdp'))
The draws below stay inside these ranges and needn't reach their ends.
Inputs may be any that keep to these rules, and one draw needn't show every extreme that they name: lengths[i] counts the true tokens of the item on device i, rows 0 to lengths[i] - 1 of its 512 rows; some item has exactly 512 and some exactly 256.
All inputs are finite; a program needn't handle non-finite values.
Results may differ from the reference program's by a relative error of at most 0.015.
Values may be sent and summed in bfloat16 or wider, within the bound.
A program may use at most 192 MiB of HBM per device.

```python
import jax
import jax.numpy as jnp
from jax import lax

D = 512
FF = 2048
HD = 64
BAND = 30
LAYERS = 2
SEQ = 512
ITEMS = 32
TOKENS = 16384


def draw_lengths(key, part):
    key = jax.random.fold_in(key, 7)
    first_key, second_key = jax.random.split(key)
    drawn = jax.random.randint(first_key, (ITEMS,), SEQ // 2, SEQ + 1)
    order = jax.random.permutation(second_key, ITEMS)
    drawn = drawn.at[order[0]].set(SEQ)
    drawn = drawn.at[order[1]].set(SEQ // 2)
    return drawn.astype(jnp.int32)


def block_levels(own_key, extent, cuts, low, top_value):
    factor_of = 1.0
    for position, blocks in cuts:
        draws = jax.random.uniform(jax.random.fold_in(jax.random.fold_in(own_key, 6), position), (blocks,), jnp.float32, low / len(cuts), top_value / len(cuts))
        factor_of = factor_of * jnp.repeat(jnp.exp(draws), extent[position] // blocks).reshape((-1,) + (1,) * (len(extent) - 1 - position))
    return factor_of


def bell_draw(rng, shape, spread, limit, cuts=(), kind=jnp.bfloat16):
    values = jax.random.normal(rng, shape, jnp.float32) * spread
    if len(cuts) > 0:
        values = block_levels(rng, shape, cuts, -0.22, 0.18) * values
    return jnp.clip(values, min=-limit, max=limit).astype(kind)


def setup_inputs(seed: int = 0) -> dict:
    streams_of = jax.random.split(jax.random.key(seed), 14)
    tokens = bell_draw(streams_of[0], (TOKENS, D), 1.0, 6.0, ((0, 32),))
    lengths = draw_lengths(jax.random.fold_in(streams_of[13], 71), 0)
    norm_gains = jnp.clip(1.0 + 0.1 * jax.random.normal(streams_of[2], (LAYERS, 2, D), jnp.float32), 0.5, 1.5).astype(jnp.bfloat16)
    norm_shifts = bell_draw(streams_of[3], (LAYERS, 2, D), 0.3, 1.796875, ((2, 32),))
    w_qkv = bell_draw(streams_of[4], (LAYERS, D, 3 * D), D ** -0.5, 0.25, ((1, 32),))
    b_qkv = bell_draw(streams_of[5], (LAYERS, 3 * D), 0.3, 1.796875, ((1, 32),))
    w_attn = bell_draw(streams_of[6], (LAYERS, D, D), (D // (2 * BAND + 1)) ** -0.5, 2.0, ((1, 32),))
    blend_weights = jnp.clip(0.5 + 1.0 * jax.random.uniform(streams_of[7], (LAYERS, 3, D), jnp.float32) ** block_levels(streams_of[7], (LAYERS, 3, D), ((2, 32),), -0.2, 0.2), 0.5, 1.5).astype(jnp.bfloat16)
    w_in = bell_draw(streams_of[8], (LAYERS, D, FF), D ** -0.5, 0.25, ((1, 32),))
    b_in = bell_draw(streams_of[9], (LAYERS, FF), 0.3, 1.796875, ((1, 32),))
    w_out = bell_draw(streams_of[10], (LAYERS, FF, D), FF ** -0.5, 0.125, ((1, 32),))
    out_bias = bell_draw(streams_of[11], (LAYERS, 2, D), 0.3, 1.796875, ((2, 32),))
    cotangent = bell_draw(streams_of[12], (TOKENS, D), 1.0, 6.0, ((0, 32),))
    return {"tokens": tokens, "lengths": lengths, "norm_gains": norm_gains, "norm_shifts": norm_shifts, "w_qkv": w_qkv, "b_qkv": b_qkv, "w_attn": w_attn, "blend_weights": blend_weights, "w_in": w_in, "b_in": b_in, "w_out": w_out, "out_bias": out_bias, "cotangent": cotangent}


EPSILON = 1e-05
MARGIN = 64
HIGHEST = lax.Precision.HIGHEST

@jax.custom_vjp
def low(v):
    return lax.optimization_barrier(v.astype(jnp.bfloat16)).astype(jnp.float32)

@jax.custom_vjp
def low_back(v):
    return v

def low_keep(v):
    return (low(v), None)

def low_pass(kept, grad):
    return (grad,)

def back_keep(v):
    return (v, None)

def back_low(kept, grad):
    return (low(grad),)
low.defvjp(low_keep, low_pass)
low_back.defvjp(back_keep, back_low)

def norm_rows(row_data, gain_row, shift_row):
    centered = row_data - lax.optimization_barrier(jnp.mean(row_data, axis=-1, keepdims=True))
    variance = lax.optimization_barrier(jnp.mean(centered * centered, axis=-1, keepdims=True))
    return centered * lax.rsqrt(variance + EPSILON) * gain_row + shift_row

def band_keep(first_row, block_rows, window, length):
    row_pos = first_row + jnp.arange(block_rows, dtype=jnp.int32)
    col_pos = first_row - MARGIN + jnp.arange(window, dtype=jnp.int32)
    offset = col_pos[None, :] - row_pos[:, None]
    inside = (jnp.abs(offset) <= BAND) & (col_pos[None, :] >= 0)
    return inside & ((col_pos[None, :] < length) | (offset == 0))

def near_field(queries, keys_in, values_in, length):
    block_rows = min(512, SEQ)
    window = block_rows + 2 * MARGIN
    score_scale = HD ** (-0.5)
    head_count = queries.shape[1]
    key_pad = jnp.pad(keys_in, ((MARGIN, MARGIN), (0, 0), (0, 0)))
    value_pad = jnp.pad(values_in, ((MARGIN, MARGIN), (0, 0), (0, 0)))
    query_blocks = queries.reshape(SEQ // block_rows, block_rows, head_count, HD)
    starts = jnp.arange(SEQ // block_rows, dtype=jnp.int32) * block_rows

    def one_block(block_args):
        query_blk, first_row = block_args
        key_win = lax.dynamic_slice_in_dim(key_pad, first_row, window, 0)
        value_win = lax.dynamic_slice_in_dim(value_pad, first_row, window, 0)
        scores = jnp.einsum('qhe,khe->hqk', query_blk, key_win, precision=HIGHEST) * score_scale
        allowed = band_keep(first_row, block_rows, window, length)
        scores = jnp.where(allowed[None], scores, -1e+30)
        largest = lax.optimization_barrier(jnp.max(scores, axis=-1, keepdims=True))
        weights = jnp.exp(scores - largest)
        attention = weights / lax.optimization_barrier(jnp.sum(weights, axis=-1, keepdims=True))
        return jnp.einsum('hqk,khe->qhe', low(attention), value_win, precision=HIGHEST)
    result = lax.map(jax.checkpoint(one_block), (query_blocks, starts))
    return result.reshape(SEQ, head_count, HD)

def far_field(queries, keys_in, values_in, keep_cube, length):
    phi_query = low(jax.nn.elu(queries) + 1.0)
    phi_key = low(jax.nn.elu(keys_in) + 1.0) * keep_cube
    state_one = jnp.einsum('khe,khc->hec', phi_key, values_in, precision=HIGHEST)
    key_total = lax.optimization_barrier(jnp.sum(phi_key, axis=0))
    numerator = jnp.einsum('qhe,hec->qhc', phi_query, state_one, precision=HIGHEST)
    denominator = jnp.einsum('qhe,he->qh', phi_query, key_total, precision=HIGHEST)[..., None]
    far_elu = numerator / denominator
    tanh_query = low(jnp.tanh(queries))
    tanh_key = low(jnp.tanh(keys_in)) * keep_cube
    state_two = jnp.einsum('khe,khc->hec', tanh_key, values_in, precision=HIGHEST)
    coefficient = lax.rsqrt(HD * length.astype(jnp.float32))
    far_tanh = jnp.einsum('qhe,hec->qhc', tanh_query, state_two, precision=HIGHEST) * coefficient
    return (far_elu, far_tanh)

def layer_apply(hidden_in, keep_rows, length, params):
    gain_rows, shift_rows, qkv_weight, qkv_bias, attn_weight, blend_rows, in_weight, in_bias, out_weight, bias_rows = params
    model_width = attn_weight.shape[0]
    head_count = model_width // HD
    normed = low(norm_rows(hidden_in, gain_rows[0], shift_rows[0]))
    projected = low(low_back(jnp.dot(normed, qkv_weight, precision=HIGHEST) + qkv_bias))
    queries = projected[:, :model_width].reshape(SEQ, head_count, HD)
    keys_in = projected[:, model_width:2 * model_width].reshape(SEQ, head_count, HD)
    values_in = projected[:, 2 * model_width:].reshape(SEQ, head_count, HD)
    near_out = near_field(queries, keys_in, values_in, length).reshape(SEQ, model_width)
    far_elu, far_tanh = far_field(queries, keys_in, values_in, keep_rows[:, :, None], length)
    mixed_heads = low(low_back(blend_rows[0] * near_out + blend_rows[1] * far_elu.reshape(SEQ, model_width) + blend_rows[2] * far_tanh.reshape(SEQ, model_width)))
    attn_out = low_back(jnp.dot(mixed_heads, attn_weight, precision=HIGHEST) + bias_rows[0])
    after_attn = hidden_in + keep_rows * attn_out
    normed_two = low(norm_rows(after_attn, gain_rows[1], shift_rows[1]))
    hidden_pre = low_back(jnp.dot(normed_two, in_weight, precision=HIGHEST) + in_bias)
    activated = low(jax.nn.gelu(hidden_pre))
    ffn_out = low_back(jnp.dot(activated, out_weight, precision=HIGHEST) + bias_rows[1])
    return after_attn + keep_rows * ffn_out

def forward_all(tokens_all, lengths, params):

    def one_item(item_args):
        item_rows, length = item_args
        keep_rows = (jnp.arange(SEQ, dtype=jnp.int32) < length).astype(jnp.float32)[:, None]
        hidden = item_rows
        for layer_idx in range(LAYERS):
            hidden = layer_apply(hidden, keep_rows, length, [stacked[layer_idx] for stacked in params])
        return hidden
    return lax.map(jax.checkpoint(one_item), (tokens_all, lengths))

def reference(tokens, lengths, norm_gains, norm_shifts, w_qkv, b_qkv, w_attn, blend_weights, w_in, b_in, w_out, out_bias, cotangent):
    params = tuple((argument.astype(jnp.float32) for argument in (norm_gains, norm_shifts, w_qkv, b_qkv, w_attn, blend_weights, w_in, b_in, w_out, out_bias)))
    start_rows = tokens.astype(jnp.float32).reshape(ITEMS, SEQ, D)

    def run_layers(rows_in, *weights):
        return forward_all(rows_in, lengths, weights)
    outputs, pullback = jax.vjp(run_layers, start_rows, *params)
    gradients = pullback(cotangent.astype(jnp.float32).reshape(ITEMS, SEQ, D))
    return (outputs.reshape(TOKENS, D).astype(jnp.bfloat16), gradients[0].reshape(TOKENS, D), gradients[1], gradients[2], gradients[3], gradients[4], gradients[5], gradients[6], gradients[7], gradients[8], gradients[9], gradients[10])
```

```python
import functools
import itertools
import jax
import jax.numpy as jnp
from jax import lax
from jax.experimental import pallas as pl
from jax.experimental.pallas import tpu as pltpu
from jax.sharding import PartitionSpec as P

HD = 64
BAND = 30
EPSILON = 1e-05
MESH = pl.DeviceIdType.MESH
F32 = jnp.float32
BF16 = jnp.bfloat16
GROUP = 16
TILE = 128
PAD = 32
WINDOW = TILE + 2 * PAD
TWINS = {"acc_t": "acc", "gm_t": "normed"}
ROWS = 64
GELU_C = 0.7978845608028654
GELU_A = 0.044715
GAIN, SHIFT, BQKV, BLEND, BIN, OBIAS, VROWS = 0, 2, 4, 7, 10, 14, 16


def nn(a, b):
    return jnp.dot(a, b, preferred_element_type=F32)


def nt(a, b):
    return lax.dot_general(a, b, (((1,), (1,)), ((), ())), preferred_element_type=F32)


def split(a):
    high = a.astype(BF16)
    return high, (a - high.astype(F32)).astype(BF16)


def row_index(shape):
    return lax.broadcasted_iota(jnp.int32, shape, 0)


def col_index(shape):
    return lax.broadcasted_iota(jnp.int32, shape, 1)


def head_diag(a):
    return jnp.where((row_index(a.shape) < HD) == (col_index(a.shape) < HD), a, 0.0)


def spread(tile):
    top, bottom = tile[:HD], tile[HD:]
    zero = jnp.zeros_like(top)
    return jnp.concatenate(
        [jnp.concatenate([top, zero], axis=1), jnp.concatenate([zero, bottom], axis=1)], axis=0
    )


def fold(wide):
    half = wide.shape[1] // 2
    return jnp.concatenate([wide[:HD, :half], wide[HD:, half:]], axis=0)


def col_sum(a):
    return jnp.sum(a, axis=0, keepdims=True)


GBLEND = 64


def group_shape(width, hidden):
    first = hidden // width
    return (first, width // GROUP // first // 4, 2, 2)


class Net:
    def __init__(self, layers, seq, width, hidden, length, r):
        self.layers, self.seq, self.width, self.hidden = layers, seq, width, hidden
        self.pairs = width // (2 * HD)
        self.tiles = seq // TILE
        self.length = length
        self.padded = seq + TILE
        self.ff_blocks = hidden // width
        self.groups = group_shape(width, hidden)
        self.__dict__.update(r)
        for name, twin in TWINS.items():
            if name not in r:
                setattr(self, name, r[twin])

    @staticmethod
    def scratch(layers, seq, width, hidden):
        padded = seq + TILE
        pairs = width // (2 * HD)
        tiles = seq // TILE
        ff = hidden // width
        v = pltpu.VMEM
        arrays = dict(
            acc=v((seq, width), F32),
            acc_t=v((width, seq), F32),
            xhat=v((layers, 2, seq, width), BF16),
            rstd=v((seq, 128), F32),
            normed=v((seq, width), BF16),
            normed_t=v((layers, 2, width, seq), BF16),
            q_t=v((layers, width, seq), BF16),
            k_pad=v((layers, padded, width), BF16),
            v_pad=v((layers, padded, width), BF16),
            tr_pad=v((width, padded), BF16),
            probs=v((layers, pairs, tiles, WINDOW, 2 * TILE), BF16),
            near_t=v((layers, width, seq), BF16),
            tanh_t=v((layers, width, seq), BF16),
            s_one=v((layers, pairs, 2 * HD, 2 * HD), F32),
            s_two=v((layers, pairs, 2 * HD, 2 * HD), F32),
            rden=v((layers, pairs, 8, seq), F32),
            mixed_t=v((layers, width, seq), BF16),
            act_t=v((layers, ff, width, seq), BF16),
            dact=v((layers, ff, seq, width), BF16),
            band=v((tiles, WINDOW, 2 * TILE), BF16),
            cols=v((width, 128), F32),
            gm_t=v((width, seq), BF16),
            gk_pad=v((padded, width), F32),
            gv_pad=v((padded, width), F32),
            vecs=v((layers, VROWS, width), F32),
            vgrads=v((layers, VROWS, width), F32),
        )
        return {n: a for n, a in arrays.items() if seq != width or n not in TWINS}

    def w_rows(self, l, first):
        return self.packed[l, :, :, :, :, pl.ds(first, GROUP), :].reshape(self.width, self.width)

    def w_qkv(self, l, n):
        return self.w_rows(l, GROUP * n)

    def w_attn(self, l):
        return self.w_rows(l, 3 * GROUP)

    def w_in(self, l, j):
        return self.w_rows(l, pl.multiple_of(4 * GROUP + GROUP * j, GROUP))

    def out_at(self, j):
        per = self.hidden // (self.width // GROUP)
        return j, pl.ds((4 + self.ff_blocks) * GROUP, per)

    def w_out(self, l, j):
        groups, rows = self.out_at(j)
        return self.packed[l, groups, :, :, :, rows, :].reshape(self.width, self.width)

    def put_rows(self, l, first, value):
        self.grads[:, :, :, :, pl.ds(first, GROUP), :] = value.astype(BF16).reshape(
            self.groups + (GROUP, self.width)
        )

    def put_out(self, l, j, value):
        groups, rows = self.out_at(j)
        per = self.hidden // (self.width // GROUP)
        self.grads[groups, :, :, :, rows, :] = value.astype(BF16).reshape(
            self.groups[1:] + (per, self.width)
        )

    def vec(self, l, row):
        return self.vecs[l, pl.ds(row, 1), :]

    def keep(self, value):
        return jnp.where(row_index(value.shape) < self.length, value, 0.0)

    def setup(self):
        shape = (WINDOW, 2 * TILE)
        key, query = row_index(shape) - PAD, col_index(shape) % TILE
        for t in range(self.tiles):
            pos = key + t * TILE
            ok = (jnp.abs(key - query) <= BAND) & (pos >= 0)
            ok = ok & ((pos < self.length) | (key == query))
            self.band[t] = jnp.where(ok, 0.0, -1e30).astype(BF16)
        zero_head = jnp.zeros((PAD, self.width), BF16)
        zero_tail = jnp.zeros((self.padded - PAD - self.seq, self.width), BF16)
        for l in range(self.layers):
            for ref in (self.k_pad, self.v_pad):
                ref[l, :PAD] = zero_head
                ref[l, PAD + self.seq :] = zero_tail

    def setup_vecs(self):
        eye = (row_index((self.width, self.width)) == col_index((self.width, self.width))).astype(
            BF16
        )
        for l in range(self.layers):
            self.cols[:, VROWS * l : VROWS * (l + 1)] = nt(eye, self.vecs[l].astype(BF16))

    def rows(self, body):
        @pl.loop(0, self.seq // ROWS)
        def _(i):
            body(pl.ds(pl.multiple_of(i * ROWS, ROWS), ROWS))

    def norm(self, l, which, source):
        def body(at):
            value = source[at, :]
            centered = value - jnp.mean(value, axis=-1, keepdims=True)
            rstd = lax.rsqrt(jnp.mean(centered * centered, axis=-1, keepdims=True) + EPSILON)
            xhat = centered * rstd
            n = 2 * l + which
            self.rstd[at, n : n + 1] = rstd
            self.xhat[l, which, at, :] = xhat.astype(BF16)
            normed = xhat * self.vec(l, GAIN + which) + self.vec(l, SHIFT + which)
            self.normed[at, :] = normed.astype(BF16)

        self.rows(body)
        self.normed_t[l, which] = self.normed[...].T

    def pad_keep(self):
        row = row_index((self.padded, 2 * HD)) - PAD
        return (row >= 0) & (row < self.length)

    def fwd_qkv(self, l):
        normed = self.normed[...]
        q = (nn(normed, self.w_qkv(l, 0)) + self.vec(l, BQKV)).astype(BF16)
        self.q_t[l] = q.T
        k = (nn(normed, self.w_qkv(l, 1)) + self.vec(l, BQKV + 1)).astype(BF16)
        self.k_pad[l, PAD : PAD + self.seq] = k
        v = (nn(normed, self.w_qkv(l, 2)) + self.vec(l, BQKV + 2)).astype(BF16)
        self.v_pad[l, PAD : PAD + self.seq] = v
        self.tr_pad[...] = self.v_pad[l].T

    def pair_at(self, p):
        return pl.ds(pl.multiple_of(p * 2 * HD, 2 * HD), 2 * HD)

    def fwd_near(self, l, p):
        at = self.pair_at(p)
        for t in range(self.tiles):
            here, window = slice(t * TILE, (t + 1) * TILE), slice(t * TILE, t * TILE + WINDOW)
            wide = spread(self.q_t[l, at, here])
            scores = nn(self.k_pad[l, window, at], wide) * (HD**-0.5) + self.band[t].astype(F32)
            weights = jnp.exp(scores - jnp.max(scores, axis=0, keepdims=True))
            inverse = 1.0 / jnp.sum(weights, axis=0, keepdims=True)
            probs = (weights * inverse).astype(BF16)
            self.probs[l, p, t] = probs
            near = fold(nn(self.tr_pad[at, window], probs))
            self.near_t[l, at, here] = near.astype(BF16)

    def features(self, x):
        grown = jnp.exp(jnp.minimum(x, 0.0))
        return jnp.where(x > 0, x + 1.0, grown), grown, jnp.tanh(x)

    def key_features(self, l, at):
        phi, slope, tanh = self.features(self.k_pad[l, :, at].astype(F32))
        ok = self.pad_keep()
        return (
            jnp.where(ok, phi, 0.0).astype(BF16),
            slope,
            jnp.where(ok, tanh, 0.0).astype(BF16),
            tanh,
        )

    def coefficient(self):
        wide = jnp.full((1, 1), HD, F32) * self.length.astype(F32)
        return lax.rsqrt(wide)

    def heads_row(self, two, seq):
        return jnp.concatenate(
            [
                jnp.broadcast_to(two[0:1], (HD, seq)),
                jnp.broadcast_to(two[1:2], (HD, seq)),
            ],
            axis=0,
        )

    def fwd_far(self, l, p):
        at = self.pair_at(p)
        phk, _, tk, _ = self.key_features(l, at)
        values_t = self.tr_pad[at, :]
        s_one = head_diag(nn(values_t, phk))
        s_two = head_diag(nn(values_t, tk))
        total = col_sum(phk.astype(F32))
        self.s_one[l, p], self.s_two[l, p] = s_one, s_two
        phi, _, tanh = self.features(self.q_t[l, at, :].astype(F32))
        phq, tq = phi.astype(BF16), tanh.astype(BF16)
        shape = (8, 2 * HD)
        mine = (row_index(shape) == 0) == (col_index(shape) < HD)
        z_high, z_low = split(jnp.where(mine & (row_index(shape) < 2), total, 0.0))
        den = nn(z_high, phq) + nn(z_low, phq)
        rden = 1.0 / jnp.where(row_index(den.shape) < 2, den, 1.0)
        self.rden[l, p] = rden
        total_col = jnp.broadcast_to(total, (8, 2 * HD)).T
        n = VROWS * l
        self.cols[at, n : n + 1] = total_col[:, 0:1]
        high, low = split(s_one)
        far_elu = (nn(high, phq) + nn(low, phq)) * self.heads_row(rden, self.seq)
        high, low = split(s_two)
        far_tanh = (nn(high, tq) + nn(low, tq)) * self.coefficient()
        self.tanh_t[l, at, :] = far_tanh.astype(BF16)
        blend = self.cols[at, VROWS * l : VROWS * (l + 1)]
        self.mixed_t[l, at, :] = (
            blend[:, BLEND : BLEND + 1] * self.near_t[l, at, :].astype(F32)
            + blend[:, BLEND + 1 : BLEND + 2] * far_elu
            + blend[:, BLEND + 2 : BLEND + 3] * far_tanh
        ).astype(BF16)

    def fwd_attn(self, l):
        mixed = self.mixed_t[l].T
        out = nn(mixed, self.w_attn(l)) + self.vec(l, OBIAS)
        self.gk_pad[: self.seq] = self.h[...] + self.keep(out)
        self.norm(l, 1, self.gk_pad)

    def fwd_ff(self, l, j):
        pre = nn(self.normed[...], self.w_in(l, j)) + self.vec(l, BIN + j)
        square = pre * pre
        th = jnp.tanh(GELU_C * pre * (1.0 + GELU_A * square))
        half = 0.5 * (1.0 + th)
        act = (pre * half).astype(BF16)
        slope = half + (0.5 * GELU_C) * pre * (1.0 - th * th) * (1.0 + 3.0 * GELU_A * square)
        self.dact[l, j] = slope.astype(BF16)
        self.act_t[l, j] = act.T
        part = nn(act, self.w_out(l, j))
        self.acc[...] = jnp.where(j == 0, part, self.acc[...] + part)

    def fwd_end(self, l):
        self.h[...] = self.gk_pad[: self.seq] + self.keep(self.acc[...] + self.vec(l, OBIAS + 1))

    def put_vec(self, l, row, value):
        self.vgrads[l, pl.ds(row, 1), :] = value

    def bwd_start(self, l):
        gz = self.keep(self.h[...]).astype(BF16)
        self.normed[...] = gz
        self.put_vec(l, OBIAS + 1, col_sum(gz.astype(F32)))

    def bwd_ff(self, l, j):
        gz = self.normed[...]
        gpre = (nt(gz, self.w_out(l, j)) * self.dact[l, j].astype(F32)).astype(BF16)
        self.put_vec(l, BIN + j, col_sum(gpre.astype(F32)))
        self.put_out(l, j, nn(self.act_t[l, j], gz))
        self.put_rows(
            l, pl.multiple_of(4 * GROUP + GROUP * j, GROUP), nn(self.normed_t[l, 1], gpre)
        )
        part = nt(gpre, self.w_in(l, j))
        self.acc[...] = jnp.where(j == 0, part, self.acc[...] + part)

    def norm_back(self, l, which):
        self.put_vec(l, GAIN + which, jnp.zeros((1, self.width), F32))
        self.put_vec(l, SHIFT + which, jnp.zeros((1, self.width), F32))

        def body(at):
            grad = self.acc[at, :]
            xhat = self.xhat[l, which, at, :].astype(F32)
            self.vgrads[l, pl.ds(GAIN + which, 1), :] += col_sum(grad * xhat)
            self.vgrads[l, pl.ds(SHIFT + which, 1), :] += col_sum(grad)
            grad = grad * self.vec(l, GAIN + which)
            mean = jnp.mean(grad, axis=-1, keepdims=True)
            slope = jnp.mean(grad * xhat, axis=-1, keepdims=True)
            n = 2 * l + which
            self.h[at, :] += self.rstd[at, n : n + 1] * (grad - mean - xhat * slope)

        self.rows(body)

    def bwd_attn(self, l):
        self.norm_back(l, 1)
        go = self.keep(self.h[...]).astype(BF16)
        self.put_vec(l, OBIAS, col_sum(go.astype(F32)))
        self.put_rows(l, 3 * GROUP, nn(self.mixed_t[l], go))
        self.gm_t[...] = nt(self.w_attn(l), go).astype(BF16)
        self.tr_pad[...] = self.k_pad[l].T
        self.gk_pad[...] = jnp.zeros_like(self.gk_pad)
        self.gv_pad[...] = jnp.zeros_like(self.gv_pad)

    def bwd_near(self, l, p):
        at = self.pair_at(p)
        blend = self.cols[at, VROWS * l : VROWS * (l + 1)]
        for t in range(self.tiles):
            here, window = slice(t * TILE, (t + 1) * TILE), slice(t * TILE, t * TILE + WINDOW)
            grad = (blend[:, BLEND : BLEND + 1] * self.gm_t[at, here].astype(F32)).astype(BF16)
            grad = spread(grad)
            probs = self.probs[l, p, t]
            wide = probs.astype(F32)
            dprobs = nn(self.v_pad[l, window, at], grad)
            term = wide * dprobs
            inner = jnp.sum(term, axis=0, keepdims=True)
            gs = ((term - wide * inner) * (HD**-0.5)).astype(BF16)
            self.acc_t[at, here] = fold(nn(self.tr_pad[at, window], gs))
            self.gk_pad[window, at] += nt(gs, spread(self.q_t[l, at, here]))
            self.gv_pad[window, at] += nt(probs, grad)

    def bwd_far(self, l, p):
        at = self.pair_at(p)
        seq = self.seq
        blend = self.cols[at, VROWS * l : VROWS * (l + 1)]
        gm = self.gm_t[at, :].astype(F32)
        q = self.q_t[l, at, :].astype(F32)
        phi_q, slope_q, tanh_q = self.features(q)
        phq, tq = phi_q.astype(BF16), tanh_q.astype(BF16)
        high, low = split(self.s_one[l, p])
        far_elu = (nn(high, phq) + nn(low, phq)) * self.heads_row(self.rden[l, p], seq)
        column = lambda a: jnp.sum(a, axis=1, keepdims=True)
        sums = [
            column(gm * self.near_t[l, at, :].astype(F32)),
            column(gm * far_elu),
            column(gm * self.tanh_t[l, at, :].astype(F32)),
        ]
        for n, one in enumerate(sums):
            self.cols[at, GBLEND + n : GBLEND + n + 1] = one
        phk, slope_k, tk, tanh_k = self.key_features(l, at)
        values = self.v_pad[l, :, at]
        gnum = (blend[:, BLEND + 1 : BLEND + 2] * gm * self.heads_row(self.rden[l, p], seq)).astype(
            BF16
        )
        prod = gnum.astype(F32) * far_elu
        gden_one = -col_sum(prod[:HD])
        gden_two = -col_sum(prod[HD:])
        gden = jnp.concatenate([gden_one, gden_two, jnp.zeros((6, seq), F32)], axis=0)
        s_one = self.s_one[l, p].T
        high, low = split(s_one)
        gphq = nn(high, gnum) + nn(low, gnum) + self.cols[at, VROWS * l : VROWS * l + 1] * self.heads_row(gden, seq)
        gs_one = head_diag(nt(phq, gnum))
        gs_high, gs_low = split(gs_one)
        gden_high, gden_low = split(gden)
        both = nt(gden_high, phq) + nt(gden_low, phq)
        gzz = jnp.where(col_index((1, 2 * HD)) < HD, both[0:1], both[1:2])
        gtanh = (blend[:, BLEND + 2 : BLEND + 3] * gm * self.coefficient()).astype(BF16)
        gtq = nn(self.s_two[l, p].T.astype(BF16), gtanh)
        gs_two = head_diag(nt(tq, gtanh)).astype(BF16)
        self.acc_t[at, :] += gphq * jnp.where(q > 0, 1.0, slope_q) + gtq * (1.0 - tanh_q * tanh_q)
        gphk = nt(values, gs_high) + nt(values, gs_low) + gzz
        gtk = nt(values, gs_two)
        grad_k = gphk * slope_k + gtk * (1.0 - tanh_k * tanh_k)
        self.gk_pad[:, at] += jnp.where(self.pad_keep(), grad_k, 0.0)
        self.gv_pad[:, at] += nn(phk, gs_high) + nn(tk, gs_two)

    def bwd_qkv(self, l):
        rows = slice(PAD, PAD + self.seq)
        self.vgrads[l, pl.ds(BLEND, 3), :] = self.cols[...].T[GBLEND : GBLEND + 3]
        normed_t = self.normed_t[l, 0]
        for n in range(3):
            if n == 0:
                grad = self.acc_t[...].T.astype(BF16)
            else:
                grad = (self.gk_pad, self.gv_pad)[n - 1][rows, :].astype(BF16)
            self.put_vec(l, BQKV + n, col_sum(grad.astype(F32)))
            self.put_rows(l, GROUP * n, nn(normed_t, grad))
            part = nt(grad, self.w_qkv(l, n))
            self.acc[...] = part if n == 0 else self.acc[...] + part
        self.norm_back(l, 0)

    def loop(self, count, body):
        @pl.loop(0, count)
        def _(n):
            body(n)


class Comm:
    def __init__(self, depth, sems):
        self.send, self.recv = sems
        self.count = 0
        self.sent = []
        dp, fsdp = lax.axis_index("dp"), lax.axis_index("fsdp")
        self.depth = depth
        self.at = {"z": dp // 2, "x": dp % 2, "y": fsdp // 2, "c": fsdp % 2}

    def device(self, **moved):
        at = dict(self.at, **moved)
        return (at["z"] * 2 + at["x"], at["y"] * 2 + at["c"])

    def other(self, axis, step=1):
        if axis == "z":
            return lax.rem(self.at["z"] + step, self.depth)
        return 1 - self.at[axis]

    def neighbours(self):
        steps = [("z", k) for k in range(1, self.depth)] + [("x", 1), ("y", 1), ("c", 1)]
        return [self.device(**{axis: self.other(axis, k)}) for axis, k in steps]

    def barrier(self):
        semaphore = pltpu.get_barrier_semaphore()
        peers = self.neighbours()
        for peer in peers:
            pl.semaphore_signal(semaphore, inc=1, device_id=peer, device_id_type=MESH)
        pl.semaphore_wait(semaphore, len(peers))

    def copy(self, source, target, peer):
        n = self.count
        self.count += 1
        made = pltpu.make_async_remote_copy(
            src_ref=source,
            dst_ref=target,
            send_sem=self.send.at[n],
            recv_sem=self.recv.at[n],
            device_id=peer,
            device_id_type=MESH,
        )
        made.start()
        return made

    def index(self, whole, moved=None):
        at = dict(self.at, **(moved or {}))
        return tuple(slice(None) if axis in whole else at[axis] for axis in "zxyc")

    @staticmethod
    def add(mine, other):
        @pl.loop(0, mine.shape[0])
        def _(z):
            for rest in itertools.product(*[range(n) for n in mine.shape[1:-2]]):
                at = (z,) + rest
                mine[at] = mine[at] + other[at]

    def gather(self, parts):
        waiting = []
        cores = []
        for stage in range(4):
            started = []
            for view, order in parts:
                whole = order[:stage]
                if stage < 3:
                    axis = order[stage]
                    block = view(self.index(whole))
                    steps = range(1, self.depth) if axis == "z" else (1,)
                    for k in steps:
                        peer = self.device(**{axis: self.other(axis, k)})
                        started.append(self.copy(block, block, peer))
                if stage > 0:
                    axis = order[stage - 1]
                    if axis == "z":
                        block = view(self.index(whole))
                    elif "z" in whole:
                        moved = {axis: self.other(axis)}
                        block = view(self.index(order[: stage - 1], moved))
                    else:
                        continue
                    cores.append(self.copy(block, block, self.device(c=self.other("c"))))
            yield
            for one in started:
                one.wait_recv()
            self.sent += started
        for one in cores:
            one.wait_recv()
        self.sent += cores

    def scatter(self, parts, done):
        pending = []
        stages = ["c"] + [None] * 3
        for stage in range(4):
            started = []
            for view, slots, order in parts:
                axes = ("c",) + tuple(order)
                axis, whole = axes[stage], axes[stage + 1 :]
                if axis == "z":
                    for k in range(1, self.depth):
                        moved = {"z": self.other("z", k)}
                        peer = self.device(**moved)
                        block = view(self.index((), moved))
                        started.append(self.copy(block, slots[stage](k - 1), peer))
                else:
                    moved = {axis: self.other(axis)}
                    block = view(self.index(whole, moved))
                    started.append(self.copy(block, slots[stage](None), self.device(**moved)))
            yield
            for one in started:
                one.wait_recv()
            pending += started
            for view, slots, order in parts:
                axes = ("c",) + tuple(order)
                axis, whole = axes[stage], axes[stage + 1 :]
                if axis != "z":
                    self.add(view(self.index(whole)), slots[stage](None))
                else:
                    total = view(self.index(()))[...].astype(F32)
                    for k in range(1, self.depth):
                        total = total + slots[stage](k - 1)[...].astype(F32)
                    done(view, total)
        for one in pending:
            one.wait_send()


def lane_hits(first, cols, per, lane, rows=128):
    shape = (rows, cols)
    element = col_index(shape) + first
    return (row_index(shape) - lane == element - per * owner_of(element, per)).astype(BF16)


def owner_of(element, per):
    if per & (per - 1) == 0:
        return lax.shift_right_logical(element, per.bit_length() - 1)
    return lax.shift_right_logical(element * (-(-65536 // per)), 16)


def owner_mask(owner, first, cols, per):
    return owner == owner_of(col_index((owner.shape[0], cols)) + first, per)


class Vectors:
    def __init__(self, layers, width, hidden):
        self.layers, self.width = layers, width
        self.devices = width // GROUP
        self.lanes = 128 // layers
        self.wide = [(BQKV, 3, 3 * GROUP), (BIN, hidden // width, hidden // self.devices)]

    def spread(self, shares, vecs):
        width = self.width
        n = self.devices // shares.shape[0]
        vecs[...] = jnp.zeros_like(vecs)

        @pl.loop(0, shares.shape[0])
        def _(z):
            tiles = shares[z].reshape(n, VROWS, 128)
            flat = tiles.reshape(n * VROWS, 128)
            shape = (n * VROWS, width)
            own = owner_mask(n * z + lax.shift_right_logical(row_index(shape), 4), 0, width, GROUP)
            mine = n * z + row_index((n, width))
            for l in range(self.layers):
                lane = self.lanes * l
                rows = nn(flat, lane_hits(0, width, GROUP, lane))
                rows = jnp.sum(jnp.where(own, rows, 0.0).reshape(n, VROWS, width), axis=0)
                for first, last in self.plain_rows():
                    vecs[l, first:last, :] += rows[first:last]
                for row, count, per in self.wide:
                    one = tiles.astype(F32)[:, row, :].astype(BF16)
                    for j in range(count):
                        values = nn(one, lane_hits(j * width, width, per, lane))
                        values = jnp.where(owner_mask(mine, j * width, width, per), values, 0.0)
                        vecs[l, row + j : row + j + 1, :] += col_sum(values)

    def plain_rows(self):
        first, spans = 0, []
        for row, count, _ in self.wide:
            spans.append((first, row))
            first = row + count
        return spans + [(first, VROWS)]

    def collect(self, vgrads, shares):
        width = self.width
        n = self.devices // shares.shape[0]

        def exact(values, hits):
            high, low = split(values)
            return nt(high, hits) + nt(low, hits)

        @pl.loop(0, shares.shape[0])
        def _(z):
            shape = (n * VROWS, width)
            own = owner_mask(n * z + lax.shift_right_logical(row_index(shape), 4), 0, width, GROUP)
            mine = n * z + row_index((n, width))
            result = jnp.zeros((n, VROWS, 128), F32)
            kind = lax.broadcasted_iota(jnp.int32, result.shape, 1)
            for l in range(self.layers):
                lane = self.lanes * l
                rows = vgrads[l]
                wide = jnp.broadcast_to(rows[None], (n, VROWS, width)).reshape(shape)
                part = exact(jnp.where(own, wide, 0.0), lane_hits(0, width, GROUP, lane))
                part = part.reshape(n, VROWS, 128)
                for row, count, per in self.wide:
                    total = jnp.zeros((n, 128), F32)
                    for j in range(count):
                        values = jnp.broadcast_to(rows[row + j : row + j + 1], (n, width))
                        values = jnp.where(owner_mask(mine, j * width, width, per), values, 0.0)
                        total = total + exact(values, lane_hits(j * width, width, per, lane))
                    inside = (kind >= row) & (kind < row + count)
                    first = jnp.broadcast_to(total[:, None, :], part.shape)
                    part = jnp.where(inside, jnp.where(kind == row, first, 0.0), part)
                result = result + part
            shares[z] = result.reshape(shares.shape[1:])


def step(*generators):
    for one in generators:
        next(one, None)


class Program:
    def __init__(self, net, comm, vectors, r):
        self.net, self.comm, self.vectors = net, comm, vectors
        self.__dict__.update(r)

    def fill(self):
        own = self.comm.index(())
        width = self.net.width
        for l in range(self.net.layers):
            first = 0
            for ref in (self.w_qkv, self.w_attn, self.w_in):
                for n in range(ref.shape[2] // width):
                    rows = pl.ds(first, GROUP)
                    self.net.packed[(l,) + own + (rows,)] = ref[l, :, n * width : (n + 1) * width]
                    first += GROUP
            rows = pl.ds(first, self.w_out.shape[1])
            self.net.packed[(l,) + own + (rows,)] = self.w_out[l]
        self.shares[own] = self.small[...]

    def weight_part(self, l, first, rows, order):
        at = pl.ds(first, rows)
        return (lambda index: self.net.packed.at[(l,) + index + (at,)], order)

    def gather(self, l, cuts):
        parts = []
        for first, one, two in cuts:
            parts.append(self.weight_part(l, first, one, "zxy"))
            parts.append(self.weight_part(l, first + one, two, "zyx"))
        if l == 0 and cuts[0][0] == 0:
            parts.append((lambda index: self.shares.at[index], "zxy"))
        return self.comm.gather(parts)

    def scatter(self, l, cuts, vectors=False):
        parts, puts = [], {}

        def add(view, arrivals, at, order, put):
            slots = [
                lambda k: arrivals[0].at[(slice(None),) * 3 + at],
                lambda k: arrivals[1].at[(slice(None),) * 2 + at],
                lambda k: arrivals[2].at[(slice(None),) + at],
                lambda k: arrivals[3].at[(k,) + at],
            ]
            puts[view] = put
            parts.append((view, slots, order))

        def add_rows(first, rows, order):
            at = (pl.ds(first, rows),)
            view = lambda index: self.net.grads.at[index + at]
            add(view, self.arrivals, at, order, functools.partial(self.put, l, first, rows))

        for first, one, two in cuts:
            add_rows(first, one, "yxz")
            add_rows(first + one, two, "xyz")
        if vectors:
            view = lambda index: self.vshares.at[index]
            add(view, self.varrivals, (), "yxz", self.put_small)
        return self.comm.scatter(parts, lambda view, total: puts[view](total))

    def put_small(self, total):
        self.gsmall[...] = total

    def put(self, l, first, rows, total):
        width = self.net.width
        begin = 0
        for ref in (self.gw_qkv, self.gw_attn, self.gw_in):
            for n in range(ref.shape[2] // width):
                if first <= begin < first + rows:
                    ref[l, :, n * width : (n + 1) * width] = total[begin - first :][:GROUP]
                begin += GROUP
        low, high = max(first, begin), first + rows
        if high > low:
            self.gw_out[l, low - begin : high - begin, :] = total[low - first :]

    def run(self):
        net, comm = self.net, self.comm
        loop = net.loop
        cuts = [
            [[(0, 32, 16)], [(48, 32, 48)], [(128, 32, 32)]],
            [[(0, 16, 32)], [(48, 48, 32)], [(128, 32, 32)]],
        ]
        qkv, up, down = zip(*[[self.gather(l, c) for c in cuts[l]] for l in range(2)])
        self.fill()
        comm.barrier()
        step(qkv[0])
        net.setup()
        net.h[...] = self.tokens[...].astype(F32)
        step(qkv[0], up[0], qkv[0], up[0], down[0], qkv[0], qkv[0])
        self.vectors.spread(self.shares, net.vecs)
        net.setup_vecs()
        net.norm(0, 0, net.h)
        net.fwd_qkv(0)
        step(up[0], down[0], qkv[1])
        loop(net.pairs, functools.partial(net.fwd_near, 0))
        step(up[0])
        loop(net.pairs, functools.partial(net.fwd_far, 0))
        step(down[0], qkv[1], up[1], up[0])
        net.fwd_attn(0)
        step(down[0], down[0])
        loop(net.ff_blocks, functools.partial(net.fwd_ff, 0))
        net.fwd_end(0)
        step(qkv[1], up[1], down[1], qkv[1], qkv[1])
        net.norm(1, 0, net.h)
        net.fwd_qkv(1)
        step(up[1], down[1])
        loop(net.pairs, functools.partial(net.fwd_near, 1))
        step(up[1])
        loop(net.pairs, functools.partial(net.fwd_far, 1))
        step(down[1], up[1])
        net.fwd_attn(1)
        step(down[1], down[1])
        loop(net.ff_blocks, functools.partial(net.fwd_ff, 1))
        net.fwd_end(1)
        self.mixed_out[...] = net.h[...].astype(BF16)
        net.h[...] = self.cotangent[...].astype(F32)
        ffs = [self.scatter(l, [(64, 64, 64)]) for l in range(2)]
        rest = [
            self.scatter(0, [(0, 32, 32)], vectors=True),
            self.scatter(1, [(0, 32, 32)]),
        ]
        for l in (1, 0):
            net.bwd_start(l)
            loop(net.ff_blocks, functools.partial(net.bwd_ff, l))
            step(ffs[l])
            if l == 0:
                step(rest[1])
            net.bwd_attn(l)
            step(ffs[l])
            if l == 0:
                step(rest[1])
            loop(net.pairs, functools.partial(net.bwd_near, l))
            step(ffs[l])
            loop(net.pairs, functools.partial(net.bwd_far, l))
            step(ffs[l])
            net.bwd_qkv(l)
            step(ffs[l])
            if l == 0:
                self.vectors.collect(net.vgrads, self.vshares)
            step(rest[l])
            if l == 1:
                step(rest[1], rest[1], rest[1], rest[1])
        step(rest[0], rest[0], rest[0], rest[0])
        for one in comm.sent:
            one.wait_send()


INPUTS = ("tokens", "cotangent", "small", "w_qkv", "w_attn", "w_in", "w_out")
OUTPUTS = ("mixed_out", "h", "gsmall", "gw_qkv", "gw_attn", "gw_in", "gw_out")
COPIES = 160


def fused_body(sizes, depth, names, length_ref, *refs):
    named = dict(zip(INPUTS + OUTPUTS + names, refs))
    arrivals = [named.pop("arrive%d" % n) for n in range(4)]
    varrivals = [named.pop("varrive%d" % n) for n in range(4)]
    sems = named.pop("send"), named.pop("recv")
    inner = {n: r for n, r in named.items() if n not in INPUTS}
    net = Net(*sizes, length_ref[0], inner)
    comm = Comm(depth, sems)
    vectors = Vectors(sizes[0], sizes[2], sizes[3])
    Program(net, comm, vectors, dict(named, arrivals=arrivals, varrivals=varrivals)).run()


def fused(mesh, lengths, tokens, cotangent, small, weights):
    layers, _, width = weights[1].shape
    hidden = weights[2].shape[2]
    seq = tokens.shape[0]
    sizes = (layers, seq, width, hidden)
    rows = sum(w.shape[1] * w.shape[2] for w in weights) // width
    groups = group_shape(width, hidden)
    vmem = pl.BlockSpec(memory_space=pltpu.VMEM)
    scratch = dict(Net.scratch(*sizes))
    scratch["packed"] = pltpu.VMEM((layers,) + groups + (rows, width), BF16)
    scratch["grads"] = pltpu.VMEM(groups + (rows, width), BF16)
    scratch["shares"] = pltpu.VMEM(groups + small.shape, BF16)
    scratch["vshares"] = pltpu.VMEM(groups + small.shape, F32)
    kept = (groups[:3], groups[:2], groups[:1], (groups[0] - 1,))
    for n, lead in enumerate(kept):
        scratch["arrive%d" % n] = pltpu.VMEM(lead + (rows, width), BF16)
        scratch["varrive%d" % n] = pltpu.VMEM(lead + small.shape, F32)
    scratch["send"] = pltpu.SemaphoreType.DMA((COPIES,))
    scratch["recv"] = pltpu.SemaphoreType.DMA((COPIES,))
    return pl.pallas_call(
        functools.partial(fused_body, sizes, groups[0], tuple(scratch)),
        out_shape=(
            jax.ShapeDtypeStruct(tokens.shape, BF16),
            jax.ShapeDtypeStruct(tokens.shape, F32),
            jax.ShapeDtypeStruct(small.shape, F32),
        )
        + tuple(jax.ShapeDtypeStruct(w.shape, F32) for w in weights),
        in_specs=[pl.BlockSpec(memory_space=pltpu.SMEM)] + [vmem] * len(INPUTS),
        out_specs=(vmem,) * len(OUTPUTS),
        scratch_shapes=list(scratch.values()),
        compiler_params=pltpu.CompilerParams(
            collective_id=0, has_side_effects=True, vmem_limit_bytes=63 * 2**20
        ),
    )(lengths, tokens, cotangent, small, *weights)


def pack_small(vectors, layers):
    lanes = 128 // layers
    rows = []
    for v, count in zip(vectors, (2, 2, 3, 3, 4, 2)):
        v = v.reshape(layers, -1, v.shape[-1])
        rows.append(jnp.pad(v, ((0, 0), (0, count - v.shape[1]), (0, lanes - v.shape[2]))))
    return jnp.concatenate(rows, axis=1).transpose(1, 0, 2).reshape(VROWS, 128)


def unpack_small(tile, vectors, layers):
    cube = tile.reshape(VROWS, layers, 128 // layers).transpose(1, 0, 2)
    outs = []
    for v, row in zip(vectors, (GAIN, SHIFT, BQKV, BLEND, BIN, OBIAS)):
        count = 1 if v.ndim == 2 else v.shape[1]
        outs.append(cube[:, row : row + count, : v.shape[-1]].reshape(v.shape))
    return outs


def plain_body(sizes, names, length_ref, *refs):
    names = ("tokens", "cotangent", "packed", "vecs", "mixed_out", "h", "grads_out", "vgrads") + names
    named = dict(zip(names, refs))
    net = Net(*sizes, length_ref[0], named)
    loop = net.loop
    net.setup()
    net.setup_vecs()
    net.h[...] = named["tokens"][...].astype(F32)
    for l in range(net.layers):
        net.norm(l, 0, net.h)
        net.fwd_qkv(l)
        loop(net.pairs, functools.partial(net.fwd_near, l))
        loop(net.pairs, functools.partial(net.fwd_far, l))
        net.fwd_attn(l)
        loop(net.ff_blocks, functools.partial(net.fwd_ff, l))
        net.fwd_end(l)
    named["mixed_out"][...] = net.h[...].astype(BF16)
    net.h[...] = named["cotangent"][...].astype(F32)
    for l in reversed(range(net.layers)):
        net.bwd_start(l)
        loop(net.ff_blocks, functools.partial(net.bwd_ff, l))
        net.bwd_attn(l)
        loop(net.pairs, functools.partial(net.bwd_near, l))
        loop(net.pairs, functools.partial(net.bwd_far, l))
        net.bwd_qkv(l)
        copy = pltpu.make_async_copy(named["grads"], named["grads_out"].at[l], named["sem"])
        copy.start()
        copy.wait()


def plain(lengths, tokens, cotangent, packed, vecs):
    layers, rows, width = packed.shape[0], packed.shape[-2], packed.shape[-1]
    seq = tokens.shape[0]
    hidden = (rows // GROUP - 4) // 2 * width
    sizes = (layers, seq, width, hidden)
    scratch = dict(Net.scratch(*sizes))
    del scratch["vecs"], scratch["vgrads"]
    scratch["grads"] = pltpu.VMEM(packed.shape[1:], BF16)
    scratch["sem"] = pltpu.SemaphoreType.DMA
    vmem = pl.BlockSpec(memory_space=pltpu.VMEM)
    return pl.pallas_call(
        functools.partial(plain_body, sizes, tuple(scratch)),
        out_shape=(
            jax.ShapeDtypeStruct((seq, width), BF16),
            jax.ShapeDtypeStruct((seq, width), F32),
            jax.ShapeDtypeStruct(packed.shape, BF16),
            jax.ShapeDtypeStruct((layers, VROWS, width), F32),
        ),
        in_specs=[pl.BlockSpec(memory_space=pltpu.SMEM)] + [vmem] * 4,
        out_specs=(vmem, vmem, pl.BlockSpec(memory_space=pl.ANY), vmem),
        scratch_shapes=list(scratch.values()),
        compiler_params=pltpu.CompilerParams(vmem_limit_bytes=63 * 2**20),
    )(lengths, tokens, cotangent, packed, vecs)


BOTH = ("dp", "fsdp")


def general(lengths, tokens, cotangent, vectors, weights):
    whole = lambda v, axis: lax.all_gather(v, BOTH, axis=axis, tiled=True)
    w_all = [whole(w, 1) for w in weights]
    v_all = [whole(v, v.ndim - 1) for v in vectors]
    layers, width, _ = w_all[1].shape
    groups = group_shape(width, w_all[2].shape[2])
    blocks = []
    for w in w_all[:3]:
        cut = w.reshape((layers,) + groups + (GROUP, -1, width))
        blocks.append(jnp.moveaxis(cut, -2, -3).reshape((layers,) + groups + (-1, width)))
    blocks.append(w_all[3].reshape((layers,) + groups + (-1, width)))
    vecs = jnp.concatenate([v.reshape(layers, -1, width) for v in v_all], axis=1).astype(F32)
    mixed, grad_tokens, grads, vgrads = plain(
        lengths, tokens, cotangent, jnp.concatenate(blocks, axis=-2), vecs
    )
    reduce = lambda g, axis: lax.psum_scatter(g, BOTH, scatter_dimension=axis, tiled=True)
    w_grads, first = [], 0
    for n, (w, block) in enumerate(zip(w_all, blocks)):
        part = grads[..., first : first + block.shape[-2], :].astype(F32)
        first += block.shape[-2]
        if n < 3:
            part = part.reshape((layers,) + groups + (-1, GROUP, width))
            part = jnp.moveaxis(part, -3, -2)
        w_grads.append(reduce(part.reshape(w.shape), 1))
    v_grads, first = [], 0
    for v in v_all:
        count = v.size // (layers * width)
        part = vgrads[:, first : first + count].reshape(v.shape)
        first += count
        v_grads.append(reduce(part, v.ndim - 1))
    return mixed, grad_tokens, v_grads, w_grads


def on_device(mesh, tokens, lengths, *rest):
    gains, shifts, w_qkv, b_qkv, w_attn, blends, w_in, b_in, w_out, biases, cotangent = rest
    vectors = (gains, shifts, b_qkv, blends, b_in, biases)
    weights = (w_qkv, w_attn, w_in, w_out)
    layers, _, width = w_attn.shape
    groups = group_shape(width, w_in.shape[2])
    if (mesh.shape["dp"], mesh.shape["fsdp"]) == (groups[0] * groups[1], groups[2] * groups[3]):
        small = pack_small(vectors, layers)
        mixed, grad_tokens, tile, *w_grads = fused(
            mesh, lengths, tokens, cotangent, small, weights
        )
        v_grads = unpack_small(tile, vectors, layers)
    else:
        mixed, grad_tokens, v_grads, w_grads = general(
            lengths, tokens, cotangent, vectors, weights
        )
    d_gains, d_shifts, d_b_qkv, d_blends, d_b_in, d_biases = v_grads
    d_w_qkv, d_w_attn, d_w_in, d_w_out = w_grads
    return (
        mixed,
        grad_tokens,
        d_gains,
        d_shifts,
        d_w_qkv,
        d_b_qkv,
        d_w_attn,
        d_blends,
        d_w_in,
        d_b_in,
        d_w_out,
        d_biases,
    )


def solution(mesh):
    rows, vector = P(BOTH, None), P(None, None, BOTH)
    weight, bias = P(None, BOTH, None), P(None, BOTH)
    in_specs = (
        rows,
        P(BOTH),
        vector,
        vector,
        weight,
        bias,
        weight,
        vector,
        weight,
        bias,
        weight,
        vector,
        rows,
    )
    out_specs = (
        rows,
        rows,
        vector,
        vector,
        weight,
        bias,
        weight,
        vector,
        weight,
        bias,
        weight,
        vector,
    )
    return jax.shard_map(
        functools.partial(on_device, mesh),
        mesh=mesh,
        in_specs=in_specs,
        out_specs=out_specs,
        check_vma=False,
    )
```

```python
import functools
import itertools
import jax
import jax.numpy as jnp
from jax import lax
from jax.experimental import pallas as pl
from jax.experimental.pallas import tpu as pltpu
from jax.sharding import PartitionSpec as P

HD = 64
BAND = 30
EPSILON = 1e-05
MESH = pl.DeviceIdType.MESH
F32 = jnp.float32
BF16 = jnp.bfloat16
GROUP = 16
TILE = 128
PAD = 32
WINDOW = TILE + 2 * PAD
TWINS = {"acc_t": "acc", "gm_t": "normed"}
ROWS = 64
GELU_C = 0.7978845608028654
GELU_A = 0.044715
GAIN, SHIFT, BQKV, BLEND, BIN, OBIAS, VROWS = 0, 2, 4, 7, 10, 14, 16


def nn(a, b):
    return jnp.dot(a, b, preferred_element_type=F32)


def nt(a, b):
    return lax.dot_general(a, b, (((1,), (1,)), ((), ())), preferred_element_type=F32)


def split(a):
    high = a.astype(BF16)
    return high, (a - high.astype(F32)).astype(BF16)


def row_index(shape):
    return lax.broadcasted_iota(jnp.int32, shape, 0)


def col_index(shape):
    return lax.broadcasted_iota(jnp.int32, shape, 1)


def head_diag(a):
    return jnp.where((row_index(a.shape) < HD) == (col_index(a.shape) < HD), a, 0.0)


def spread(tile):
    top, bottom = tile[:HD], tile[HD:]
    zero = jnp.zeros_like(top)
    return jnp.concatenate(
        [jnp.concatenate([top, zero], axis=1), jnp.concatenate([zero, bottom], axis=1)], axis=0
    )


def fold(wide):
    half = wide.shape[1] // 2
    return jnp.concatenate([wide[:HD, :half], wide[HD:, half:]], axis=0)


def col_sum(a):
    return jnp.sum(a, axis=0, keepdims=True)


GBLEND = 64


def group_shape(width, hidden):
    first = hidden // width
    return (first, width // GROUP // first // 4, 2, 2)


class Net:
    def __init__(self, layers, seq, width, hidden, length, r):
        self.layers, self.seq, self.width, self.hidden = layers, seq, width, hidden
        self.pairs = width // (2 * HD)
        self.tiles = seq // TILE
        self.length = length
        self.padded = seq + TILE
        self.ff_blocks = hidden // width
        self.groups = group_shape(width, hidden)
        self.__dict__.update(r)
        for name, twin in TWINS.items():
            if name not in r:
                setattr(self, name, r[twin])

    @staticmethod
    def scratch(layers, seq, width, hidden):
        padded = seq + TILE
        pairs = width // (2 * HD)
        tiles = seq // TILE
        ff = hidden // width
        v = pltpu.VMEM
        arrays = dict(
            acc=v((seq, width), F32),
            acc_t=v((width, seq), F32),
            xhat=v((layers, 2, seq, width), BF16),
            rstd=v((seq, 128), F32),
            normed=v((seq, width), BF16),
            normed_t=v((layers, 2, width, seq), BF16),
            q_t=v((layers, width, seq), BF16),
            k_pad=v((layers, padded, width), BF16),
            v_pad=v((layers, padded, width), BF16),
            tr_pad=v((width, padded), BF16),
            probs=v((layers, pairs, tiles, WINDOW, 2 * TILE), BF16),
            near_t=v((layers, width, seq), BF16),
            tanh_t=v((layers, width, seq), BF16),
            s_one=v((layers, pairs, 2 * HD, 2 * HD), F32),
            s_two=v((layers, pairs, 2 * HD, 2 * HD), F32),
            rden=v((layers, pairs, 8, seq), F32),
            mixed_t=v((layers, width, seq), BF16),
            act_t=v((layers, ff, width, seq), BF16),
            dact=v((layers, ff, seq, width), BF16),
            band=v((tiles, WINDOW, 2 * TILE), BF16),
            cols=v((width, 128), F32),
            gm_t=v((width, seq), BF16),
            gk_pad=v((padded, width), F32),
            gv_pad=v((padded, width), F32),
            vecs=v((layers, VROWS, width), F32),
            vgrads=v((layers, VROWS, width), F32),
        )
        return {n: a for n, a in arrays.items() if seq != width or n not in TWINS}

    def w_rows(self, l, first):
        return self.packed[l, :, :, :, :, pl.ds(first, GROUP), :].reshape(self.width, self.width)

    def w_qkv(self, l, n):
        return self.w_rows(l, GROUP * n)

    def w_attn(self, l):
        return self.w_rows(l, 3 * GROUP)

    def w_in(self, l, j):
        return self.w_rows(l, pl.multiple_of(4 * GROUP + GROUP * j, GROUP))

    def out_at(self, j):
        per = self.hidden // (self.width // GROUP)
        return j, pl.ds((4 + self.ff_blocks) * GROUP, per)

    def w_out(self, l, j):
        groups, rows = self.out_at(j)
        return self.packed[l, groups, :, :, :, rows, :].reshape(self.width, self.width)

    def put_rows(self, l, first, value):
        self.grads[:, :, :, :, pl.ds(first, GROUP), :] = value.astype(BF16).reshape(
            self.groups + (GROUP, self.width)
        )

    def put_out(self, l, j, value):
        groups, rows = self.out_at(j)
        per = self.hidden // (self.width // GROUP)
        self.grads[groups, :, :, :, rows, :] = value.astype(BF16).reshape(
            self.groups[1:] + (per, self.width)
        )

    def vec(self, l, row):
        return self.vecs[l, pl.ds(row, 1), :]

    def keep(self, value):
        return jnp.where(row_index(value.shape) < self.length, value, 0.0)

    def setup(self):
        shape = (WINDOW, 2 * TILE)
        key, query = row_index(shape) - PAD, col_index(shape) % TILE
        for t in range(self.tiles):
            pos = key + t * TILE
            ok = (jnp.abs(key - query) <= BAND) & (pos >= 0)
            ok = ok & ((pos < self.length) | (key == query))
            self.band[t] = jnp.where(ok, 0.0, -1e30).astype(BF16)
        zero_head = jnp.zeros((PAD, self.width), BF16)
        zero_tail = jnp.zeros((self.padded - PAD - self.seq, self.width), BF16)
        for l in range(self.layers):
            for ref in (self.k_pad, self.v_pad):
                ref[l, :PAD] = zero_head
                ref[l, PAD + self.seq :] = zero_tail

    def setup_vecs(self):
        eye = (row_index((self.width, self.width)) == col_index((self.width, self.width))).astype(
            BF16
        )
        for l in range(self.layers):
            self.cols[:, VROWS * l : VROWS * (l + 1)] = nt(eye, self.vecs[l].astype(BF16))

    def rows(self, body):
        @pl.loop(0, self.seq // ROWS)
        def _(i):
            body(pl.ds(pl.multiple_of(i * ROWS, ROWS), ROWS))

    def norm(self, l, which, source):
        def body(at):
            value = source[at, :]
            centered = value - jnp.mean(value, axis=-1, keepdims=True)
            rstd = lax.rsqrt(jnp.mean(centered * centered, axis=-1, keepdims=True) + EPSILON)
            xhat = centered * rstd
            n = 2 * l + which
            self.rstd[at, n : n + 1] = rstd
            self.xhat[l, which, at, :] = xhat.astype(BF16)
            normed = xhat * self.vec(l, GAIN + which) + self.vec(l, SHIFT + which)
            self.normed[at, :] = normed.astype(BF16)

        self.rows(body)
        self.normed_t[l, which] = self.normed[...].T

    def pad_keep(self):
        row = row_index((self.padded, 2 * HD)) - PAD
        return (row >= 0) & (row < self.length)

    def fwd_qkv(self, l, n):
        out = (nn(self.normed[...], self.w_qkv(l, n)) + self.vec(l, BQKV + n)).astype(BF16)
        if n == 0:
            self.q_t[l] = out.T
        else:
            (self.k_pad, self.v_pad)[n - 1][l, PAD : PAD + self.seq] = out
        if n == 2:
            self.tr_pad[...] = self.v_pad[l].T

    def pair_at(self, p):
        return pl.ds(pl.multiple_of(p * 2 * HD, 2 * HD), 2 * HD)

    def fwd_near(self, l, p):
        at = self.pair_at(p)
        for t in range(self.tiles):
            here, window = slice(t * TILE, (t + 1) * TILE), slice(t * TILE, t * TILE + WINDOW)
            wide = spread(self.q_t[l, at, here])
            scores = nn(self.k_pad[l, window, at], wide) * (HD**-0.5) + self.band[t].astype(F32)
            weights = jnp.exp(scores - jnp.max(scores, axis=0, keepdims=True))
            inverse = 1.0 / jnp.sum(weights, axis=0, keepdims=True)
            probs = (weights * inverse).astype(BF16)
            self.probs[l, p, t] = probs
            near = fold(nn(self.tr_pad[at, window], probs))
            self.near_t[l, at, here] = near.astype(BF16)

    def features(self, x):
        grown = jnp.exp(jnp.minimum(x, 0.0))
        return jnp.where(x > 0, x + 1.0, grown), grown, jnp.tanh(x)

    def key_features(self, l, at):
        phi, slope, tanh = self.features(self.k_pad[l, :, at].astype(F32))
        ok = self.pad_keep()
        return (
            jnp.where(ok, phi, 0.0).astype(BF16),
            slope,
            jnp.where(ok, tanh, 0.0).astype(BF16),
            tanh,
        )

    def coefficient(self):
        wide = jnp.full((1, 1), HD, F32) * self.length.astype(F32)
        return lax.rsqrt(wide)

    def heads_row(self, two, seq):
        return jnp.concatenate(
            [
                jnp.broadcast_to(two[0:1], (HD, seq)),
                jnp.broadcast_to(two[1:2], (HD, seq)),
            ],
            axis=0,
        )

    def fwd_far(self, l, p):
        at = self.pair_at(p)
        phk, _, tk, _ = self.key_features(l, at)
        values_t = self.tr_pad[at, :]
        s_one = head_diag(nn(values_t, phk))
        s_two = head_diag(nn(values_t, tk))
        total = col_sum(phk.astype(F32))
        self.s_one[l, p], self.s_two[l, p] = s_one, s_two
        phi, _, tanh = self.features(self.q_t[l, at, :].astype(F32))
        phq, tq = phi.astype(BF16), tanh.astype(BF16)
        shape = (8, 2 * HD)
        mine = (row_index(shape) == 0) == (col_index(shape) < HD)
        z_high, z_low = split(jnp.where(mine & (row_index(shape) < 2), total, 0.0))
        den = nn(z_high, phq) + nn(z_low, phq)
        rden = 1.0 / jnp.where(row_index(den.shape) < 2, den, 1.0)
        self.rden[l, p] = rden
        total_col = jnp.broadcast_to(total, (8, 2 * HD)).T
        n = VROWS * l
        self.cols[at, n : n + 1] = total_col[:, 0:1]
        high, low = split(s_one)
        far_elu = (nn(high, phq) + nn(low, phq)) * self.heads_row(rden, self.seq)
        high, low = split(s_two)
        far_tanh = (nn(high, tq) + nn(low, tq)) * self.coefficient()
        self.tanh_t[l, at, :] = far_tanh.astype(BF16)
        blend = self.cols[at, VROWS * l : VROWS * (l + 1)]
        self.mixed_t[l, at, :] = (
            blend[:, BLEND : BLEND + 1] * self.near_t[l, at, :].astype(F32)
            + blend[:, BLEND + 1 : BLEND + 2] * far_elu
            + blend[:, BLEND + 2 : BLEND + 3] * far_tanh
        ).astype(BF16)

    def fwd_attn(self, l):
        mixed = self.mixed_t[l].T
        out = nn(mixed, self.w_attn(l)) + self.vec(l, OBIAS)
        self.gk_pad[: self.seq] = self.h[...] + self.keep(out)
        self.norm(l, 1, self.gk_pad)

    def fwd_up(self, l, j):
        pre = nn(self.normed[...], self.w_in(l, j)) + self.vec(l, BIN + j)
        square = pre * pre
        th = jnp.tanh(GELU_C * pre * (1.0 + GELU_A * square))
        half = 0.5 * (1.0 + th)
        slope = half + (0.5 * GELU_C) * pre * (1.0 - th * th) * (1.0 + 3.0 * GELU_A * square)
        self.dact[l, j] = slope.astype(BF16)
        self.act_t[l, j] = (pre * half).astype(BF16).T

    def fwd_down(self, l, j):
        part = nn(self.act_t[l, j].T, self.w_out(l, j))
        self.acc[...] = part if j == 0 else self.acc[...] + part

    def fwd_end(self, l):
        self.h[...] = self.gk_pad[: self.seq] + self.keep(self.acc[...] + self.vec(l, OBIAS + 1))

    def put_vec(self, l, row, value):
        self.vgrads[l, pl.ds(row, 1), :] = value

    def bwd_start(self, l, source):
        gz = self.keep(source[...].astype(F32)).astype(BF16)
        self.normed[...] = gz
        self.put_vec(l, OBIAS + 1, col_sum(gz.astype(F32)))

    def bwd_out(self, l, j):
        self.put_out(l, j, nn(self.act_t[l, j], self.normed[...]))

    def bwd_up(self, l, j):
        grad = nt(self.normed[...], self.w_out(l, j))
        gpre = (grad * self.dact[l, j].astype(F32)).astype(BF16)
        self.put_vec(l, BIN + j, col_sum(gpre.astype(F32)))
        self.put_rows(l, 4 * GROUP + GROUP * j, nn(self.normed_t[l, 1], gpre))
        part = nt(gpre, self.w_in(l, j))
        self.acc[...] = part if j == 0 else self.acc[...] + part

    def norm_back(self, l, which):
        self.put_vec(l, GAIN + which, jnp.zeros((1, self.width), F32))
        self.put_vec(l, SHIFT + which, jnp.zeros((1, self.width), F32))

        def body(at):
            grad = self.acc[at, :]
            xhat = self.xhat[l, which, at, :].astype(F32)
            self.vgrads[l, pl.ds(GAIN + which, 1), :] += col_sum(grad * xhat)
            self.vgrads[l, pl.ds(SHIFT + which, 1), :] += col_sum(grad)
            grad = grad * self.vec(l, GAIN + which)
            mean = jnp.mean(grad, axis=-1, keepdims=True)
            slope = jnp.mean(grad * xhat, axis=-1, keepdims=True)
            n = 2 * l + which
            self.h[at, :] += self.rstd[at, n : n + 1] * (grad - mean - xhat * slope)

        self.rows(body)

    def bwd_attn(self, l):
        self.norm_back(l, 1)
        go = self.keep(self.h[...]).astype(BF16)
        self.put_vec(l, OBIAS, col_sum(go.astype(F32)))
        self.put_rows(l, 3 * GROUP, nn(self.mixed_t[l], go))
        self.gm_t[...] = nt(self.w_attn(l), go).astype(BF16)
        self.tr_pad[...] = self.k_pad[l].T
        self.gk_pad[...] = jnp.zeros_like(self.gk_pad)
        self.gv_pad[...] = jnp.zeros_like(self.gv_pad)

    def bwd_near(self, l, p):
        at = self.pair_at(p)
        blend = self.cols[at, VROWS * l : VROWS * (l + 1)]
        for t in range(self.tiles):
            here, window = slice(t * TILE, (t + 1) * TILE), slice(t * TILE, t * TILE + WINDOW)
            grad = (blend[:, BLEND : BLEND + 1] * self.gm_t[at, here].astype(F32)).astype(BF16)
            grad = spread(grad)
            probs = self.probs[l, p, t]
            wide = probs.astype(F32)
            dprobs = nn(self.v_pad[l, window, at], grad)
            term = wide * dprobs
            inner = jnp.sum(term, axis=0, keepdims=True)
            gs = ((term - wide * inner) * (HD**-0.5)).astype(BF16)
            self.acc_t[at, here] = fold(nn(self.tr_pad[at, window], gs))
            self.gk_pad[window, at] += nt(gs, spread(self.q_t[l, at, here]))
            self.gv_pad[window, at] += nt(probs, grad)

    def bwd_far(self, l, p):
        at = self.pair_at(p)
        seq = self.seq
        blend = self.cols[at, VROWS * l : VROWS * (l + 1)]
        gm = self.gm_t[at, :].astype(F32)
        q = self.q_t[l, at, :].astype(F32)
        phi_q, slope_q, tanh_q = self.features(q)
        phq, tq = phi_q.astype(BF16), tanh_q.astype(BF16)
        high, low = split(self.s_one[l, p])
        far_elu = (nn(high, phq) + nn(low, phq)) * self.heads_row(self.rden[l, p], seq)
        column = lambda a: jnp.sum(a, axis=1, keepdims=True)
        sums = [
            column(gm * self.near_t[l, at, :].astype(F32)),
            column(gm * far_elu),
            column(gm * self.tanh_t[l, at, :].astype(F32)),
        ]
        for n, one in enumerate(sums):
            self.cols[at, GBLEND + n : GBLEND + n + 1] = one
        phk, slope_k, tk, tanh_k = self.key_features(l, at)
        values = self.v_pad[l, :, at]
        gnum = (blend[:, BLEND + 1 : BLEND + 2] * gm * self.heads_row(self.rden[l, p], seq)).astype(
            BF16
        )
        prod = gnum.astype(F32) * far_elu
        gden_one = -col_sum(prod[:HD])
        gden_two = -col_sum(prod[HD:])
        gden = jnp.concatenate([gden_one, gden_two, jnp.zeros((6, seq), F32)], axis=0)
        s_one = self.s_one[l, p].T
        high, low = split(s_one)
        gphq = nn(high, gnum) + nn(low, gnum) + self.cols[at, VROWS * l : VROWS * l + 1] * self.heads_row(gden, seq)
        gs_one = head_diag(nt(phq, gnum))
        gs_high, gs_low = split(gs_one)
        gden_high, gden_low = split(gden)
        both = nt(gden_high, phq) + nt(gden_low, phq)
        gzz = jnp.where(col_index((1, 2 * HD)) < HD, both[0:1], both[1:2])
        gtanh = (blend[:, BLEND + 2 : BLEND + 3] * gm * self.coefficient()).astype(BF16)
        gtq = nn(self.s_two[l, p].T.astype(BF16), gtanh)
        gs_two = head_diag(nt(tq, gtanh)).astype(BF16)
        self.acc_t[at, :] += gphq * jnp.where(q > 0, 1.0, slope_q) + gtq * (1.0 - tanh_q * tanh_q)
        gphk = nt(values, gs_high) + nt(values, gs_low) + gzz
        gtk = nt(values, gs_two)
        grad_k = gphk * slope_k + gtk * (1.0 - tanh_k * tanh_k)
        self.gk_pad[:, at] += jnp.where(self.pad_keep(), grad_k, 0.0)
        self.gv_pad[:, at] += nn(phk, gs_high) + nn(tk, gs_two)

    def bwd_qkv(self, l, n):
        rows = slice(PAD, PAD + self.seq)
        if n == 0:
            grad = self.acc_t[...].T.astype(BF16)
        else:
            grad = (self.gk_pad, self.gv_pad)[n - 1][rows, :].astype(BF16)
        self.put_vec(l, BQKV + n, col_sum(grad.astype(F32)))
        self.put_rows(l, GROUP * n, nn(self.normed_t[l, 0], grad))
        total = self.gv_pad.at[rows]
        part = nt(grad, self.w_qkv(l, n))
        if n == 2:
            total[...] = part
        elif n == 1:
            total[...] += part
        else:
            self.acc[...] = total[...] + part

    def bwd_end(self, l):
        self.vgrads[l, pl.ds(BLEND, 3), :] = self.cols[...].T[GBLEND : GBLEND + 3]
        self.norm_back(l, 0)


class Comm:
    def __init__(self, depth, sems):
        self.send, self.recv = sems
        self.count = 0
        self.sent = []
        dp, fsdp = lax.axis_index("dp"), lax.axis_index("fsdp")
        self.depth = depth
        self.at = {"z": dp // 2, "x": dp % 2, "y": fsdp // 2, "c": fsdp % 2}

    def device(self, **moved):
        at = dict(self.at, **moved)
        return (at["z"] * 2 + at["x"], at["y"] * 2 + at["c"])

    def steps(self, axis):
        return range(1, self.depth) if axis == "z" else range(1, 2)

    def other(self, axis, step=1):
        if axis == "z":
            return lax.rem(self.at["z"] + step, self.depth)
        return 1 - self.at[axis]

    def barrier(self):
        semaphore = pltpu.get_barrier_semaphore()
        peers = [
            self.device(**{axis: self.other(axis, k)}) for axis in "zxyc" for k in self.steps(axis)
        ]
        for peer in peers:
            pl.semaphore_signal(semaphore, inc=1, device_id=peer, device_id_type=MESH)
        pl.semaphore_wait(semaphore, len(peers))

    def copy(self, source, target, peer):
        n = self.count
        self.count += 1
        made = pltpu.make_async_remote_copy(
            src_ref=source,
            dst_ref=target,
            send_sem=self.send.at[n],
            recv_sem=self.recv.at[n],
            device_id=peer,
            device_id_type=MESH,
        )
        made.start()
        return made

    def index(self, whole, moved=None):
        at = dict(self.at, **(moved or {}))
        return tuple(slice(None) if axis in whole else at[axis] for axis in "zxyc")

    def gather(self, view, order):
        cores = []
        for stage in range(4):
            whole, started = order[:stage], []
            if stage < 3:
                axis = order[stage]
                block = view(self.index(whole))
                for k in self.steps(axis):
                    peer = self.device(**{axis: self.other(axis, k)})
                    started.append(self.copy(block, block, peer))
            if "z" in whole:
                axis = order[stage - 1]
                if axis == "z":
                    block = view(self.index(whole))
                else:
                    block = view(self.index(order[: stage - 1], {axis: self.other(axis)}))
                cores.append(self.copy(block, block, self.device(c=self.other("c"))))
            yield
            for one in started:
                one.wait_recv()
            self.sent += started
        for one in cores:
            one.wait_recv()
        self.sent += cores

    @staticmethod
    def add(mine, others):
        @pl.loop(0, mine.shape[0])
        def _(n):
            for rest in itertools.product(*[range(m) for m in mine.shape[1:-2]]):
                at = (n,) + rest
                total = mine[at]
                for other in others:
                    total = total + other[at]
                mine[at] = total

    def scatter(self, view, slot, order, put):
        axes = "c" + order
        pending = []
        for stage, axis in enumerate(axes):
            whole = axes[stage + 1 :]
            started = []
            for k in self.steps(axis):
                moved = {axis: self.other(axis, k)}
                block = view(self.index(whole, moved))
                started.append(self.copy(block, slot(stage, k - 1), self.device(**moved)))
            yield
            for one in started:
                one.wait_recv()
            pending += started
            mine = view(self.index(whole))
            arrived = [slot(stage, k - 1) for k in self.steps(axis)]
            if whole:
                self.add(mine, arrived)
            else:
                total = mine[...].astype(F32)
                for one in arrived:
                    total = total + one[...].astype(F32)
                put(total)
        for one in pending:
            one.wait_send()


ORDERS = ("zxy", "zyx", "xzy", "yzx", "zxy", "zyx", "zxy", "zyx", "xzy", "yzx", "zxy", "zyx")
LINK, HOP = 0.0238, 2.0
CORE, CORE_HOP = 0.0027, 0.9
ISSUE, BACKLOG, AHEAD = 0.06, 4.0, 12


def plan(layers, segments, parts):
    size = {"z": 4, "x": 2, "y": 2, "c": 2}
    free = dict.fromkeys("zxyc", 0.0)
    clock, steps = 0.0, []
    stage = dict.fromkeys(parts, 0)
    ready = {n: 0.0 if not scatter else None for n, (_, _, scatter) in parts.items()}
    done = set()
    waiting = list(segments)

    def send(axis, blocks, rows):
        link, hop = (CORE, CORE_HOP) if axis == "c" else (LINK, HOP)
        load = blocks * rows * link * (size["z"] if axis == "z" else 1)
        free[axis] = max(free[axis], clock) + load
        return free[axis] + hop

    def count(axes):
        total = 1
        for axis in axes:
            total *= size[axis]
        return total

    def step(name):
        nonlocal clock
        rows, order, scatter = parts[name]
        now = stage[name]
        steps.append((name,))
        stage[name] += 1
        last = 4
        if scatter:
            axes = "c" + order
            if now > 0:
                clock += 0.1 + count(axes[now:]) * rows * 0.0006
            if now < last:
                arrives = send(axes[now], count(axes[now + 1 :]), rows)
                clock += ISSUE * (3 if axes[now] == "z" else 1)
        else:
            arrives = ready[name]
            if now < 3:
                arrives = send(order[now], count(order[:now]), rows)
                clock += ISSUE * (3 if order[now] == "z" else 1)
            if "z" in order[:now] and now < last:
                whole = order[:now] if order[now - 1] == "z" else order[: now - 1]
                core = send("c", count(whole), rows)
                clock += ISSUE
                if now == 3:
                    arrives = core
        if now == last:
            done.add(name)
            ready[name] = None
        else:
            ready[name] = arrives

    def startable(name):
        _, order, scatter = parts[name]
        first = "c" if scatter else order[0]
        return stage[name] > 0 or free[first] <= clock + BACKLOG

    while len(done) < len(parts) or waiting:
        left = [n for n in parts if n not in done][:AHEAD]
        able = [n for n in left if ready[n] is not None and ready[n] <= clock and startable(n)]
        if able:
            step(able[0])
            continue
        if waiting:
            name, layer, argument, cost, needs, makes = waiting[0]
            if all(n in done for n in needs):
                waiting.pop(0)
                steps.append((name, layer, argument))
                clock += cost
                for n in makes:
                    ready[n] = clock
                continue
        later = [ready[n] for n in left if ready[n] is not None and ready[n] > clock]
        later += [free[a] - BACKLOG for a in "zxyc" if free[a] - BACKLOG > clock]
        clock = min(later)
    return steps, clock


def make_plan(layers, pairs, ff, rows):
    units = rows // GROUP
    parts = {("gather", 0, "vectors"): (4, "zxy", False)}
    for l in range(layers):
        for u in range(units):
            parts["gather", l, u] = (GROUP, ORDERS[u % len(ORDERS)], False)
    late = list(range(units - ff, units)) + list(range(4, units - ff)) + [3, 2, 1, 0]
    for l in reversed(range(layers)):
        for u in late:
            parts["scatter", l, u] = (GROUP, ORDERS[u % len(ORDERS)][::-1], True)
    parts["scatter", 0, "vectors"] = (8, "yxz", True)
    gathers = lambda l, us: [("gather", l, u) for u in us]
    scatters = lambda l, us: [("scatter", l, u) for u in us]
    downs = range(units - ff, units)
    segments = []
    add = lambda *s: segments.append(s)
    halves = [(0, pairs // 2), (pairs // 2, pairs)]
    add("start", 0, None, 1.0, [], [])
    add("spread", 0, None, 3.0, [("gather", 0, "vectors")], [])
    for l in range(layers):
        add("norm", l, 0, 0.9, [], [])
        for n in range(3):
            add("fwd_qkv", l, n, 0.6, gathers(l, [n]), [])
        for half in halves:
            add("fwd_near", l, half, 2.7, [], [])
        for half in halves:
            add("fwd_far", l, half, 1.3, [], [])
        add("fwd_attn", l, None, 2.4, gathers(l, [3]), [])
        for j in range(ff):
            add("fwd_up", l, j, 0.9, gathers(l, [4 + j]), [])
        if l == layers - 1:
            add("bwd_start", l, None, 0.3, [], [])
            for j in range(ff):
                add("bwd_out", l, j, 0.3, [], scatters(l, downs) if j == ff - 1 else [])
        for j in range(ff):
            add("fwd_down", l, j, 0.4, gathers(l, downs) if j == 0 else [], [])
        add("fwd_end", l, None, 0.3, [], [])
    for l in reversed(range(layers)):
        again = lambda us: scatters(l + 1, us) if l < layers - 1 else []
        if l < layers - 1:
            add("bwd_start", l, None, 0.3, [], [])
            for j in range(ff):
                makes = scatters(l, downs) if j == ff - 1 else []
                add("bwd_out", l, j, 0.3, again(downs) if j == 0 else [], makes)
        for j in range(ff):
            add("bwd_up", l, j, 1.2, again([4 + j]), scatters(l, [4 + j]))
        add("bwd_attn", l, None, 2.1, again([3]), scatters(l, [3]))
        for half in halves:
            add("bwd_near", l, half, 2.8, [], [])
        for half in halves:
            add("bwd_far", l, half, 2.0, [], [])
        for n in (2, 1, 0):
            add("bwd_qkv", l, n, 0.9, again([n]), scatters(l, [n]))
        add("bwd_end", l, None, 0.8, [], [])
    add("collect", 0, None, 3.0, [], scatters(0, ["vectors"]))
    return plan(layers, segments, parts), parts


def lane_hits(first, cols, per, lane, rows=128):
    shape = (rows, cols)
    element = col_index(shape) + first
    return (row_index(shape) - lane == element - per * owner_of(element, per)).astype(BF16)


def owner_of(element, per):
    if per & (per - 1) == 0:
        return lax.shift_right_logical(element, per.bit_length() - 1)
    return lax.shift_right_logical(element * (-(-65536 // per)), 16)


def owner_mask(owner, first, cols, per):
    return owner == owner_of(col_index((owner.shape[0], cols)) + first, per)


class Vectors:
    def __init__(self, layers, width, hidden):
        self.layers, self.width = layers, width
        self.devices = width // GROUP
        self.lanes = 128 // layers
        self.wide = [(BQKV, 3, 3 * GROUP), (BIN, hidden // width, hidden // self.devices)]

    def spread(self, shares, vecs):
        width = self.width
        n = self.devices // shares.shape[0]
        vecs[...] = jnp.zeros_like(vecs)

        @pl.loop(0, shares.shape[0])
        def _(z):
            tiles = shares[z].reshape(n, VROWS, 128)
            flat = tiles.reshape(n * VROWS, 128)
            shape = (n * VROWS, width)
            own = owner_mask(n * z + lax.shift_right_logical(row_index(shape), 4), 0, width, GROUP)
            mine = n * z + row_index((n, width))
            for l in range(self.layers):
                lane = self.lanes * l
                rows = nn(flat, lane_hits(0, width, GROUP, lane))
                rows = jnp.sum(jnp.where(own, rows, 0.0).reshape(n, VROWS, width), axis=0)
                for first, last in self.plain_rows():
                    vecs[l, first:last, :] += rows[first:last]
                for row, count, per in self.wide:
                    one = tiles.astype(F32)[:, row, :].astype(BF16)
                    for j in range(count):
                        values = nn(one, lane_hits(j * width, width, per, lane))
                        values = jnp.where(owner_mask(mine, j * width, width, per), values, 0.0)
                        vecs[l, row + j : row + j + 1, :] += col_sum(values)

    def plain_rows(self):
        first, spans = 0, []
        for row, count, _ in self.wide:
            spans.append((first, row))
            first = row + count
        return spans + [(first, VROWS)]

    def collect(self, vgrads, shares):
        width = self.width
        n = self.devices // shares.shape[0]

        def exact(values, hits):
            high, low = split(values)
            return nt(high, hits) + nt(low, hits)

        @pl.loop(0, shares.shape[0])
        def _(z):
            shape = (n * VROWS, width)
            own = owner_mask(n * z + lax.shift_right_logical(row_index(shape), 4), 0, width, GROUP)
            mine = n * z + row_index((n, width))
            result = jnp.zeros((n, VROWS, 128), F32)
            kind = lax.broadcasted_iota(jnp.int32, result.shape, 1)
            for l in range(self.layers):
                lane = self.lanes * l
                rows = vgrads[l]
                wide = jnp.broadcast_to(rows[None], (n, VROWS, width)).reshape(shape)
                part = exact(jnp.where(own, wide, 0.0), lane_hits(0, width, GROUP, lane))
                part = part.reshape(n, VROWS, 128)
                for row, count, per in self.wide:
                    total = jnp.zeros((n, 128), F32)
                    for j in range(count):
                        values = jnp.broadcast_to(rows[row + j : row + j + 1], (n, width))
                        values = jnp.where(owner_mask(mine, j * width, width, per), values, 0.0)
                        total = total + exact(values, lane_hits(j * width, width, per, lane))
                    inside = (kind >= row) & (kind < row + count)
                    first = jnp.broadcast_to(total[:, None, :], part.shape)
                    part = jnp.where(inside, jnp.where(kind == row, first, 0.0), part)
                result = result + part
            shares[z] = result.reshape(shares.shape[1:])


class Program:
    def __init__(self, net, comm, vectors, r):
        self.net, self.comm, self.vectors = net, comm, vectors
        self.__dict__.update(r)

    def fill(self):
        own = self.comm.index(())
        width = self.net.width
        for l in range(self.net.layers):
            first = 0
            for ref in (self.w_qkv, self.w_attn, self.w_in):
                for n in range(ref.shape[2] // width):
                    rows = pl.ds(first, GROUP)
                    self.net.packed[(l,) + own + (rows,)] = ref[l, :, n * width : (n + 1) * width]
                    first += GROUP
            rows = pl.ds(first, self.w_out.shape[1])
            self.net.packed[(l,) + own + (rows,)] = self.w_out[l]
        self.shares[own] = self.small[...]

    def gather(self, l, unit, order):
        if unit == "vectors":
            return self.comm.gather(lambda index: self.shares.at[index], order)
        at = pl.ds(unit * GROUP, GROUP)
        return self.comm.gather(lambda index: self.net.packed.at[(l,) + index + (at,)], order)

    def scatter(self, l, unit, order):
        if unit == "vectors":
            arrivals, at, source = self.varrivals, (), self.vshares
        else:
            at = (pl.ds(unit * GROUP, GROUP),)
            arrivals, source = self.arrivals, self.net.grads
        depth = self.comm.depth
        every = slice(None)

        def slot(stage, k):
            if stage < 2:
                return arrivals[stage].at[(every,) * (3 - stage) + at]
            if stage == 2:
                span = slice(2 * k, 2 * k + 2) if order[1] == "z" else slice(0, depth)
                return arrivals[2].at[(span,) + at]
            return arrivals[2].at[(2 * (depth - 1) if order[1] == "z" else depth + k,) + at]

        put = functools.partial(self.put, l, unit)
        return self.comm.scatter(lambda index: source.at[index + at], slot, order, put)

    def put(self, l, unit, total):
        if unit == "vectors":
            self.gsmall[...] = total
            return
        width = self.net.width
        for ref in (self.gw_qkv, self.gw_attn, self.gw_in):
            count = ref.shape[2] // width
            if unit < count:
                ref[l, :, unit * width : (unit + 1) * width] = total
                return
            unit -= count
        self.gw_out[l, unit * GROUP : (unit + 1) * GROUP, :] = total

    def start(self, l, _):
        self.net.setup()
        self.net.h[...] = self.tokens[...].astype(F32)

    def spread(self, l, _):
        self.vectors.spread(self.shares, self.net.vecs)
        self.net.setup_vecs()

    def collect(self, l, _):
        self.vectors.collect(self.net.vgrads, self.vshares)

    def norm(self, l, _):
        self.net.norm(l, 0, self.net.h)

    def fwd_attn(self, l, _):
        self.net.fwd_attn(l)

    def fwd_end(self, l, _):
        self.net.fwd_end(l)
        if l == self.net.layers - 1:
            self.mixed_out[...] = self.net.h[...].astype(BF16)
            self.net.h[...] = self.cotangent[...].astype(F32)

    def bwd_start(self, l, _):
        self.net.bwd_start(l, self.cotangent if l == self.net.layers - 1 else self.net.h)

    def bwd_attn(self, l, _):
        self.net.bwd_attn(l)

    def bwd_end(self, l, _):
        self.net.bwd_end(l)

    def over(self, body, l, span):
        @pl.loop(*span)
        def _(p):
            body(l, p)

    def run(self):
        net = self.net
        rows = net.packed.shape[-2]
        (steps, _), parts = make_plan(net.layers, net.pairs, net.ff_blocks, rows)
        running = {}
        for (kind, l, unit), (_, order, _) in parts.items():
            make = self.gather if kind == "gather" else self.scatter
            running[kind, l, unit] = make(l, unit, order)
        self.fill()
        self.comm.barrier()
        for name, *rest in steps:
            if not rest:
                next(running[name], None)
            elif hasattr(self, name):
                getattr(self, name)(*rest)
            elif isinstance(rest[1], tuple):
                self.over(getattr(net, name), *rest)
            else:
                getattr(net, name)(*rest)
        for one in self.comm.sent:
            one.wait_send()


INPUTS = ("tokens", "cotangent", "small", "w_qkv", "w_attn", "w_in", "w_out")
OUTPUTS = ("mixed_out", "h", "gsmall", "gw_qkv", "gw_attn", "gw_in", "gw_out")
COPIES = 400


def fused_body(sizes, depth, names, length_ref, *refs):
    named = dict(zip(INPUTS + OUTPUTS + names, refs))
    arrivals = [named.pop("arrive%d" % n) for n in range(3)]
    varrivals = [named.pop("varrive%d" % n) for n in range(3)]
    sems = named.pop("send"), named.pop("recv")
    inner = {n: r for n, r in named.items() if n not in INPUTS}
    net = Net(*sizes, length_ref[0], inner)
    comm = Comm(depth, sems)
    vectors = Vectors(sizes[0], sizes[2], sizes[3])
    Program(net, comm, vectors, dict(named, arrivals=arrivals, varrivals=varrivals)).run()


def fused(mesh, lengths, tokens, cotangent, small, weights):
    layers, _, width = weights[1].shape
    hidden = weights[2].shape[2]
    seq = tokens.shape[0]
    sizes = (layers, seq, width, hidden)
    rows = sum(w.shape[1] * w.shape[2] for w in weights) // width
    groups = group_shape(width, hidden)
    vmem = pl.BlockSpec(memory_space=pltpu.VMEM)
    scratch = dict(Net.scratch(*sizes))
    scratch["packed"] = pltpu.VMEM((layers,) + groups + (rows, width), BF16)
    scratch["grads"] = pltpu.VMEM(groups + (rows, width), BF16)
    scratch["shares"] = pltpu.VMEM(groups + small.shape, BF16)
    scratch["vshares"] = pltpu.VMEM(groups + small.shape, F32)
    kept = (groups[:3], groups[:2], (2 * groups[0] - 1,))
    for n, lead in enumerate(kept):
        scratch["arrive%d" % n] = pltpu.VMEM(lead + (rows, width), BF16)
        scratch["varrive%d" % n] = pltpu.VMEM(lead + small.shape, F32)
    scratch["send"] = pltpu.SemaphoreType.DMA((COPIES,))
    scratch["recv"] = pltpu.SemaphoreType.DMA((COPIES,))
    return pl.pallas_call(
        functools.partial(fused_body, sizes, groups[0], tuple(scratch)),
        out_shape=(
            jax.ShapeDtypeStruct(tokens.shape, BF16),
            jax.ShapeDtypeStruct(tokens.shape, F32),
            jax.ShapeDtypeStruct(small.shape, F32),
        )
        + tuple(jax.ShapeDtypeStruct(w.shape, F32) for w in weights),
        in_specs=[pl.BlockSpec(memory_space=pltpu.SMEM)] + [vmem] * len(INPUTS),
        out_specs=(vmem,) * len(OUTPUTS),
        scratch_shapes=list(scratch.values()),
        compiler_params=pltpu.CompilerParams(
            collective_id=0, has_side_effects=True, vmem_limit_bytes=63 * 2**20
        ),
    )(lengths, tokens, cotangent, small, *weights)


def pack_small(vectors, layers):
    lanes = 128 // layers
    rows = []
    for v, count in zip(vectors, (2, 2, 3, 3, 4, 2)):
        v = v.reshape(layers, -1, v.shape[-1])
        rows.append(jnp.pad(v, ((0, 0), (0, count - v.shape[1]), (0, lanes - v.shape[2]))))
    return jnp.concatenate(rows, axis=1).transpose(1, 0, 2).reshape(VROWS, 128)


def unpack_small(tile, vectors, layers):
    cube = tile.reshape(VROWS, layers, 128 // layers).transpose(1, 0, 2)
    outs = []
    for v, row in zip(vectors, (GAIN, SHIFT, BQKV, BLEND, BIN, OBIAS)):
        count = 1 if v.ndim == 2 else v.shape[1]
        outs.append(cube[:, row : row + count, : v.shape[-1]].reshape(v.shape))
    return outs


def plain_body(sizes, names, length_ref, *refs):
    names = ("tokens", "cotangent", "packed", "vecs", "mixed_out", "h", "grads_out", "vgrads") + names
    named = dict(zip(names, refs))
    net = Net(*sizes, length_ref[0], named)

    def over(body, l):
        @pl.loop(0, net.pairs)
        def _(p):
            body(l, p)

    net.setup()
    net.setup_vecs()
    net.h[...] = named["tokens"][...].astype(F32)
    for l in range(net.layers):
        net.norm(l, 0, net.h)
        for n in range(3):
            net.fwd_qkv(l, n)
        over(net.fwd_near, l)
        over(net.fwd_far, l)
        net.fwd_attn(l)
        for j in range(net.ff_blocks):
            net.fwd_up(l, j)
        for j in range(net.ff_blocks):
            net.fwd_down(l, j)
        net.fwd_end(l)
    named["mixed_out"][...] = net.h[...].astype(BF16)
    net.h[...] = named["cotangent"][...].astype(F32)
    for l in reversed(range(net.layers)):
        net.bwd_start(l, net.h)
        for j in range(net.ff_blocks):
            net.bwd_out(l, j)
            net.bwd_up(l, j)
        net.bwd_attn(l)
        over(net.bwd_near, l)
        over(net.bwd_far, l)
        for n in (2, 1, 0):
            net.bwd_qkv(l, n)
        net.bwd_end(l)
        copy = pltpu.make_async_copy(named["grads"], named["grads_out"].at[l], named["sem"])
        copy.start()
        copy.wait()


def plain(lengths, tokens, cotangent, packed, vecs):
    layers, rows, width = packed.shape[0], packed.shape[-2], packed.shape[-1]
    seq = tokens.shape[0]
    hidden = (rows // GROUP - 4) // 2 * width
    sizes = (layers, seq, width, hidden)
    scratch = dict(Net.scratch(*sizes))
    del scratch["vecs"], scratch["vgrads"]
    scratch["grads"] = pltpu.VMEM(packed.shape[1:], BF16)
    scratch["sem"] = pltpu.SemaphoreType.DMA
    vmem = pl.BlockSpec(memory_space=pltpu.VMEM)
    return pl.pallas_call(
        functools.partial(plain_body, sizes, tuple(scratch)),
        out_shape=(
            jax.ShapeDtypeStruct((seq, width), BF16),
            jax.ShapeDtypeStruct((seq, width), F32),
            jax.ShapeDtypeStruct(packed.shape, BF16),
            jax.ShapeDtypeStruct((layers, VROWS, width), F32),
        ),
        in_specs=[pl.BlockSpec(memory_space=pltpu.SMEM)] + [vmem] * 4,
        out_specs=(vmem, vmem, pl.BlockSpec(memory_space=pl.ANY), vmem),
        scratch_shapes=list(scratch.values()),
        compiler_params=pltpu.CompilerParams(vmem_limit_bytes=63 * 2**20),
    )(lengths, tokens, cotangent, packed, vecs)


BOTH = ("dp", "fsdp")


def general(lengths, tokens, cotangent, vectors, weights):
    whole = lambda v, axis: lax.all_gather(v, BOTH, axis=axis, tiled=True)
    w_all = [whole(w, 1) for w in weights]
    v_all = [whole(v, v.ndim - 1) for v in vectors]
    layers, width, _ = w_all[1].shape
    groups = group_shape(width, w_all[2].shape[2])
    blocks = []
    for w in w_all[:3]:
        cut = w.reshape((layers,) + groups + (GROUP, -1, width))
        blocks.append(jnp.moveaxis(cut, -2, -3).reshape((layers,) + groups + (-1, width)))
    blocks.append(w_all[3].reshape((layers,) + groups + (-1, width)))
    vecs = jnp.concatenate([v.reshape(layers, -1, width) for v in v_all], axis=1).astype(F32)
    mixed, grad_tokens, grads, vgrads = plain(
        lengths, tokens, cotangent, jnp.concatenate(blocks, axis=-2), vecs
    )
    reduce = lambda g, axis: lax.psum_scatter(g, BOTH, scatter_dimension=axis, tiled=True)
    w_grads, first = [], 0
    for n, (w, block) in enumerate(zip(w_all, blocks)):
        part = grads[..., first : first + block.shape[-2], :].astype(F32)
        first += block.shape[-2]
        if n < 3:
            part = part.reshape((layers,) + groups + (-1, GROUP, width))
            part = jnp.moveaxis(part, -3, -2)
        w_grads.append(reduce(part.reshape(w.shape), 1))
    v_grads, first = [], 0
    for v in v_all:
        count = v.size // (layers * width)
        part = vgrads[:, first : first + count].reshape(v.shape)
        first += count
        v_grads.append(reduce(part, v.ndim - 1))
    return mixed, grad_tokens, v_grads, w_grads


def on_device(mesh, tokens, lengths, *rest):
    gains, shifts, w_qkv, b_qkv, w_attn, blends, w_in, b_in, w_out, biases, cotangent = rest
    vectors = (gains, shifts, b_qkv, blends, b_in, biases)
    weights = (w_qkv, w_attn, w_in, w_out)
    layers, _, width = w_attn.shape
    groups = group_shape(width, w_in.shape[2])
    if (mesh.shape["dp"], mesh.shape["fsdp"]) == (groups[0] * groups[1], groups[2] * groups[3]):
        small = pack_small(vectors, layers)
        mixed, grad_tokens, tile, *w_grads = fused(
            mesh, lengths, tokens, cotangent, small, weights
        )
        v_grads = unpack_small(tile, vectors, layers)
    else:
        mixed, grad_tokens, v_grads, w_grads = general(
            lengths, tokens, cotangent, vectors, weights
        )
    d_gains, d_shifts, d_b_qkv, d_blends, d_b_in, d_biases = v_grads
    d_w_qkv, d_w_attn, d_w_in, d_w_out = w_grads
    return (
        mixed,
        grad_tokens,
        d_gains,
        d_shifts,
        d_w_qkv,
        d_b_qkv,
        d_w_attn,
        d_blends,
        d_w_in,
        d_b_in,
        d_w_out,
        d_biases,
    )


def solution(mesh):
    rows, vector = P(BOTH, None), P(None, None, BOTH)
    weight, bias = P(None, BOTH, None), P(None, BOTH)
    in_specs = (
        rows,
        P(BOTH),
        vector,
        vector,
        weight,
        bias,
        weight,
        vector,
        weight,
        bias,
        weight,
        vector,
        rows,
    )
    out_specs = (
        rows,
        rows,
        vector,
        vector,
        weight,
        bias,
        weight,
        vector,
        weight,
        bias,
        weight,
        vector,
    )
    return jax.shard_map(
        functools.partial(on_device, mesh),
        mesh=mesh,
        in_specs=in_specs,
        out_specs=out_specs,
        check_vma=False,
    )
```

```python
import functools
import itertools
import jax
import jax.numpy as jnp
from jax import lax
from jax.experimental import pallas as pl
from jax.experimental.pallas import tpu as pltpu
from jax.sharding import PartitionSpec as P

HD = 64
BAND = 30
EPSILON = 1e-05
MESH = pl.DeviceIdType.MESH
F32 = jnp.float32
BF16 = jnp.bfloat16
GROUP = 16
TILE = 128
PAD = 32
WINDOW = TILE + 2 * PAD
TWINS = {"acc_t": "acc", "gm_t": "normed"}
ROWS = 64
GELU_C = 0.7978845608028654
GELU_A = 0.044715
GAIN, SHIFT, BQKV, BLEND, BIN, OBIAS, VROWS = 0, 2, 4, 7, 10, 14, 16
VECTOR_ROWS = (GAIN, SHIFT, BQKV, BLEND, BIN, OBIAS)


def nn(a, b):
    return jnp.dot(a, b, preferred_element_type=F32)


def nt(a, b):
    return lax.dot_general(a, b, (((1,), (1,)), ((), ())), preferred_element_type=F32)


def split(a):
    high = a.astype(BF16)
    return high, (a - high.astype(F32)).astype(BF16)


def row_index(shape):
    return lax.broadcasted_iota(jnp.int32, shape, 0)


def col_index(shape):
    return lax.broadcasted_iota(jnp.int32, shape, 1)


def head_diag(a):
    return jnp.where((row_index(a.shape) < HD) == (col_index(a.shape) < HD), a, 0.0)


def spread(tile):
    top, bottom = tile[:HD], tile[HD:]
    zero = jnp.zeros_like(top)
    return jnp.concatenate(
        [jnp.concatenate([top, zero], axis=1), jnp.concatenate([zero, bottom], axis=1)], axis=0
    )


def fold(wide):
    half = wide.shape[1] // 2
    return jnp.concatenate([wide[:HD, :half], wide[HD:, half:]], axis=0)


def col_sum(a):
    return jnp.sum(a, axis=0, keepdims=True)


GBLEND = 64


def group_shape(width, hidden):
    first = hidden // width
    return (first, width // GROUP // first // 4, 2, 2)


class Net:
    def __init__(self, layers, seq, width, hidden, length, r):
        self.layers, self.seq, self.width, self.hidden = layers, seq, width, hidden
        self.pairs = width // (2 * HD)
        self.tiles = seq // TILE
        self.length = length
        self.padded = seq + TILE
        self.ff_blocks = hidden // width
        self.groups = group_shape(width, hidden)
        self.__dict__.update(r)
        for name, twin in TWINS.items():
            if name not in r:
                setattr(self, name, r[twin])

    @staticmethod
    def scratch(layers, seq, width, hidden):
        padded = seq + TILE
        pairs = width // (2 * HD)
        tiles = seq // TILE
        ff = hidden // width
        v = pltpu.VMEM
        arrays = dict(
            acc=v((seq, width), F32),
            acc_t=v((width, seq), F32),
            xhat=v((layers, 2, seq, width), BF16),
            rstd=v((seq, 128), F32),
            normed=v((seq, width), BF16),
            normed_t=v((layers, 2, width, seq), BF16),
            q_t=v((layers, width, seq), BF16),
            k_pad=v((layers, padded, width), BF16),
            v_pad=v((layers, padded, width), BF16),
            tr_pad=v((width, padded), BF16),
            probs=v((layers, pairs, tiles, WINDOW, 2 * TILE), BF16),
            near_t=v((layers, width, seq), BF16),
            tanh_t=v((layers, width, seq), BF16),
            s_one=v((layers, pairs, 2 * HD, 2 * HD), F32),
            s_two=v((layers, pairs, 2 * HD, 2 * HD), F32),
            rden=v((layers, pairs, 8, seq), F32),
            mixed_t=v((layers, width, seq), BF16),
            act_t=v((layers, ff, width, seq), BF16),
            dact=v((layers, ff, seq, width), BF16),
            band=v((tiles, WINDOW, 2 * TILE), BF16),
            cols=v((width, 128), F32),
            gm_t=v((width, seq), BF16),
            gk_pad=v((padded, width), F32),
            gv_pad=v((padded, width), F32),
            vecs=v((layers, VROWS, width), F32),
            vgrads=v((layers, VROWS, width), F32),
        )
        return {n: a for n, a in arrays.items() if seq != width or n not in TWINS}

    def w_rows(self, l, first):
        return self.packed[l, :, :, :, :, pl.ds(first, GROUP), :].reshape(self.width, self.width)

    def w_qkv(self, l, n):
        return self.w_rows(l, GROUP * n)

    def w_attn(self, l):
        return self.w_rows(l, 3 * GROUP)

    def w_in(self, l, j):
        return self.w_rows(l, pl.multiple_of(4 * GROUP + GROUP * j, GROUP))

    def out_at(self, j):
        per = self.hidden // (self.width // GROUP)
        return j, pl.ds((4 + self.ff_blocks) * GROUP, per)

    def w_out(self, l, j):
        groups, rows = self.out_at(j)
        return self.packed[l, groups, :, :, :, rows, :].reshape(self.width, self.width)

    def put_rows(self, l, first, value):
        self.grads[:, :, :, :, pl.ds(first, GROUP), :] = value.astype(BF16).reshape(
            self.groups + (GROUP, self.width)
        )

    def put_out(self, l, j, value):
        groups, rows = self.out_at(j)
        per = self.hidden // (self.width // GROUP)
        self.grads[groups, :, :, :, rows, :] = value.astype(BF16).reshape(
            self.groups[1:] + (per, self.width)
        )

    def vec(self, l, row):
        return self.vecs[l, pl.ds(row, 1), :]

    def keep(self, value):
        return jnp.where(row_index(value.shape) < self.length, value, 0.0)

    def setup(self):
        shape = (WINDOW, 2 * TILE)
        key, query = row_index(shape) - PAD, col_index(shape) % TILE
        for t in range(self.tiles):
            pos = key + t * TILE
            ok = (jnp.abs(key - query) <= BAND) & (pos >= 0)
            ok = ok & ((pos < self.length) | (key == query))
            self.band[t] = jnp.where(ok, 0.0, -1e30).astype(BF16)
        zero_head = jnp.zeros((PAD, self.width), BF16)
        zero_tail = jnp.zeros((self.padded - PAD - self.seq, self.width), BF16)
        for l in range(self.layers):
            for ref in (self.k_pad, self.v_pad):
                ref[l, :PAD] = zero_head
                ref[l, PAD + self.seq :] = zero_tail

    def setup_vecs(self):
        eye = (row_index((self.width, self.width)) == col_index((self.width, self.width))).astype(
            BF16
        )
        for l in range(self.layers):
            self.cols[:, VROWS * l : VROWS * (l + 1)] = nt(eye, self.vecs[l].astype(BF16))

    def rows(self, body):
        @pl.loop(0, self.seq // ROWS)
        def _(i):
            body(pl.ds(pl.multiple_of(i * ROWS, ROWS), ROWS))

    def norm(self, l, which, source):
        def body(at):
            value = source[at, :]
            centered = value - jnp.mean(value, axis=-1, keepdims=True)
            rstd = lax.rsqrt(jnp.mean(centered * centered, axis=-1, keepdims=True) + EPSILON)
            xhat = centered * rstd
            n = 2 * l + which
            self.rstd[at, n : n + 1] = rstd
            self.xhat[l, which, at, :] = xhat.astype(BF16)
            normed = xhat * self.vec(l, GAIN + which) + self.vec(l, SHIFT + which)
            self.normed[at, :] = normed.astype(BF16)

        self.rows(body)
        self.normed_t[l, which] = self.normed[...].T

    def pad_keep(self):
        row = row_index((self.padded, 2 * HD)) - PAD
        return (row >= 0) & (row < self.length)

    def fwd_qkv(self, l, n):
        out = (nn(self.normed[...], self.w_qkv(l, n)) + self.vec(l, BQKV + n)).astype(BF16)
        if n == 0:
            self.q_t[l] = out.T
        else:
            (self.k_pad, self.v_pad)[n - 1][l, PAD : PAD + self.seq] = out
        if n == 2:
            self.tr_pad[...] = self.v_pad[l].T

    def pair_at(self, p):
        return pl.ds(pl.multiple_of(p * 2 * HD, 2 * HD), 2 * HD)

    def fwd_near(self, l, p):
        at = self.pair_at(p)
        for t in range(self.tiles):
            here, window = slice(t * TILE, (t + 1) * TILE), slice(t * TILE, t * TILE + WINDOW)
            wide = spread(self.q_t[l, at, here])
            scores = nn(self.k_pad[l, window, at], wide) * (HD**-0.5) + self.band[t].astype(F32)
            weights = jnp.exp(scores - jnp.max(scores, axis=0, keepdims=True))
            inverse = 1.0 / jnp.sum(weights, axis=0, keepdims=True)
            probs = (weights * inverse).astype(BF16)
            self.probs[l, p, t] = probs
            near = fold(nn(self.tr_pad[at, window], probs))
            self.near_t[l, at, here] = near.astype(BF16)

    def features(self, x):
        grown = jnp.exp(jnp.minimum(x, 0.0))
        return jnp.where(x > 0, x + 1.0, grown), grown, jnp.tanh(x)

    def key_features(self, l, at):
        phi, slope, tanh = self.features(self.k_pad[l, :, at].astype(F32))
        ok = self.pad_keep()
        return (
            jnp.where(ok, phi, 0.0).astype(BF16),
            slope,
            jnp.where(ok, tanh, 0.0).astype(BF16),
            tanh,
        )

    def coefficient(self):
        wide = jnp.full((1, 1), HD, F32) * self.length.astype(F32)
        return lax.rsqrt(wide)

    def heads_row(self, two, seq):
        return jnp.concatenate(
            [
                jnp.broadcast_to(two[0:1], (HD, seq)),
                jnp.broadcast_to(two[1:2], (HD, seq)),
            ],
            axis=0,
        )

    def fwd_far(self, l, p):
        at = self.pair_at(p)
        phk, _, tk, _ = self.key_features(l, at)
        values_t = self.tr_pad[at, :]
        s_one = head_diag(nn(values_t, phk))
        s_two = head_diag(nn(values_t, tk))
        total = col_sum(phk.astype(F32))
        self.s_one[l, p], self.s_two[l, p] = s_one, s_two
        phi, _, tanh = self.features(self.q_t[l, at, :].astype(F32))
        phq, tq = phi.astype(BF16), tanh.astype(BF16)
        shape = (8, 2 * HD)
        mine = (row_index(shape) == 0) == (col_index(shape) < HD)
        z_high, z_low = split(jnp.where(mine & (row_index(shape) < 2), total, 0.0))
        den = nn(z_high, phq) + nn(z_low, phq)
        rden = 1.0 / jnp.where(row_index(den.shape) < 2, den, 1.0)
        self.rden[l, p] = rden
        total_col = jnp.broadcast_to(total, (8, 2 * HD)).T
        n = VROWS * l
        self.cols[at, n : n + 1] = total_col[:, 0:1]
        high, low = split(s_one)
        far_elu = (nn(high, phq) + nn(low, phq)) * self.heads_row(rden, self.seq)
        high, low = split(s_two)
        far_tanh = (nn(high, tq) + nn(low, tq)) * self.coefficient()
        self.tanh_t[l, at, :] = far_tanh.astype(BF16)
        blend = self.cols[at, VROWS * l : VROWS * (l + 1)]
        self.mixed_t[l, at, :] = (
            blend[:, BLEND : BLEND + 1] * self.near_t[l, at, :].astype(F32)
            + blend[:, BLEND + 1 : BLEND + 2] * far_elu
            + blend[:, BLEND + 2 : BLEND + 3] * far_tanh
        ).astype(BF16)

    def fwd_attn(self, l):
        mixed = self.mixed_t[l].T
        out = nn(mixed, self.w_attn(l)) + self.vec(l, OBIAS)
        self.gk_pad[: self.seq] = self.h[...] + self.keep(out)
        self.norm(l, 1, self.gk_pad)

    def fwd_up(self, l, j):
        pre = nn(self.normed[...], self.w_in(l, j)) + self.vec(l, BIN + j)
        square = pre * pre
        th = jnp.tanh(GELU_C * pre * (1.0 + GELU_A * square))
        half = 0.5 * (1.0 + th)
        slope = half + (0.5 * GELU_C) * pre * (1.0 - th * th) * (1.0 + 3.0 * GELU_A * square)
        self.dact[l, j] = slope.astype(BF16)
        self.act_t[l, j] = (pre * half).astype(BF16).T

    def fwd_down(self, l, j):
        part = nn(self.act_t[l, j].T, self.w_out(l, j))
        self.acc[...] = part if j == 0 else self.acc[...] + part

    def fwd_end(self, l):
        self.h[...] = self.gk_pad[: self.seq] + self.keep(self.acc[...] + self.vec(l, OBIAS + 1))

    def put_vec(self, l, row, value):
        self.vgrads[l, pl.ds(row, 1), :] = value

    def bwd_start(self, l, source):
        gz = self.keep(source[...].astype(F32)).astype(BF16)
        self.normed[...] = gz
        self.put_vec(l, OBIAS + 1, col_sum(gz.astype(F32)))

    def bwd_out(self, l, j):
        self.put_out(l, j, nn(self.act_t[l, j], self.normed[...]))

    def bwd_up(self, l, j):
        grad = nt(self.normed[...], self.w_out(l, j))
        gpre = (grad * self.dact[l, j].astype(F32)).astype(BF16)
        self.put_vec(l, BIN + j, col_sum(gpre.astype(F32)))
        self.put_rows(l, 4 * GROUP + GROUP * j, nn(self.normed_t[l, 1], gpre))
        part = nt(gpre, self.w_in(l, j))
        self.acc[...] = part if j == 0 else self.acc[...] + part

    def norm_back(self, l, which):
        self.put_vec(l, GAIN + which, jnp.zeros((1, self.width), F32))
        self.put_vec(l, SHIFT + which, jnp.zeros((1, self.width), F32))

        def body(at):
            grad = self.acc[at, :]
            xhat = self.xhat[l, which, at, :].astype(F32)
            self.vgrads[l, pl.ds(GAIN + which, 1), :] += col_sum(grad * xhat)
            self.vgrads[l, pl.ds(SHIFT + which, 1), :] += col_sum(grad)
            grad = grad * self.vec(l, GAIN + which)
            mean = jnp.mean(grad, axis=-1, keepdims=True)
            slope = jnp.mean(grad * xhat, axis=-1, keepdims=True)
            n = 2 * l + which
            self.h[at, :] += self.rstd[at, n : n + 1] * (grad - mean - xhat * slope)

        self.rows(body)

    def bwd_attn(self, l):
        self.norm_back(l, 1)
        go = self.keep(self.h[...]).astype(BF16)
        self.put_vec(l, OBIAS, col_sum(go.astype(F32)))
        self.put_rows(l, 3 * GROUP, nn(self.mixed_t[l], go))
        self.gm_t[...] = nt(self.w_attn(l), go).astype(BF16)
        self.tr_pad[...] = self.k_pad[l].T
        self.gk_pad[...] = jnp.zeros_like(self.gk_pad)
        self.gv_pad[...] = jnp.zeros_like(self.gv_pad)

    def bwd_near(self, l, p):
        at = self.pair_at(p)
        blend = self.cols[at, VROWS * l : VROWS * (l + 1)]
        for t in range(self.tiles):
            here, window = slice(t * TILE, (t + 1) * TILE), slice(t * TILE, t * TILE + WINDOW)
            grad = (blend[:, BLEND : BLEND + 1] * self.gm_t[at, here].astype(F32)).astype(BF16)
            grad = spread(grad)
            probs = self.probs[l, p, t]
            wide = probs.astype(F32)
            dprobs = nn(self.v_pad[l, window, at], grad)
            term = wide * dprobs
            inner = jnp.sum(term, axis=0, keepdims=True)
            gs = ((term - wide * inner) * (HD**-0.5)).astype(BF16)
            self.acc_t[at, here] = fold(nn(self.tr_pad[at, window], gs))
            self.gk_pad[window, at] += nt(gs, spread(self.q_t[l, at, here]))
            self.gv_pad[window, at] += nt(probs, grad)

    def bwd_far(self, l, p):
        at = self.pair_at(p)
        seq = self.seq
        blend = self.cols[at, VROWS * l : VROWS * (l + 1)]
        gm = self.gm_t[at, :].astype(F32)
        q = self.q_t[l, at, :].astype(F32)
        phi_q, slope_q, tanh_q = self.features(q)
        phq, tq = phi_q.astype(BF16), tanh_q.astype(BF16)
        high, low = split(self.s_one[l, p])
        far_elu = (nn(high, phq) + nn(low, phq)) * self.heads_row(self.rden[l, p], seq)
        column = lambda a: jnp.sum(a, axis=1, keepdims=True)
        sums = [
            column(gm * self.near_t[l, at, :].astype(F32)),
            column(gm * far_elu),
            column(gm * self.tanh_t[l, at, :].astype(F32)),
        ]
        for n, one in enumerate(sums):
            self.cols[at, GBLEND + n : GBLEND + n + 1] = one
        phk, slope_k, tk, tanh_k = self.key_features(l, at)
        values = self.v_pad[l, :, at]
        gnum = (blend[:, BLEND + 1 : BLEND + 2] * gm * self.heads_row(self.rden[l, p], seq)).astype(
            BF16
        )
        prod = gnum.astype(F32) * far_elu
        gden_one = -col_sum(prod[:HD])
        gden_two = -col_sum(prod[HD:])
        gden = jnp.concatenate([gden_one, gden_two, jnp.zeros((6, seq), F32)], axis=0)
        s_one = self.s_one[l, p].T
        high, low = split(s_one)
        gphq = nn(high, gnum) + nn(low, gnum) + self.cols[at, VROWS * l : VROWS * l + 1] * self.heads_row(gden, seq)
        gs_one = head_diag(nt(phq, gnum))
        gs_high, gs_low = split(gs_one)
        gden_high, gden_low = split(gden)
        both = nt(gden_high, phq) + nt(gden_low, phq)
        gzz = jnp.where(col_index((1, 2 * HD)) < HD, both[0:1], both[1:2])
        gtanh = (blend[:, BLEND + 2 : BLEND + 3] * gm * self.coefficient()).astype(BF16)
        gtq = nn(self.s_two[l, p].T.astype(BF16), gtanh)
        gs_two = head_diag(nt(tq, gtanh)).astype(BF16)
        self.acc_t[at, :] += gphq * jnp.where(q > 0, 1.0, slope_q) + gtq * (1.0 - tanh_q * tanh_q)
        gphk = nt(values, gs_high) + nt(values, gs_low) + gzz
        gtk = nt(values, gs_two)
        grad_k = gphk * slope_k + gtk * (1.0 - tanh_k * tanh_k)
        self.gk_pad[:, at] += jnp.where(self.pad_keep(), grad_k, 0.0)
        self.gv_pad[:, at] += nn(phk, gs_high) + nn(tk, gs_two)

    def bwd_qkv(self, l, n):
        rows = slice(PAD, PAD + self.seq)
        if n == 0:
            grad = self.acc_t[...].T.astype(BF16)
        else:
            grad = (self.gk_pad, self.gv_pad)[n - 1][rows, :].astype(BF16)
        self.put_vec(l, BQKV + n, col_sum(grad.astype(F32)))
        self.put_rows(l, GROUP * n, nn(self.normed_t[l, 0], grad))
        total = self.gv_pad.at[rows]
        part = nt(grad, self.w_qkv(l, n))
        if n == 2:
            total[...] = part
        elif n == 1:
            total[...] += part
        else:
            self.acc[...] = total[...] + part

    def bwd_end(self, l):
        self.vgrads[l, pl.ds(BLEND, 3), :] = self.cols[...].T[GBLEND : GBLEND + 3]
        self.norm_back(l, 0)


class Comm:
    def __init__(self, depth, sems):
        self.sems = sems
        self.free = ([], [])
        self.made = [0, 0]
        self.clock = 0
        self.heard = {}
        dp, fsdp = lax.axis_index("dp"), lax.axis_index("fsdp")
        self.depth = depth
        self.at = {"z": dp // 2, "x": dp % 2, "y": fsdp // 2, "c": fsdp % 2}

    def device(self, **moved):
        at = dict(self.at, **moved)
        return (at["z"] * 2 + at["x"], at["y"] * 2 + at["c"])

    def steps(self, axis):
        return range(1, self.depth) if axis == "z" else range(1, 2)

    def other(self, axis, step=1):
        if axis == "z":
            return lax.rem(self.at["z"] + step, self.depth)
        return 1 - self.at[axis]

    def barrier(self):
        semaphore = pltpu.get_barrier_semaphore()
        peers = [
            self.device(**{axis: self.other(axis, k)}) for axis in "zxyc" for k in self.steps(axis)
        ]
        for peer in peers:
            pl.semaphore_signal(semaphore, inc=1, device_id=peer, device_id_type=MESH)
        pl.semaphore_wait(semaphore, len(peers))

    def take(self, side, before):
        for entry in self.free[side]:
            if entry[0] < before:
                self.free[side].remove(entry)
                return entry[1]
        self.made[side] += 1
        return self.made[side] - 1

    def copy(self, source, target, axis, step):
        self.clock += 1
        sent = self.take(0, self.clock)
        arrived = self.take(1, self.heard.get((axis, step), -1))
        made = pltpu.make_async_remote_copy(
            src_ref=source,
            dst_ref=target,
            send_sem=self.sems[0].at[sent],
            recv_sem=self.sems[1].at[arrived],
            device_id=self.device(**{axis: self.other(axis, step)}),
            device_id_type=MESH,
        )
        made.start()
        back = (axis, self.depth - step if axis == "z" else 1)
        return made, sent, arrived, back, self.clock

    def wait(self, copies):
        for made, sent, arrived, back, when in copies:
            made.wait()
            self.clock += 1
            self.free[0].append((self.clock, sent))
            self.free[1].append((self.clock, arrived))
            self.heard[back] = max(when, self.heard.get(back, -1))

    def index(self, whole, moved=None):
        at = dict(self.at, **(moved or {}))
        return tuple(slice(None) if axis in whole else at[axis] for axis in "zxyc")

    def gather(self, view, order):
        cores = []
        for stage in range(4):
            whole, started = order[:stage], []
            if stage < 3:
                axis = order[stage]
                block = view(self.index(whole))
                started = [self.copy(block, block, axis, k) for k in self.steps(axis)]
            if "z" in whole:
                axis = order[stage - 1]
                if axis == "z":
                    block = view(self.index(whole))
                else:
                    block = view(self.index(order[: stage - 1], {axis: self.other(axis)}))
                cores.append(self.copy(block, block, "c", 1))
            yield
            self.wait(started)
        self.wait(cores)

    @staticmethod
    def add(mine, others):
        @pl.loop(0, mine.shape[0])
        def _(n):
            for rest in itertools.product(*[range(m) for m in mine.shape[1:-2]]):
                at = (n,) + rest
                total = mine[at]
                for other in others:
                    total = total + other[at]
                mine[at] = total

    def scatter(self, view, slot, order, put):
        axes = "c" + order
        for stage, axis in enumerate(axes):
            whole = axes[stage + 1 :]
            started = []
            for k in self.steps(axis):
                block = view(self.index(whole, {axis: self.other(axis, k)}))
                started.append(self.copy(block, slot(stage, k - 1), axis, k))
            yield
            self.wait(started)
            mine = view(self.index(whole))
            arrived = [slot(stage, k - 1) for k in self.steps(axis)]
            if whole:
                self.add(mine, arrived)
            else:
                total = mine[...].astype(F32)
                for one in arrived:
                    total = total + one[...].astype(F32)
                put(total)


ORDERS = {
    ("gather", 0): (
        "zxy", "zyx", "zxy", "zxy", "zxy", "zxy",
        "zxy", "zxy", "zyx", "yzx", "yzx", "zyx",
    ),
    ("gather", 1): (
        "zyx", "yzx", "xzy", "zxy", "xzy", "zyx",
        "zxy", "zxy", "yzx", "yzx", "zyx", "xzy",
    ),
    ("scatter", 0): (
        "xyz", "yzx", "xyz", "xyz", "yzx", "yzx",
        "yxz", "xyz", "xyz", "xyz", "yzx", "xyz",
    ),
    ("scatter", 1): (
        "yxz", "xzy", "xzy", "yxz", "yzx", "xyz",
        "yxz", "xyz", "yxz", "xzy", "xzy", "yxz",
    ),
}
LINK, HOP = 0.0235, 1.8
CORE, CORE_HOP = 0.0027, 0.9
ISSUE, BACKLOG, AHEAD = 0.04, 6.0, 12


def plan(layers, segments, parts):
    size = {"z": 4, "x": 2, "y": 2, "c": 2}
    free = dict.fromkeys("zxyc", 0.0)
    clock, steps = 0.0, []
    stage = dict.fromkeys(parts, 0)
    ready = {n: 0.0 if not scatter else None for n, (_, _, scatter) in parts.items()}
    done = set()
    waiting = list(segments)

    def send(axis, blocks, rows):
        link, hop = (CORE, CORE_HOP) if axis == "c" else (LINK, HOP)
        load = blocks * rows * link * (size["z"] if axis == "z" else 1)
        free[axis] = max(free[axis], clock) + load
        return free[axis] + hop

    def count(axes):
        total = 1
        for axis in axes:
            total *= size[axis]
        return total

    def step(name):
        nonlocal clock
        rows, order, scatter = parts[name]
        now = stage[name]
        steps.append((name,))
        stage[name] += 1
        last = 4
        if scatter:
            axes = "c" + order
            if now > 0:
                clock += 0.02 + count(axes[now:]) * rows * 0.0002
            if now < last:
                arrives = send(axes[now], count(axes[now + 1 :]), rows)
                clock += ISSUE * (3 if axes[now] == "z" else 1)
        else:
            arrives = ready[name]
            if now < 3:
                arrives = send(order[now], count(order[:now]), rows)
                clock += ISSUE * (3 if order[now] == "z" else 1)
            if "z" in order[:now] and now < last:
                whole = order[:now] if order[now - 1] == "z" else order[: now - 1]
                core = send("c", count(whole), rows)
                clock += ISSUE
                if now == 3:
                    arrives = core
        if now == last:
            done.add(name)
            ready[name] = None
        else:
            ready[name] = arrives

    def startable(name):
        _, order, scatter = parts[name]
        first = "c" if scatter else order[0]
        return stage[name] > 0 or free[first] <= clock + BACKLOG

    while len(done) < len(parts) or waiting:
        left = [n for n in parts if n not in done][:AHEAD]
        able = [n for n in left if ready[n] is not None and ready[n] <= clock and startable(n)]
        if able:
            step(able[0])
            continue
        if waiting:
            name, layer, argument, cost, needs, makes = waiting[0]
            if all(n in done for n in needs):
                waiting.pop(0)
                steps.append((name, layer, argument))
                clock += cost
                for n in makes:
                    ready[n] = clock
                continue
        later = [ready[n] for n in left if ready[n] is not None and ready[n] > clock]
        later += [free[a] - BACKLOG for a in "zxyc" if free[a] - BACKLOG > clock]
        clock = min(later)
    return steps, clock


def make_plan(layers, pairs, ff, rows):
    units = rows // GROUP
    parts = {("gather", 0, "vectors"): (4, "zxy", False)}
    for l in range(layers):
        for u in range(units):
            parts["gather", l, u] = (GROUP, ORDERS["gather", l][u], False)
    late = list(range(units - ff, units)) + list(range(4, units - ff)) + [3, 2, 1, 0]
    for l in reversed(range(layers)):
        for u in late:
            parts["scatter", l, u] = (GROUP, ORDERS["scatter", l][u], True)
    parts["scatter", 0, "vectors"] = (8, "yxz", True)
    gathers = lambda l, us: [("gather", l, u) for u in us]
    scatters = lambda l, us: [("scatter", l, u) for u in us]
    downs = range(units - ff, units)
    segments = []
    add = lambda *s: segments.append(s)
    halves = [(0, pairs // 2), (pairs // 2, pairs)]
    add("start", 0, None, 0.5, [], [])
    add("spread", 0, None, 0.5, [("gather", 0, "vectors")], [])
    for l in range(layers):
        add("norm", l, 0, 0.7, [], [])
        for n in range(3):
            add("fwd_qkv", l, n, 0.4, gathers(l, [n]), [])
        for half in halves:
            add("fwd_near", l, half, 2.5, [], [])
        for half in halves:
            add("fwd_far", l, half, 1.3, [], [])
        add("fwd_attn", l, None, 2.1, gathers(l, [3]), [])
        for j in range(ff):
            add("fwd_up", l, j, 0.85, gathers(l, [4 + j]), [])
        if l == layers - 1:
            add("bwd_start", l, None, 0.3, [], [])
            for j in range(ff):
                add("bwd_out", l, j, 0.3, [], scatters(l, downs) if j == ff - 1 else [])
        for j in range(ff):
            add("fwd_down", l, j, 0.35, gathers(l, downs) if j == 0 else [], [])
        add("fwd_end", l, None, 0.3, [], [])
    for l in reversed(range(layers)):
        again = lambda us: scatters(l + 1, us) if l < layers - 1 else []
        if l < layers - 1:
            add("bwd_start", l, None, 0.3, [], [])
            for j in range(ff):
                makes = scatters(l, downs) if j == ff - 1 else []
                add("bwd_out", l, j, 0.3, again(downs) if j == 0 else [], makes)
        for j in range(ff):
            add("bwd_up", l, j, 1.2, again([4 + j]), scatters(l, [4 + j]))
        add("bwd_attn", l, None, 2.1, again([3]), scatters(l, [3]))
        for half in halves:
            add("bwd_near", l, half, 2.6, [], [])
        for half in halves:
            add("bwd_far", l, half, 1.9, [], [])
        for n in (2, 1, 0):
            add("bwd_qkv", l, n, 0.9, again([n]), scatters(l, [n]))
        add("bwd_end", l, None, 0.8, [], [])
    add("collect", 0, None, 0.5, [], scatters(0, ["vectors"]))
    return plan(layers, segments, parts), parts


class Vectors:
    def __init__(self, layers, width, hidden):
        self.layers, self.width = layers, width
        self.devices = width // GROUP
        self.long = [(BQKV, 3), (BIN, hidden // width)]

    def swap(self, tiles, back):
        lane = lax.broadcasted_iota(jnp.int32, tiles.shape, 2)
        result = tiles
        for l in range(self.layers):
            for row, count in self.long:
                first = l * VROWS + row
                columns = [tiles[:, :, first + n : first + n + 1] for n in range(count)]
                if back:
                    both = jnp.stack(columns, axis=1).reshape(count, self.devices, GROUP, 1)
                    columns = [both[n] for n in range(count)]
                else:
                    both = jnp.concatenate(columns, axis=0)
                    both = both.reshape(self.devices, count, GROUP, 1)
                    columns = [both[:, n] for n in range(count)]
                for n in range(count):
                    result = jnp.where(lane == first + n, columns[n], result)
        return result

    def spread(self, shares, vecs, cols):
        tiles = shares[...].reshape(self.devices, GROUP, 128).astype(F32)
        columns = self.swap(tiles, True).reshape(self.width, 128)
        cols[...] = columns
        vecs[...] = columns.T[: self.layers * VROWS].reshape(vecs.shape)

    def collect(self, vgrads, shares):
        rows = vgrads[...].reshape(self.layers * VROWS, self.width)
        rest = jnp.zeros((128 - self.layers * VROWS, self.width), F32)
        columns = jnp.concatenate([rows, rest], axis=0).T
        tiles = self.swap(columns.reshape(self.devices, GROUP, 128), False)
        shares[...] = tiles.reshape(shares.shape)

    def pack(self, refs, table):
        table[...] = jnp.zeros_like(table)
        for l in range(self.layers):
            for ref, row in zip(refs, VECTOR_ROWS):
                row += l * VROWS
                if len(ref.shape) == 3:
                    table[row : row + ref.shape[1], :GROUP] = ref[l].astype(F32)
                else:
                    value = ref[l : l + 1, :].astype(F32)
                    for n in range(ref.shape[1] // GROUP):
                        piece = value[:, n * GROUP : (n + 1) * GROUP]
                        table[row + n : row + n + 1, :GROUP] = piece
        return table[...].T[:GROUP]

    def unpack(self, tile, table, refs):
        rest = jnp.zeros((128 - GROUP, 128), F32)
        table[...] = jnp.concatenate([tile, rest], axis=0).T
        for l in range(self.layers):
            for ref, row in zip(refs, VECTOR_ROWS):
                row += l * VROWS
                if len(ref.shape) == 3:
                    ref[l] = table[row : row + ref.shape[1], :GROUP]
                else:
                    count = ref.shape[1] // GROUP
                    rows = [table[row + n : row + n + 1, :GROUP] for n in range(count)]
                    ref[l : l + 1, :] = jnp.concatenate(rows, axis=1)


class Program:
    def __init__(self, net, comm, vectors, r):
        self.net, self.comm, self.vectors = net, comm, vectors
        self.__dict__.update(r)

    def fill(self):
        own = self.comm.index(())
        width = self.net.width
        for l in range(self.net.layers):
            first = 0
            for ref in (self.w_qkv, self.w_attn, self.w_in):
                for n in range(ref.shape[2] // width):
                    rows = pl.ds(first, GROUP)
                    self.net.packed[(l,) + own + (rows,)] = ref[l, :, n * width : (n + 1) * width]
                    first += GROUP
            rows = pl.ds(first, self.w_out.shape[1])
            self.net.packed[(l,) + own + (rows,)] = self.w_out[l]
        refs = [getattr(self, name) for name in VECTORS]
        self.shares[own] = self.vectors.pack(refs, self.table).astype(BF16)

    def gather(self, l, unit, order):
        if unit == "vectors":
            return self.comm.gather(lambda index: self.shares.at[index], order)
        at = pl.ds(unit * GROUP, GROUP)
        return self.comm.gather(lambda index: self.net.packed.at[(l,) + index + (at,)], order)

    def scatter(self, l, unit, order):
        if unit == "vectors":
            arrivals, at, source = self.varrivals, (), self.vshares
        else:
            at = (pl.ds(unit * GROUP, GROUP),)
            arrivals, source = self.arrivals, self.net.grads
        depth = self.comm.depth
        every = slice(None)

        def slot(stage, k):
            if stage < 2:
                return arrivals[stage].at[(every,) * (3 - stage) + at]
            if stage == 2:
                span = slice(2 * k, 2 * k + 2) if order[1] == "z" else slice(0, depth)
                return arrivals[2].at[(span,) + at]
            return arrivals[2].at[(2 * (depth - 1) if order[1] == "z" else depth + k,) + at]

        put = functools.partial(self.put, l, unit)
        return self.comm.scatter(lambda index: source.at[index + at], slot, order, put)

    def put(self, l, unit, total):
        if unit == "vectors":
            self.gsmall[...] = total
            return
        width = self.net.width
        for ref in (self.gw_qkv, self.gw_attn, self.gw_in):
            count = ref.shape[2] // width
            if unit < count:
                ref[l, :, unit * width : (unit + 1) * width] = total
                return
            unit -= count
        self.gw_out[l, unit * GROUP : (unit + 1) * GROUP, :] = total

    def start(self, l, _):
        self.net.setup()
        self.net.h[...] = self.tokens[...].astype(F32)

    def spread(self, l, _):
        self.vectors.spread(self.shares, self.net.vecs, self.net.cols)

    def collect(self, l, _):
        self.vectors.collect(self.net.vgrads, self.vshares)

    def norm(self, l, _):
        self.net.norm(l, 0, self.net.h)

    def fwd_attn(self, l, _):
        self.net.fwd_attn(l)

    def fwd_end(self, l, _):
        self.net.fwd_end(l)
        if l == self.net.layers - 1:
            self.mixed_out[...] = self.net.h[...].astype(BF16)
            self.net.h[...] = self.cotangent[...].astype(F32)

    def bwd_start(self, l, _):
        self.net.bwd_start(l, self.cotangent if l == self.net.layers - 1 else self.net.h)

    def bwd_attn(self, l, _):
        self.net.bwd_attn(l)

    def bwd_end(self, l, _):
        self.net.bwd_end(l)

    def over(self, body, l, span):
        @pl.loop(*span)
        def _(p):
            body(l, p)

    def run(self):
        net = self.net
        rows = net.packed.shape[-2]
        (steps, _), parts = make_plan(net.layers, net.pairs, net.ff_blocks, rows)
        running = {}
        for (kind, l, unit), (_, order, _) in parts.items():
            make = self.gather if kind == "gather" else self.scatter
            running[kind, l, unit] = make(l, unit, order)
        self.fill()
        self.comm.barrier()
        for name, *rest in steps:
            if not rest:
                next(running[name], None)
            elif hasattr(self, name):
                getattr(self, name)(*rest)
            elif isinstance(rest[1], tuple):
                self.over(getattr(net, name), *rest)
            else:
                getattr(net, name)(*rest)
        assert max(self.comm.made) <= SEMAPHORES


VECTORS = ("gains", "shifts", "b_qkv", "blends", "b_in", "biases")
WEIGHTS = ("w_qkv", "w_attn", "w_in", "w_out")
INPUTS = ("tokens", "cotangent") + VECTORS + WEIGHTS
OUTPUTS = ("mixed_out", "h", "gsmall", "gw_qkv", "gw_attn", "gw_in", "gw_out")
SEMAPHORES = 96


def fused_body(sizes, depth, names, length_ref, *refs):
    named = dict(zip(INPUTS + OUTPUTS + names, refs))
    arrivals = [named.pop("arrive%d" % n) for n in range(3)]
    varrivals = [named.pop("varrive%d" % n) for n in range(3)]
    sems = named.pop("send"), named.pop("recv")
    inner = {n: r for n, r in named.items() if n not in INPUTS}
    net = Net(*sizes, length_ref[0], inner)
    comm = Comm(depth, sems)
    vectors = Vectors(sizes[0], sizes[2], sizes[3])
    Program(net, comm, vectors, dict(named, arrivals=arrivals, varrivals=varrivals)).run()


def fused(lengths, tokens, cotangent, vectors, weights):
    layers, _, width = weights[1].shape
    hidden = weights[2].shape[2]
    seq = tokens.shape[0]
    sizes = (layers, seq, width, hidden)
    rows = sum(w.shape[1] * w.shape[2] for w in weights) // width
    groups = group_shape(width, hidden)
    tile = (GROUP, 128)
    vmem = pl.BlockSpec(memory_space=pltpu.VMEM)
    scratch = dict(Net.scratch(*sizes))
    scratch["packed"] = pltpu.VMEM((layers,) + groups + (rows, width), BF16)
    scratch["grads"] = pltpu.VMEM(groups + (rows, width), BF16)
    scratch["shares"] = pltpu.VMEM(groups + tile, BF16)
    scratch["vshares"] = pltpu.VMEM(groups + tile, F32)
    scratch["table"] = pltpu.VMEM((128, 128), F32)
    kept = (groups[:3], groups[:2], (2 * groups[0] - 1,))
    for n, lead in enumerate(kept):
        scratch["arrive%d" % n] = pltpu.VMEM(lead + (rows, width), BF16)
        scratch["varrive%d" % n] = pltpu.VMEM(lead + tile, F32)
    scratch["send"] = pltpu.SemaphoreType.DMA((SEMAPHORES,))
    scratch["recv"] = pltpu.SemaphoreType.DMA((SEMAPHORES,))
    return pl.pallas_call(
        functools.partial(fused_body, sizes, groups[0], tuple(scratch)),
        out_shape=(
            jax.ShapeDtypeStruct(tokens.shape, BF16),
            jax.ShapeDtypeStruct(tokens.shape, F32),
            jax.ShapeDtypeStruct(tile, F32),
        )
        + tuple(jax.ShapeDtypeStruct(w.shape, F32) for w in weights),
        in_specs=[pl.BlockSpec(memory_space=pltpu.SMEM)] + [vmem] * len(INPUTS),
        out_specs=(vmem,) * len(OUTPUTS),
        scratch_shapes=list(scratch.values()),
        compiler_params=pltpu.CompilerParams(
            collective_id=0, has_side_effects=True, vmem_limit_bytes=63 * 2**20
        ),
    )(lengths, tokens, cotangent, *vectors, *weights)


def finish_body(vectors, big, *refs):
    sources, tile, refs = refs[:big], refs[big], refs[big + 1 :]
    targets, outs, table, sems = refs[:big], refs[big : -big - 2], refs[-big - 2], refs[-big - 1]
    buffers = refs[-big:]
    loads = [
        pltpu.make_async_copy(source, buffer, sems.at[0, n])
        for n, (source, buffer) in enumerate(zip(sources, buffers))
    ]
    stores = [
        pltpu.make_async_copy(buffer, target, sems.at[1, n])
        for n, (buffer, target) in enumerate(zip(buffers, targets))
    ]
    for one in loads:
        one.start()
    vectors.unpack(tile[...], table, outs)
    for load, store in zip(loads, stores):
        load.wait()
        store.start()
    for one in stores:
        one.wait()


def finish(vectors, large, tile, shapes):
    anywhere, vmem = pl.BlockSpec(memory_space=pl.ANY), pl.BlockSpec(memory_space=pltpu.VMEM)
    outs = pl.pallas_call(
        functools.partial(finish_body, vectors, len(large)),
        out_shape=tuple(jax.ShapeDtypeStruct(a.shape, a.dtype) for a in large)
        + tuple(jax.ShapeDtypeStruct(shape, F32) for shape in shapes),
        in_specs=[anywhere] * len(large) + [vmem],
        out_specs=(anywhere,) * len(large) + (vmem,) * len(shapes),
        scratch_shapes=[
            pltpu.VMEM((128, 128), F32),
            pltpu.SemaphoreType.DMA((2, len(large))),
        ]
        + [pltpu.VMEM(a.shape, a.dtype) for a in large],
        compiler_params=pltpu.CompilerParams(vmem_limit_bytes=62 * 2**20),
    )(*large, tile)
    return outs[: len(large)], outs[len(large) :]


def plain_body(sizes, names, length_ref, *refs):
    names = ("tokens", "cotangent", "packed", "vecs", "mixed_out", "h", "grads_out", "vgrads") + names
    named = dict(zip(names, refs))
    net = Net(*sizes, length_ref[0], named)

    def over(body, l):
        @pl.loop(0, net.pairs)
        def _(p):
            body(l, p)

    net.setup()
    net.setup_vecs()
    net.h[...] = named["tokens"][...].astype(F32)
    for l in range(net.layers):
        net.norm(l, 0, net.h)
        for n in range(3):
            net.fwd_qkv(l, n)
        over(net.fwd_near, l)
        over(net.fwd_far, l)
        net.fwd_attn(l)
        for j in range(net.ff_blocks):
            net.fwd_up(l, j)
        for j in range(net.ff_blocks):
            net.fwd_down(l, j)
        net.fwd_end(l)
    named["mixed_out"][...] = net.h[...].astype(BF16)
    net.h[...] = named["cotangent"][...].astype(F32)
    for l in reversed(range(net.layers)):
        net.bwd_start(l, net.h)
        for j in range(net.ff_blocks):
            net.bwd_out(l, j)
            net.bwd_up(l, j)
        net.bwd_attn(l)
        over(net.bwd_near, l)
        over(net.bwd_far, l)
        for n in (2, 1, 0):
            net.bwd_qkv(l, n)
        net.bwd_end(l)
        copy = pltpu.make_async_copy(named["grads"], named["grads_out"].at[l], named["sem"])
        copy.start()
        copy.wait()


def plain(lengths, tokens, cotangent, packed, vecs):
    layers, rows, width = packed.shape[0], packed.shape[-2], packed.shape[-1]
    seq = tokens.shape[0]
    hidden = (rows // GROUP - 4) // 2 * width
    sizes = (layers, seq, width, hidden)
    scratch = dict(Net.scratch(*sizes))
    del scratch["vecs"], scratch["vgrads"]
    scratch["grads"] = pltpu.VMEM(packed.shape[1:], BF16)
    scratch["sem"] = pltpu.SemaphoreType.DMA
    vmem = pl.BlockSpec(memory_space=pltpu.VMEM)
    return pl.pallas_call(
        functools.partial(plain_body, sizes, tuple(scratch)),
        out_shape=(
            jax.ShapeDtypeStruct((seq, width), BF16),
            jax.ShapeDtypeStruct((seq, width), F32),
            jax.ShapeDtypeStruct(packed.shape, BF16),
            jax.ShapeDtypeStruct((layers, VROWS, width), F32),
        ),
        in_specs=[pl.BlockSpec(memory_space=pltpu.SMEM)] + [vmem] * 4,
        out_specs=(vmem, vmem, pl.BlockSpec(memory_space=pl.ANY), vmem),
        scratch_shapes=list(scratch.values()),
        compiler_params=pltpu.CompilerParams(vmem_limit_bytes=63 * 2**20),
    )(lengths, tokens, cotangent, packed, vecs)


BOTH = ("dp", "fsdp")


def general(lengths, tokens, cotangent, vectors, weights):
    whole = lambda v, axis: lax.all_gather(v, BOTH, axis=axis, tiled=True)
    w_all = [whole(w, 1) for w in weights]
    v_all = [whole(v, v.ndim - 1) for v in vectors]
    layers, width, _ = w_all[1].shape
    groups = group_shape(width, w_all[2].shape[2])
    blocks = []
    for w in w_all[:3]:
        cut = w.reshape((layers,) + groups + (GROUP, -1, width))
        blocks.append(jnp.moveaxis(cut, -2, -3).reshape((layers,) + groups + (-1, width)))
    blocks.append(w_all[3].reshape((layers,) + groups + (-1, width)))
    vecs = jnp.concatenate([v.reshape(layers, -1, width) for v in v_all], axis=1).astype(F32)
    mixed, grad_tokens, grads, vgrads = plain(
        lengths, tokens, cotangent, jnp.concatenate(blocks, axis=-2), vecs
    )
    reduce = lambda g, axis: lax.psum_scatter(g, BOTH, scatter_dimension=axis, tiled=True)
    w_grads, first = [], 0
    for n, (w, block) in enumerate(zip(w_all, blocks)):
        part = grads[..., first : first + block.shape[-2], :].astype(F32)
        first += block.shape[-2]
        if n < 3:
            part = part.reshape((layers,) + groups + (-1, GROUP, width))
            part = jnp.moveaxis(part, -3, -2)
        w_grads.append(reduce(part.reshape(w.shape), 1))
    v_grads, first = [], 0
    for v in v_all:
        count = v.size // (layers * width)
        part = vgrads[:, first : first + count].reshape(v.shape)
        first += count
        v_grads.append(reduce(part, v.ndim - 1))
    return mixed, grad_tokens, v_grads, w_grads


def on_device(mesh, tokens, lengths, *rest):
    gains, shifts, w_qkv, b_qkv, w_attn, blends, w_in, b_in, w_out, biases, cotangent = rest
    vectors = (gains, shifts, b_qkv, blends, b_in, biases)
    weights = (w_qkv, w_attn, w_in, w_out)
    layers, _, width = w_attn.shape
    groups = group_shape(width, w_in.shape[2])
    if (mesh.shape["dp"], mesh.shape["fsdp"]) == (groups[0] * groups[1], groups[2] * groups[3]):
        mixed, grad_tokens, tile, *w_grads = fused(
            lengths, tokens, cotangent, vectors, weights
        )
        large, v_grads = finish(
            Vectors(layers, width, w_in.shape[2]),
            (mixed, grad_tokens, *w_grads),
            tile,
            [v.shape for v in vectors],
        )
        mixed, grad_tokens, *w_grads = large
    else:
        mixed, grad_tokens, v_grads, w_grads = general(
            lengths, tokens, cotangent, vectors, weights
        )
    d_gains, d_shifts, d_b_qkv, d_blends, d_b_in, d_biases = v_grads
    d_w_qkv, d_w_attn, d_w_in, d_w_out = w_grads
    return (
        mixed,
        grad_tokens,
        d_gains,
        d_shifts,
        d_w_qkv,
        d_b_qkv,
        d_w_attn,
        d_blends,
        d_w_in,
        d_b_in,
        d_w_out,
        d_biases,
    )


def solution(mesh):
    rows, vector = P(BOTH, None), P(None, None, BOTH)
    weight, bias = P(None, BOTH, None), P(None, BOTH)
    in_specs = (
        rows,
        P(BOTH),
        vector,
        vector,
        weight,
        bias,
        weight,
        vector,
        weight,
        bias,
        weight,
        vector,
        rows,
    )
    out_specs = (
        rows,
        rows,
        vector,
        vector,
        weight,
        bias,
        weight,
        vector,
        weight,
        bias,
        weight,
        vector,
    )
    return jax.shard_map(
        functools.partial(on_device, mesh),
        mesh=mesh,
        in_specs=in_specs,
        out_specs=out_specs,
        check_vma=False,
    )
```

```python
import functools
import itertools
import jax
import jax.numpy as jnp
from jax import lax
from jax.experimental import pallas as pl
from jax.experimental.pallas import tpu as pltpu
from jax.sharding import PartitionSpec as P

HD = 64
BAND = 30
EPSILON = 1e-05
MESH = pl.DeviceIdType.MESH
F32 = jnp.float32
BF16 = jnp.bfloat16
GROUP = 16
TILE = 128
PAD = 32
WINDOW = TILE + 2 * PAD
TWINS = {"acc_t": "acc", "gm_t": "normed"}
STEP = 2
ROWS = 512
GELU_C = 0.7978845608028654
GELU_A = 0.044715
GAIN, SHIFT, BQKV, BLEND, BIN, OBIAS, VROWS = 0, 2, 4, 7, 10, 14, 16
VECTOR_ROWS = (GAIN, SHIFT, BQKV, BLEND, BIN, OBIAS)


def nn(a, b):
    return jnp.dot(a, b, preferred_element_type=F32)


def nt(a, b):
    return lax.dot_general(a, b, (((1,), (1,)), ((), ())), preferred_element_type=F32)


def split(a):
    high = a.astype(BF16)
    return high, (a - high.astype(F32)).astype(BF16)


def row_index(shape):
    return lax.broadcasted_iota(jnp.int32, shape, 0)


def col_index(shape):
    return lax.broadcasted_iota(jnp.int32, shape, 1)


def head_diag(a):
    return jnp.where((row_index(a.shape) < HD) == (col_index(a.shape) < HD), a, 0.0)


def spread(tile):
    top, bottom = tile[:HD], tile[HD:]
    zero = jnp.zeros_like(top)
    return jnp.concatenate(
        [jnp.concatenate([top, zero], axis=1), jnp.concatenate([zero, bottom], axis=1)], axis=0
    )


def fold(wide):
    half = wide.shape[1] // 2
    return jnp.concatenate([wide[:HD, :half], wide[HD:, half:]], axis=0)


def col_sum(a):
    return jnp.sum(a, axis=0, keepdims=True)


GBLEND = 64


def group_shape(width, hidden):
    first = hidden // width
    return (first, width // GROUP // first // 4, 2, 2)


class Net:
    def __init__(self, layers, seq, width, hidden, length, r):
        self.layers, self.seq, self.width, self.hidden = layers, seq, width, hidden
        self.pairs = width // (2 * HD)
        self.tiles = seq // TILE
        self.length = length
        self.padded = seq + TILE
        self.ff_blocks = hidden // width
        self.groups = group_shape(width, hidden)
        self.__dict__.update(r)
        for name, twin in TWINS.items():
            if name not in r:
                setattr(self, name, r[twin])

    @staticmethod
    def scratch(layers, seq, width, hidden):
        padded = seq + TILE
        pairs = width // (2 * HD)
        tiles = seq // TILE
        ff = hidden // width
        v = pltpu.VMEM
        arrays = dict(
            acc=v((seq, width), F32),
            acc_t=v((width, seq), F32),
            xhat=v((layers, 2, seq, width), BF16),
            rstd=v((seq, 128), F32),
            normed=v((seq, width), BF16),
            normed_t=v((layers, 2, width, seq), BF16),
            q_t=v((layers, width, seq), BF16),
            k_pad=v((layers, padded, width), BF16),
            v_pad=v((layers, padded, width), BF16),
            tr_pad=v((width, padded), BF16),
            probs=v((layers, pairs, tiles, WINDOW, 2 * TILE), BF16),
            near_t=v((layers, width, seq), BF16),
            tanh_t=v((layers, width, seq), BF16),
            s_one=v((layers, pairs, 2 * HD, 2 * HD), F32),
            s_two=v((layers, pairs, 2 * HD, 2 * HD), F32),
            rden=v((layers, pairs, 8, seq), F32),
            mixed_t=v((layers, width, seq), BF16),
            act_t=v((layers, ff, width, seq), BF16),
            dact=v((layers, ff, seq, width), BF16),
            band=v((tiles, WINDOW, 2 * TILE), BF16),
            cols=v((width, 128), F32),
            gm_t=v((width, seq), BF16),
            gk_pad=v((padded, width), F32),
            gv_pad=v((padded, width), F32),
            vecs=v((layers, VROWS, width), F32),
            vgrads=v((layers, VROWS, width), F32),
        )
        return {n: a for n, a in arrays.items() if seq != width or n not in TWINS}

    def w_rows(self, l, first):
        return self.packed[l, :, :, :, :, pl.ds(first, GROUP), :].reshape(self.width, self.width)

    def w_qkv(self, l, n):
        return self.w_rows(l, GROUP * n)

    def w_attn(self, l):
        return self.w_rows(l, 3 * GROUP)

    def w_in(self, l, j):
        return self.w_rows(l, pl.multiple_of(4 * GROUP + GROUP * j, GROUP))

    def out_at(self, j):
        per = self.hidden // (self.width // GROUP)
        return j, pl.ds((4 + self.ff_blocks) * GROUP, per)

    def w_out(self, l, j):
        groups, rows = self.out_at(j)
        return self.packed[l, groups, :, :, :, rows, :].reshape(self.width, self.width)

    def put_rows(self, l, first, value):
        self.grads[:, :, :, :, pl.ds(first, GROUP), :] = value.astype(BF16).reshape(
            self.groups + (GROUP, self.width)
        )

    def put_out(self, l, j, value):
        groups, rows = self.out_at(j)
        per = self.hidden // (self.width // GROUP)
        self.grads[groups, :, :, :, rows, :] = value.astype(BF16).reshape(
            self.groups[1:] + (per, self.width)
        )

    def vec(self, l, row):
        return self.vecs[l, pl.ds(row, 1), :]

    def keep(self, value):
        return jnp.where(row_index(value.shape) < self.length, value, 0.0)

    def setup(self):
        shape = (WINDOW, 2 * TILE)
        key, query = row_index(shape) - PAD, col_index(shape) % TILE
        for t in range(self.tiles):
            pos = key + t * TILE
            ok = (jnp.abs(key - query) <= BAND) & (pos >= 0)
            ok = ok & ((pos < self.length) | (key == query))
            self.band[t] = jnp.where(ok, 0.0, -1e30).astype(BF16)
        zero_head = jnp.zeros((PAD, self.width), BF16)
        zero_tail = jnp.zeros((self.padded - PAD - self.seq, self.width), BF16)
        for l in range(self.layers):
            for ref in (self.k_pad, self.v_pad):
                ref[l, :PAD] = zero_head
                ref[l, PAD + self.seq :] = zero_tail

    def setup_vecs(self):
        eye = (row_index((self.width, self.width)) == col_index((self.width, self.width))).astype(
            BF16
        )
        for l in range(self.layers):
            self.cols[:, VROWS * l : VROWS * (l + 1)] = nt(eye, self.vecs[l].astype(BF16))

    def rows(self, body):
        @pl.loop(0, self.seq // ROWS)
        def _(i):
            body(pl.ds(pl.multiple_of(i * ROWS, ROWS), ROWS))

    def norm(self, l, which, source):
        def body(at):
            value = source[at, :]
            centered = value - jnp.mean(value, axis=-1, keepdims=True)
            rstd = lax.rsqrt(jnp.mean(centered * centered, axis=-1, keepdims=True) + EPSILON)
            xhat = centered * rstd
            n = 2 * l + which
            self.rstd[at, n : n + 1] = rstd
            self.xhat[l, which, at, :] = xhat.astype(BF16)
            normed = xhat * self.vec(l, GAIN + which) + self.vec(l, SHIFT + which)
            self.normed[at, :] = normed.astype(BF16)

        self.rows(body)
        self.normed_t[l, which] = self.normed[...].T

    def pad_keep(self):
        row = row_index((self.padded, 2 * HD)) - PAD
        return (row >= 0) & (row < self.length)

    def fwd_qkv(self, l, n):
        out = (nn(self.normed[...], self.w_qkv(l, n)) + self.vec(l, BQKV + n)).astype(BF16)
        if n == 0:
            self.q_t[l] = out.T
        else:
            (self.k_pad, self.v_pad)[n - 1][l, PAD : PAD + self.seq] = out
        if n == 2:
            self.tr_pad[...] = self.v_pad[l].T

    def pair_at(self, p):
        return pl.ds(pl.multiple_of(p * 2 * HD, 2 * HD), 2 * HD)

    def fwd_near(self, l, p):
        at = self.pair_at(p)
        spans = [
            (slice(t * TILE, (t + 1) * TILE), slice(t * TILE, t * TILE + WINDOW))
            for t in range(self.tiles)
        ]
        scores = [nn(self.k_pad[l, window, at], spread(self.q_t[l, at, here])) for here, window in spans]
        for t, (here, window) in enumerate(spans):
            one = scores[t] * (HD**-0.5) + self.band[t].astype(F32)
            weights = jnp.exp(one - jnp.max(one, axis=0, keepdims=True))
            inverse = 1.0 / jnp.sum(weights, axis=0, keepdims=True)
            probs = (weights * inverse).astype(BF16)
            self.probs[l, p, t] = probs
        for t, (here, window) in enumerate(spans):
            near = fold(nn(self.tr_pad[at, window], self.probs[l, p, t]))
            self.near_t[l, at, here] = near.astype(BF16)

    def features(self, x):
        grown = jnp.exp(jnp.minimum(x, 0.0))
        return jnp.where(x > 0, x + 1.0, grown), grown, jnp.tanh(x)

    def key_features(self, l, at):
        phi, slope, tanh = self.features(self.k_pad[l, :, at].astype(F32))
        ok = self.pad_keep()
        return (
            jnp.where(ok, phi, 0.0).astype(BF16),
            slope,
            jnp.where(ok, tanh, 0.0).astype(BF16),
            tanh,
        )

    def coefficient(self):
        wide = jnp.full((1, 1), HD, F32) * self.length.astype(F32)
        return lax.rsqrt(wide)

    def heads_row(self, two, seq):
        return jnp.concatenate(
            [
                jnp.broadcast_to(two[0:1], (HD, seq)),
                jnp.broadcast_to(two[1:2], (HD, seq)),
            ],
            axis=0,
        )

    def fwd_far(self, l, p):
        at = self.pair_at(p)
        phk, _, tk, _ = self.key_features(l, at)
        values_t = self.tr_pad[at, :]
        s_one = head_diag(nn(values_t, phk))
        s_two = head_diag(nn(values_t, tk))
        total = col_sum(phk.astype(F32))
        self.s_one[l, p], self.s_two[l, p] = s_one, s_two
        phi, _, tanh = self.features(self.q_t[l, at, :].astype(F32))
        phq, tq = phi.astype(BF16), tanh.astype(BF16)
        shape = (8, 2 * HD)
        mine = (row_index(shape) == 0) == (col_index(shape) < HD)
        z_high, z_low = split(jnp.where(mine & (row_index(shape) < 2), total, 0.0))
        den = nn(z_high, phq) + nn(z_low, phq)
        rden = 1.0 / jnp.where(row_index(den.shape) < 2, den, 1.0)
        self.rden[l, p] = rden
        total_col = jnp.broadcast_to(total, (8, 2 * HD)).T
        n = VROWS * l
        self.cols[at, n : n + 1] = total_col[:, 0:1]
        high, low = split(s_one)
        far_elu = (nn(high, phq) + nn(low, phq)) * self.heads_row(rden, self.seq)
        high, low = split(s_two)
        far_tanh = (nn(high, tq) + nn(low, tq)) * self.coefficient()
        self.tanh_t[l, at, :] = far_tanh.astype(BF16)
        blend = self.cols[at, VROWS * l : VROWS * (l + 1)]
        self.mixed_t[l, at, :] = (
            blend[:, BLEND : BLEND + 1] * self.near_t[l, at, :].astype(F32)
            + blend[:, BLEND + 1 : BLEND + 2] * far_elu
            + blend[:, BLEND + 2 : BLEND + 3] * far_tanh
        ).astype(BF16)

    def fwd_attn(self, l):
        mixed = self.mixed_t[l].T
        out = nn(mixed, self.w_attn(l)) + self.vec(l, OBIAS)
        self.gk_pad[: self.seq] = self.h[...] + self.keep(out)
        self.norm(l, 1, self.gk_pad)

    def fwd_up(self, l, j):
        pre = nn(self.normed[...], self.w_in(l, j)) + self.vec(l, BIN + j)
        square = pre * pre
        th = jnp.tanh(GELU_C * pre * (1.0 + GELU_A * square))
        half = 0.5 * (1.0 + th)
        slope = half + (0.5 * GELU_C) * pre * (1.0 - th * th) * (1.0 + 3.0 * GELU_A * square)
        self.dact[l, j] = slope.astype(BF16)
        self.act_t[l, j] = (pre * half).astype(BF16).T

    def fwd_down(self, l):
        self.acc[...] = jnp.broadcast_to(self.vec(l, OBIAS + 1), self.acc.shape)

        @pl.loop(0, self.ff_blocks)
        def _(j):
            self.acc[...] += nn(self.act_t[l, j].T, self.w_out(l, j))

    def fwd_end(self, l):
        self.h[...] = self.gk_pad[: self.seq] + self.keep(self.acc[...])

    def put_vec(self, l, row, value):
        self.vgrads[l, pl.ds(row, 1), :] = value

    def bwd_start(self, l, source):
        gz = self.keep(source[...].astype(F32)).astype(BF16)
        self.normed[...] = gz
        self.put_vec(l, OBIAS + 1, col_sum(gz.astype(F32)))

    def bwd_out(self, l, j):
        self.put_out(l, j, nn(self.act_t[l, j], self.normed[...]))

    def bwd_up(self, l, j):
        grad = nt(self.normed[...], self.w_out(l, j))
        gpre = (grad * self.dact[l, j].astype(F32)).astype(BF16)
        self.put_vec(l, BIN + j, col_sum(gpre.astype(F32)))
        first = pl.multiple_of(4 * GROUP + GROUP * j, GROUP)
        self.put_rows(l, first, nn(self.normed_t[l, 1], gpre))
        self.acc[...] += nt(gpre, self.w_in(l, j))

    def norm_back(self, l, which):
        self.put_vec(l, GAIN + which, jnp.zeros((1, self.width), F32))
        self.put_vec(l, SHIFT + which, jnp.zeros((1, self.width), F32))

        def body(at):
            grad = self.acc[at, :]
            xhat = self.xhat[l, which, at, :].astype(F32)
            self.vgrads[l, pl.ds(GAIN + which, 1), :] += col_sum(grad * xhat)
            self.vgrads[l, pl.ds(SHIFT + which, 1), :] += col_sum(grad)
            grad = grad * self.vec(l, GAIN + which)
            mean = jnp.mean(grad, axis=-1, keepdims=True)
            slope = jnp.mean(grad * xhat, axis=-1, keepdims=True)
            n = 2 * l + which
            self.h[at, :] += self.rstd[at, n : n + 1] * (grad - mean - xhat * slope)

        self.rows(body)

    def bwd_attn(self, l):
        self.norm_back(l, 1)
        go = self.keep(self.h[...]).astype(BF16)
        self.put_vec(l, OBIAS, col_sum(go.astype(F32)))
        self.put_rows(l, 3 * GROUP, nn(self.mixed_t[l], go))
        self.gm_t[...] = nt(self.w_attn(l), go).astype(BF16)
        self.tr_pad[...] = self.k_pad[l].T
        self.gk_pad[...] = jnp.zeros_like(self.gk_pad)
        self.gv_pad[...] = jnp.zeros_like(self.gv_pad)

    def bwd_near(self, l, p):
        at = self.pair_at(p)
        blend = self.cols[at, VROWS * l : VROWS * (l + 1)]
        spans = [
            (slice(t * TILE, (t + 1) * TILE), slice(t * TILE, t * TILE + WINDOW))
            for t in range(self.tiles)
        ]
        grads = []
        for here, _ in spans:
            grad = blend[:, BLEND : BLEND + 1] * self.gm_t[at, here].astype(F32)
            grads.append(spread(grad.astype(BF16)))
        dprobs = [nn(self.v_pad[l, window, at], g) for g, (_, window) in zip(grads, spans)]
        terms = []
        for t in range(self.tiles):
            wide = self.probs[l, p, t].astype(F32)
            term = wide * dprobs[t]
            inner = jnp.sum(term, axis=0, keepdims=True)
            terms.append(((term - wide * inner) * (HD**-0.5)).astype(BF16))
        for gs, (here, window) in zip(terms, spans):
            self.acc_t[at, here] = fold(nn(self.tr_pad[at, window], gs))
        keys = [nt(gs, spread(self.q_t[l, at, here])) for gs, (here, _) in zip(terms, spans)]
        values = [nt(self.probs[l, p, t], grads[t]) for t in range(self.tiles)]
        for t, (_, window) in enumerate(spans):
            self.gk_pad[window, at] += keys[t]
            self.gv_pad[window, at] += values[t]

    def bwd_far(self, l, p):
        at = self.pair_at(p)
        seq = self.seq
        blend = self.cols[at, VROWS * l : VROWS * (l + 1)]
        gm = self.gm_t[at, :].astype(F32)
        q = self.q_t[l, at, :].astype(F32)
        phi_q, slope_q, tanh_q = self.features(q)
        phq, tq = phi_q.astype(BF16), tanh_q.astype(BF16)
        high, low = split(self.s_one[l, p])
        far_elu = (nn(high, phq) + nn(low, phq)) * self.heads_row(self.rden[l, p], seq)
        column = lambda a: jnp.sum(a, axis=1, keepdims=True)
        sums = [
            column(gm * self.near_t[l, at, :].astype(F32)),
            column(gm * far_elu),
            column(gm * self.tanh_t[l, at, :].astype(F32)),
        ]
        for n, one in enumerate(sums):
            self.cols[at, GBLEND + n : GBLEND + n + 1] = one
        phk, slope_k, tk, tanh_k = self.key_features(l, at)
        values = self.v_pad[l, :, at]
        gnum = (blend[:, BLEND + 1 : BLEND + 2] * gm * self.heads_row(self.rden[l, p], seq)).astype(
            BF16
        )
        prod = gnum.astype(F32) * far_elu
        gden_one = -col_sum(prod[:HD])
        gden_two = -col_sum(prod[HD:])
        gden = jnp.concatenate([gden_one, gden_two, jnp.zeros((6, seq), F32)], axis=0)
        s_one = self.s_one[l, p].T
        high, low = split(s_one)
        gphq = nn(high, gnum) + nn(low, gnum) + self.cols[at, VROWS * l : VROWS * l + 1] * self.heads_row(gden, seq)
        gs_one = head_diag(nt(phq, gnum))
        gs_high, gs_low = split(gs_one)
        gden_high, gden_low = split(gden)
        both = nt(gden_high, phq) + nt(gden_low, phq)
        gzz = jnp.where(col_index((1, 2 * HD)) < HD, both[0:1], both[1:2])
        gtanh = (blend[:, BLEND + 2 : BLEND + 3] * gm * self.coefficient()).astype(BF16)
        gtq = nn(self.s_two[l, p].T.astype(BF16), gtanh)
        gs_two = head_diag(nt(tq, gtanh)).astype(BF16)
        self.acc_t[at, :] += gphq * jnp.where(q > 0, 1.0, slope_q) + gtq * (1.0 - tanh_q * tanh_q)
        gphk = nt(values, gs_high) + nt(values, gs_low) + gzz
        gtk = nt(values, gs_two)
        grad_k = gphk * slope_k + gtk * (1.0 - tanh_k * tanh_k)
        self.gk_pad[:, at] += jnp.where(self.pad_keep(), grad_k, 0.0)
        self.gv_pad[:, at] += nn(phk, gs_high) + nn(tk, gs_two)

    def bwd_qkv(self, l, n):
        rows = slice(PAD, PAD + self.seq)
        if n == 0:
            grad = self.acc_t[...].T.astype(BF16)
        else:
            grad = (self.gk_pad, self.gv_pad)[n - 1][rows, :].astype(BF16)
        self.put_vec(l, BQKV + n, col_sum(grad.astype(F32)))
        self.put_rows(l, GROUP * n, nn(self.normed_t[l, 0], grad))
        total = self.gv_pad.at[rows]
        part = nt(grad, self.w_qkv(l, n))
        if n == 2:
            total[...] = part
        elif n == 1:
            total[...] += part
        else:
            self.acc[...] = total[...] + part

    def bwd_end(self, l):
        self.vgrads[l, pl.ds(BLEND, 3), :] = self.cols[...].T[GBLEND : GBLEND + 3]
        self.norm_back(l, 0)


class Comm:
    def __init__(self, depth, sems):
        self.sems = sems
        self.free = ([], [])
        self.made = [0, 0]
        self.clock = 0
        self.heard = {}
        dp, fsdp = lax.axis_index("dp"), lax.axis_index("fsdp")
        self.depth = depth
        self.at = {"z": dp // 2, "x": dp % 2, "y": fsdp // 2, "c": fsdp % 2}

    def device(self, **moved):
        at = dict(self.at, **moved)
        return (at["z"] * 2 + at["x"], at["y"] * 2 + at["c"])

    def steps(self, axis):
        return range(1, self.depth) if axis == "z" else range(1, 2)

    def other(self, axis, step=1):
        if axis == "z":
            return lax.rem(self.at["z"] + step, self.depth)
        return 1 - self.at[axis]

    def barrier(self):
        semaphore = pltpu.get_barrier_semaphore()
        peers = [
            self.device(**{axis: self.other(axis, k)}) for axis in "zxyc" for k in self.steps(axis)
        ]
        for peer in peers:
            pl.semaphore_signal(semaphore, inc=1, device_id=peer, device_id_type=MESH)
        pl.semaphore_wait(semaphore, len(peers))

    def take(self, side, before):
        for entry in self.free[side]:
            if entry[0] < before:
                self.free[side].remove(entry)
                return entry[1]
        self.made[side] += 1
        return self.made[side] - 1

    def copy(self, source, target, axis, step):
        self.clock += 1
        sent = self.take(0, self.clock)
        arrived = self.take(1, self.heard.get((axis, step), -1))
        made = pltpu.make_async_remote_copy(
            src_ref=source,
            dst_ref=target,
            send_sem=self.sems[0].at[sent],
            recv_sem=self.sems[1].at[arrived],
            device_id=self.device(**{axis: self.other(axis, step)}),
            device_id_type=MESH,
        )
        made.start()
        back = (axis, self.depth - step if axis == "z" else 1)
        return made, sent, arrived, back, self.clock

    def wait(self, copies):
        for made, sent, arrived, back, when in copies:
            made.wait()
            self.clock += 1
            self.free[0].append((self.clock, sent))
            self.free[1].append((self.clock, arrived))
            self.heard[back] = max(when, self.heard.get(back, -1))

    def index(self, whole, moved=None):
        at = dict(self.at, **(moved or {}))
        return tuple(slice(None) if axis in whole else at[axis] for axis in "zxyc")

    def gather(self, view, order):
        cores = []
        for stage in range(4):
            whole, started = order[:stage], []
            if stage < 3:
                axis = order[stage]
                block = view(self.index(whole))
                started = [self.copy(block, block, axis, k) for k in self.steps(axis)]
            if "z" in whole:
                axis = order[stage - 1]
                if axis == "z":
                    block = view(self.index(whole))
                else:
                    block = view(self.index(order[: stage - 1], {axis: self.other(axis)}))
                cores.append(self.copy(block, block, "c", 1))
            yield
            self.wait(started)
        self.wait(cores)

    @staticmethod
    def add(mine, others):
        @pl.loop(0, mine.shape[0])
        def _(n):
            for rest in itertools.product(*[range(m) for m in mine.shape[1:-2]]):
                at = (n,) + rest
                total = mine[at]
                for other in others:
                    total = total + other[at]
                mine[at] = total

    def scatter(self, view, slot, order, put):
        axes = "c" + order
        for stage, axis in enumerate(axes):
            whole = axes[stage + 1 :]
            started = []
            for k in self.steps(axis):
                block = view(self.index(whole, {axis: self.other(axis, k)}))
                started.append(self.copy(block, slot(stage, k - 1), axis, k))
            yield
            self.wait(started)
            mine = view(self.index(whole))
            arrived = [slot(stage, k - 1) for k in self.steps(axis)]
            if whole:
                self.add(mine, arrived)
            else:
                total = mine[...].astype(F32)
                for one in arrived:
                    total = total + one[...].astype(F32)
                put(total)


ORDERS = {
    ("gather", 0): (
        "xzy", "zyx", "zxy", "zyx", "yzx", "zxy",
        "zyx", "zxy", "zyx", "zxy", "zyx", "zxy",
    ),
    ("gather", 1): (
        "zyx", "xzy", "yzx", "yzx", "zyx", "xzy",
        "yzx", "zxy", "zyx", "zyx", "xzy", "xzy",
    ),
    ("scatter", 0): (
        "xyz", "xyz", "yzx", "xyz", "xyz", "yxz",
        "xyz", "yxz", "xzy", "yzx", "yzx", "xyz",
    ),
    ("scatter", 1): (
        "yxz", "xzy", "yzx", "yxz", "xzy", "yzx",
        "xyz", "xyz", "xyz", "xyz", "yzx", "yzx",
    ),
}
LINK, HOP = 0.0235, 1.8
CORE, CORE_HOP = 0.0027, 0.9
ISSUE, BACKLOG, AHEAD = 0.04, 6.0, 12


def plan(layers, segments, parts):
    size = {"z": 4, "x": 2, "y": 2, "c": 2}
    free = dict.fromkeys("zxyc", 0.0)
    clock, steps = 0.0, []
    stage = dict.fromkeys(parts, 0)
    ready = {n: 0.0 if not scatter else None for n, (_, _, scatter) in parts.items()}
    done = set()
    waiting = list(segments)

    def send(axis, blocks, rows):
        link, hop = (CORE, CORE_HOP) if axis == "c" else (LINK, HOP)
        load = blocks * rows * link * (size["z"] if axis == "z" else 1)
        free[axis] = max(free[axis], clock) + load
        return free[axis] + hop

    def count(axes):
        total = 1
        for axis in axes:
            total *= size[axis]
        return total

    def step(name):
        nonlocal clock
        rows, order, scatter = parts[name]
        now = stage[name]
        steps.append((name,))
        stage[name] += 1
        last = 4
        if scatter:
            axes = "c" + order
            if now > 0:
                clock += 0.02 + count(axes[now:]) * rows * 0.0002
            if now < last:
                arrives = send(axes[now], count(axes[now + 1 :]), rows)
                clock += ISSUE * (3 if axes[now] == "z" else 1)
        else:
            arrives = ready[name]
            if now < 3:
                arrives = send(order[now], count(order[:now]), rows)
                clock += ISSUE * (3 if order[now] == "z" else 1)
            if "z" in order[:now] and now < last:
                whole = order[:now] if order[now - 1] == "z" else order[: now - 1]
                core = send("c", count(whole), rows)
                clock += ISSUE
                if now == 3:
                    arrives = core
        if now == last:
            done.add(name)
            ready[name] = None
        else:
            ready[name] = arrives

    def startable(name):
        _, order, scatter = parts[name]
        first = "c" if scatter else order[0]
        return stage[name] > 0 or free[first] <= clock + BACKLOG

    while len(done) < len(parts) or waiting:
        left = [n for n in parts if n not in done][:AHEAD]
        able = [n for n in left if ready[n] is not None and ready[n] <= clock and startable(n)]
        if able:
            step(able[0])
            continue
        if waiting:
            name, layer, argument, cost, needs, makes = waiting[0]
            if all(n in done for n in needs):
                waiting.pop(0)
                steps.append((name, layer, argument))
                clock += cost
                for n in makes:
                    ready[n] = clock
                continue
        later = [ready[n] for n in left if ready[n] is not None and ready[n] > clock]
        later += [free[a] - BACKLOG for a in "zxyc" if free[a] - BACKLOG > clock]
        clock = min(later)
    return steps, clock


def make_plan(layers, pairs, ff, rows):
    units = rows // GROUP
    parts = {("gather", 0, "vectors"): (4, "zxy", False)}
    for l in range(layers):
        for u in range(units):
            parts["gather", l, u] = (GROUP, ORDERS["gather", l][u], False)
    late = list(range(units - ff, units)) + list(range(4, units - ff)) + [3, 2, 1, 0]
    for l in reversed(range(layers)):
        for u in late:
            parts["scatter", l, u] = (GROUP, ORDERS["scatter", l][u], True)
    parts["scatter", 0, "vectors"] = (8, "yxz", True)
    gathers = lambda l, us: [("gather", l, u) for u in us]
    scatters = lambda l, us: [("scatter", l, u) for u in us]
    downs = range(units - ff, units)
    segments = []
    add = lambda *s: segments.append(s)
    halves = [(0, pairs)]
    twos = [(j, min(j + STEP, ff)) for j in range(0, ff, STEP)]
    add("start", 0, None, 0.5, [], [])
    add("spread", 0, None, 0.5, [("gather", 0, "vectors")], [])
    for l in range(layers):
        add("norm", l, 0, 0.7, [], [])
        for n in range(3):
            add("fwd_qkv", l, n, 0.25, gathers(l, [n]), [])
        for half in halves:
            add("fwd_near", l, half, 2.6, [], [])
        for half in halves:
            add("fwd_far", l, half, 2.3, [], [])
        add("fwd_attn", l, None, 1.3, gathers(l, [3]), [])
        for j, end in twos:
            add("fwd_up", l, (j, end), 1.05 * (end - j), gathers(l, range(4 + j, 4 + end)), [])
        if l == layers - 1:
            add("bwd_start", l, None, 0.3, [], [])
            add("bwd_out", l, (0, ff), 0.43 * ff, [], scatters(l, downs))
        add("fwd_down", l, None, 1.9, gathers(l, downs), [])
    for l in reversed(range(layers)):
        again = lambda us: scatters(l + 1, us) if l < layers - 1 else []
        if l < layers - 1:
            add("bwd_start", l, None, 0.3, [], [])
            add("bwd_out", l, (0, ff), 0.43 * ff, again(downs), scatters(l, downs))
        for j, end in twos:
            units = range(4 + j, 4 + end)
            add("bwd_up", l, (j, end), 1.33 * (end - j), again(units), scatters(l, units))
        add("bwd_attn", l, None, 1.6, again([3]), scatters(l, [3]))
        for half in halves:
            add("bwd_near", l, half, 3.1, [], [])
        for half in halves:
            add("bwd_far", l, half, 3.8, [], [])
        for n in (2, 1, 0):
            add("bwd_qkv", l, n, 0.6, again([n]), scatters(l, [n]))
        add("bwd_end", l, None, 0.9, [], [])
    add("collect", 0, None, 0.5, [], scatters(0, ["vectors"]))
    return plan(layers, segments, parts), parts


class Vectors:
    def __init__(self, layers, width, hidden):
        self.layers, self.width = layers, width
        self.devices = width // GROUP
        self.long = [(BQKV, 3), (BIN, hidden // width)]

    def swap(self, tiles, back):
        lane = lax.broadcasted_iota(jnp.int32, tiles.shape, 2)
        result = tiles
        for l in range(self.layers):
            for row, count in self.long:
                first = l * VROWS + row
                columns = [tiles[:, :, first + n : first + n + 1] for n in range(count)]
                if back:
                    both = jnp.stack(columns, axis=1).reshape(count, self.devices, GROUP, 1)
                    columns = [both[n] for n in range(count)]
                else:
                    both = jnp.concatenate(columns, axis=0)
                    both = both.reshape(self.devices, count, GROUP, 1)
                    columns = [both[:, n] for n in range(count)]
                for n in range(count):
                    result = jnp.where(lane == first + n, columns[n], result)
        return result

    def spread(self, shares, vecs, cols):
        tiles = shares[...].reshape(self.devices, GROUP, 128).astype(F32)
        columns = self.swap(tiles, True).reshape(self.width, 128)
        cols[...] = columns
        vecs[...] = columns.T[: self.layers * VROWS].reshape(vecs.shape)

    def collect(self, vgrads, shares):
        rows = vgrads[...].reshape(self.layers * VROWS, self.width)
        rest = jnp.zeros((128 - self.layers * VROWS, self.width), F32)
        columns = jnp.concatenate([rows, rest], axis=0).T
        tiles = self.swap(columns.reshape(self.devices, GROUP, 128), False)
        shares[...] = tiles.reshape(shares.shape)

    def pack(self, refs, table):
        table[...] = jnp.zeros_like(table)
        for l in range(self.layers):
            for ref, row in zip(refs, VECTOR_ROWS):
                row += l * VROWS
                if len(ref.shape) == 3:
                    table[row : row + ref.shape[1], :GROUP] = ref[l].astype(F32)
                else:
                    value = ref[l : l + 1, :].astype(F32)
                    for n in range(ref.shape[1] // GROUP):
                        piece = value[:, n * GROUP : (n + 1) * GROUP]
                        table[row + n : row + n + 1, :GROUP] = piece
        return table[...].T[:GROUP]

    def unpack(self, tile, table, refs):
        rest = jnp.zeros((128 - GROUP, 128), F32)
        table[...] = jnp.concatenate([tile, rest], axis=0).T
        for l in range(self.layers):
            for ref, row in zip(refs, VECTOR_ROWS):
                row += l * VROWS
                if len(ref.shape) == 3:
                    ref[l] = table[row : row + ref.shape[1], :GROUP]
                else:
                    count = ref.shape[1] // GROUP
                    rows = [table[row + n : row + n + 1, :GROUP] for n in range(count)]
                    ref[l : l + 1, :] = jnp.concatenate(rows, axis=1)


class Program:
    def __init__(self, net, comm, vectors, r):
        self.net, self.comm, self.vectors = net, comm, vectors
        self.__dict__.update(r)

    def fill(self):
        own = self.comm.index(())
        width = self.net.width
        for l in range(self.net.layers):
            first = 0
            for ref in (self.w_qkv, self.w_attn, self.w_in):
                for n in range(ref.shape[2] // width):
                    rows = pl.ds(first, GROUP)
                    self.net.packed[(l,) + own + (rows,)] = ref[l, :, n * width : (n + 1) * width]
                    first += GROUP
            rows = pl.ds(first, self.w_out.shape[1])
            self.net.packed[(l,) + own + (rows,)] = self.w_out[l]
        refs = [getattr(self, name) for name in VECTORS]
        self.shares[own] = self.vectors.pack(refs, self.table).astype(BF16)

    def gather(self, l, unit, order):
        if unit == "vectors":
            return self.comm.gather(lambda index: self.shares.at[index], order)
        at = pl.ds(unit * GROUP, GROUP)
        return self.comm.gather(lambda index: self.net.packed.at[(l,) + index + (at,)], order)

    def scatter(self, l, unit, order):
        if unit == "vectors":
            arrivals, at, source = self.varrivals, (), self.vshares
        else:
            at = (pl.ds(unit * GROUP, GROUP),)
            arrivals, source = self.arrivals, self.net.grads
        depth = self.comm.depth
        every = slice(None)

        def slot(stage, k):
            if stage < 2:
                return arrivals[stage].at[(every,) * (3 - stage) + at]
            if stage == 2:
                span = slice(2 * k, 2 * k + 2) if order[1] == "z" else slice(0, depth)
                return arrivals[2].at[(span,) + at]
            return arrivals[2].at[(2 * (depth - 1) if order[1] == "z" else depth + k,) + at]

        put = functools.partial(self.put, l, unit)
        return self.comm.scatter(lambda index: source.at[index + at], slot, order, put)

    def put(self, l, unit, total):
        if unit == "vectors":
            self.gsmall[...] = total
            return
        width = self.net.width
        for ref in (self.gw_qkv, self.gw_attn, self.gw_in):
            count = ref.shape[2] // width
            if unit < count:
                ref[l, :, unit * width : (unit + 1) * width] = total
                return
            unit -= count
        self.gw_out[l, unit * GROUP : (unit + 1) * GROUP, :] = total

    def start(self, l, _):
        self.net.setup()
        self.net.h[...] = self.tokens[...].astype(F32)

    def spread(self, l, _):
        self.vectors.spread(self.shares, self.net.vecs, self.net.cols)

    def collect(self, l, _):
        self.vectors.collect(self.net.vgrads, self.vshares)

    def norm(self, l, _):
        self.net.norm(l, 0, self.net.h)

    def fwd_attn(self, l, _):
        self.net.fwd_attn(l)

    def fwd_down(self, l, _):
        self.net.fwd_down(l)
        self.net.fwd_end(l)
        if l == self.net.layers - 1:
            self.mixed_out[...] = self.net.h[...].astype(BF16)
            self.net.h[...] = self.cotangent[...].astype(F32)

    def bwd_up(self, l, span):
        if span[0] == 0:
            self.net.acc[...] = jnp.zeros_like(self.net.acc)
        self.over(self.net.bwd_up, l, span)

    def bwd_start(self, l, _):
        self.net.bwd_start(l, self.cotangent if l == self.net.layers - 1 else self.net.h)

    def bwd_attn(self, l, _):
        self.net.bwd_attn(l)

    def bwd_end(self, l, _):
        self.net.bwd_end(l)

    def over(self, body, l, span):
        @pl.loop(*span)
        def _(p):
            body(l, p)

    def run(self):
        net = self.net
        rows = net.packed.shape[-2]
        (steps, _), parts = make_plan(net.layers, net.pairs, net.ff_blocks, rows)
        running = {}
        for (kind, l, unit), (_, order, _) in parts.items():
            make = self.gather if kind == "gather" else self.scatter
            running[kind, l, unit] = make(l, unit, order)
        self.fill()
        self.comm.barrier()
        for name, *rest in steps:
            if not rest:
                next(running[name], None)
            elif hasattr(self, name):
                getattr(self, name)(*rest)
            elif isinstance(rest[1], tuple):
                self.over(getattr(net, name), *rest)
            else:
                getattr(net, name)(*rest)
        assert max(self.comm.made) <= SEMAPHORES


VECTORS = ("gains", "shifts", "b_qkv", "blends", "b_in", "biases")
WEIGHTS = ("w_qkv", "w_attn", "w_in", "w_out")
INPUTS = ("tokens", "cotangent") + VECTORS + WEIGHTS
OUTPUTS = ("mixed_out", "h", "gsmall", "gw_qkv", "gw_attn", "gw_in", "gw_out")
SEMAPHORES = 96


def fused_body(sizes, depth, names, length_ref, *refs):
    named = dict(zip(INPUTS + OUTPUTS + names, refs))
    arrivals = [named.pop("arrive%d" % n) for n in range(3)]
    varrivals = [named.pop("varrive%d" % n) for n in range(3)]
    sems = named.pop("send"), named.pop("recv")
    inner = {n: r for n, r in named.items() if n not in INPUTS}
    net = Net(*sizes, length_ref[0], inner)
    comm = Comm(depth, sems)
    vectors = Vectors(sizes[0], sizes[2], sizes[3])
    Program(net, comm, vectors, dict(named, arrivals=arrivals, varrivals=varrivals)).run()


def fused(lengths, tokens, cotangent, vectors, weights):
    layers, _, width = weights[1].shape
    hidden = weights[2].shape[2]
    seq = tokens.shape[0]
    sizes = (layers, seq, width, hidden)
    rows = sum(w.shape[1] * w.shape[2] for w in weights) // width
    groups = group_shape(width, hidden)
    tile = (GROUP, 128)
    vmem = pl.BlockSpec(memory_space=pltpu.VMEM)
    scratch = dict(Net.scratch(*sizes))
    scratch["packed"] = pltpu.VMEM((layers,) + groups + (rows, width), BF16)
    scratch["grads"] = pltpu.VMEM(groups + (rows, width), BF16)
    scratch["shares"] = pltpu.VMEM(groups + tile, BF16)
    scratch["vshares"] = pltpu.VMEM(groups + tile, F32)
    scratch["table"] = pltpu.VMEM((128, 128), F32)
    kept = (groups[:3], groups[:2], (2 * groups[0] - 1,))
    for n, lead in enumerate(kept):
        scratch["arrive%d" % n] = pltpu.VMEM(lead + (rows, width), BF16)
        scratch["varrive%d" % n] = pltpu.VMEM(lead + tile, F32)
    scratch["send"] = pltpu.SemaphoreType.DMA((SEMAPHORES,))
    scratch["recv"] = pltpu.SemaphoreType.DMA((SEMAPHORES,))
    return pl.pallas_call(
        functools.partial(fused_body, sizes, groups[0], tuple(scratch)),
        out_shape=(
            jax.ShapeDtypeStruct(tokens.shape, BF16),
            jax.ShapeDtypeStruct(tokens.shape, F32),
            jax.ShapeDtypeStruct(tile, F32),
        )
        + tuple(jax.ShapeDtypeStruct(w.shape, F32) for w in weights),
        in_specs=[pl.BlockSpec(memory_space=pltpu.SMEM)] + [vmem] * len(INPUTS),
        out_specs=(vmem,) * len(OUTPUTS),
        scratch_shapes=list(scratch.values()),
        compiler_params=pltpu.CompilerParams(
            collective_id=0, has_side_effects=True, vmem_limit_bytes=63 * 2**20
        ),
    )(lengths, tokens, cotangent, *vectors, *weights)


def finish_body(vectors, big, *refs):
    sources, tile, refs = refs[:big], refs[big], refs[big + 1 :]
    targets, outs, table, sems = refs[:big], refs[big : -big - 2], refs[-big - 2], refs[-big - 1]
    buffers = refs[-big:]
    loads = [
        pltpu.make_async_copy(source, buffer, sems.at[0, n])
        for n, (source, buffer) in enumerate(zip(sources, buffers))
    ]
    stores = [
        pltpu.make_async_copy(buffer, target, sems.at[1, n])
        for n, (buffer, target) in enumerate(zip(buffers, targets))
    ]
    for one in loads:
        one.start()
    vectors.unpack(tile[...], table, outs)
    for load, store in zip(loads, stores):
        load.wait()
        store.start()
    for one in stores:
        one.wait()


def finish(vectors, large, tile, shapes):
    anywhere, vmem = pl.BlockSpec(memory_space=pl.ANY), pl.BlockSpec(memory_space=pltpu.VMEM)
    outs = pl.pallas_call(
        functools.partial(finish_body, vectors, len(large)),
        out_shape=tuple(jax.ShapeDtypeStruct(a.shape, a.dtype) for a in large)
        + tuple(jax.ShapeDtypeStruct(shape, F32) for shape in shapes),
        in_specs=[anywhere] * len(large) + [vmem],
        out_specs=(anywhere,) * len(large) + (vmem,) * len(shapes),
        scratch_shapes=[
            pltpu.VMEM((128, 128), F32),
            pltpu.SemaphoreType.DMA((2, len(large))),
        ]
        + [pltpu.VMEM(a.shape, a.dtype) for a in large],
        compiler_params=pltpu.CompilerParams(vmem_limit_bytes=62 * 2**20),
    )(*large, tile)
    return outs[: len(large)], outs[len(large) :]


def plain_body(sizes, names, length_ref, *refs):
    names = ("tokens", "cotangent", "packed", "vecs", "mixed_out", "h", "grads_out", "vgrads") + names
    named = dict(zip(names, refs))
    net = Net(*sizes, length_ref[0], named)

    def over(body, l):
        @pl.loop(0, net.pairs)
        def _(p):
            body(l, p)

    net.setup()
    net.setup_vecs()
    net.h[...] = named["tokens"][...].astype(F32)
    for l in range(net.layers):
        net.norm(l, 0, net.h)
        for n in range(3):
            net.fwd_qkv(l, n)
        over(net.fwd_near, l)
        over(net.fwd_far, l)
        net.fwd_attn(l)
        for j in range(net.ff_blocks):
            net.fwd_up(l, j)
        net.fwd_down(l)
        net.fwd_end(l)
    named["mixed_out"][...] = net.h[...].astype(BF16)
    net.h[...] = named["cotangent"][...].astype(F32)
    for l in reversed(range(net.layers)):
        net.bwd_start(l, net.h)
        net.acc[...] = jnp.zeros_like(net.acc)
        for j in range(net.ff_blocks):
            net.bwd_out(l, j)
            net.bwd_up(l, j)
        net.bwd_attn(l)
        over(net.bwd_near, l)
        over(net.bwd_far, l)
        for n in (2, 1, 0):
            net.bwd_qkv(l, n)
        net.bwd_end(l)
        copy = pltpu.make_async_copy(named["grads"], named["grads_out"].at[l], named["sem"])
        copy.start()
        copy.wait()


def plain(lengths, tokens, cotangent, packed, vecs):
    layers, rows, width = packed.shape[0], packed.shape[-2], packed.shape[-1]
    seq = tokens.shape[0]
    hidden = (rows // GROUP - 4) // 2 * width
    sizes = (layers, seq, width, hidden)
    scratch = dict(Net.scratch(*sizes))
    del scratch["vecs"], scratch["vgrads"]
    scratch["grads"] = pltpu.VMEM(packed.shape[1:], BF16)
    scratch["sem"] = pltpu.SemaphoreType.DMA
    vmem = pl.BlockSpec(memory_space=pltpu.VMEM)
    return pl.pallas_call(
        functools.partial(plain_body, sizes, tuple(scratch)),
        out_shape=(
            jax.ShapeDtypeStruct((seq, width), BF16),
            jax.ShapeDtypeStruct((seq, width), F32),
            jax.ShapeDtypeStruct(packed.shape, BF16),
            jax.ShapeDtypeStruct((layers, VROWS, width), F32),
        ),
        in_specs=[pl.BlockSpec(memory_space=pltpu.SMEM)] + [vmem] * 4,
        out_specs=(vmem, vmem, pl.BlockSpec(memory_space=pl.ANY), vmem),
        scratch_shapes=list(scratch.values()),
        compiler_params=pltpu.CompilerParams(vmem_limit_bytes=63 * 2**20),
    )(lengths, tokens, cotangent, packed, vecs)


BOTH = ("dp", "fsdp")


def general(lengths, tokens, cotangent, vectors, weights):
    whole = lambda v, axis: lax.all_gather(v, BOTH, axis=axis, tiled=True)
    w_all = [whole(w, 1) for w in weights]
    v_all = [whole(v, v.ndim - 1) for v in vectors]
    layers, width, _ = w_all[1].shape
    groups = group_shape(width, w_all[2].shape[2])
    blocks = []
    for w in w_all[:3]:
        cut = w.reshape((layers,) + groups + (GROUP, -1, width))
        blocks.append(jnp.moveaxis(cut, -2, -3).reshape((layers,) + groups + (-1, width)))
    blocks.append(w_all[3].reshape((layers,) + groups + (-1, width)))
    vecs = jnp.concatenate([v.reshape(layers, -1, width) for v in v_all], axis=1).astype(F32)
    mixed, grad_tokens, grads, vgrads = plain(
        lengths, tokens, cotangent, jnp.concatenate(blocks, axis=-2), vecs
    )
    reduce = lambda g, axis: lax.psum_scatter(g, BOTH, scatter_dimension=axis, tiled=True)
    w_grads, first = [], 0
    for n, (w, block) in enumerate(zip(w_all, blocks)):
        part = grads[..., first : first + block.shape[-2], :].astype(F32)
        first += block.shape[-2]
        if n < 3:
            part = part.reshape((layers,) + groups + (-1, GROUP, width))
            part = jnp.moveaxis(part, -3, -2)
        w_grads.append(reduce(part.reshape(w.shape), 1))
    v_grads, first = [], 0
    for v in v_all:
        count = v.size // (layers * width)
        part = vgrads[:, first : first + count].reshape(v.shape)
        first += count
        v_grads.append(reduce(part, v.ndim - 1))
    return mixed, grad_tokens, v_grads, w_grads


def on_device(mesh, tokens, lengths, *rest):
    gains, shifts, w_qkv, b_qkv, w_attn, blends, w_in, b_in, w_out, biases, cotangent = rest
    vectors = (gains, shifts, b_qkv, blends, b_in, biases)
    weights = (w_qkv, w_attn, w_in, w_out)
    layers, _, width = w_attn.shape
    groups = group_shape(width, w_in.shape[2])
    if (mesh.shape["dp"], mesh.shape["fsdp"]) == (groups[0] * groups[1], groups[2] * groups[3]):
        mixed, grad_tokens, tile, *w_grads = fused(
            lengths, tokens, cotangent, vectors, weights
        )
        large, v_grads = finish(
            Vectors(layers, width, w_in.shape[2]),
            (mixed, grad_tokens, *w_grads),
            tile,
            [v.shape for v in vectors],
        )
        mixed, grad_tokens, *w_grads = large
    else:
        mixed, grad_tokens, v_grads, w_grads = general(
            lengths, tokens, cotangent, vectors, weights
        )
    d_gains, d_shifts, d_b_qkv, d_blends, d_b_in, d_biases = v_grads
    d_w_qkv, d_w_attn, d_w_in, d_w_out = w_grads
    return (
        mixed,
        grad_tokens,
        d_gains,
        d_shifts,
        d_w_qkv,
        d_b_qkv,
        d_w_attn,
        d_blends,
        d_w_in,
        d_b_in,
        d_w_out,
        d_biases,
    )


def solution(mesh):
    rows, vector = P(BOTH, None), P(None, None, BOTH)
    weight, bias = P(None, BOTH, None), P(None, BOTH)
    in_specs = (
        rows,
        P(BOTH),
        vector,
        vector,
        weight,
        bias,
        weight,
        vector,
        weight,
        bias,
        weight,
        vector,
        rows,
    )
    out_specs = (
        rows,
        rows,
        vector,
        vector,
        weight,
        bias,
        weight,
        vector,
        weight,
        bias,
        weight,
        vector,
    )
    return jax.shard_map(
        functools.partial(on_device, mesh),
        mesh=mesh,
        in_specs=in_specs,
        out_specs=out_specs,
        check_vma=False,
    )
```

```python
import functools
import itertools
import jax
import jax.numpy as jnp
from jax import lax
from jax.experimental import pallas as pl
from jax.experimental.pallas import tpu as pltpu
from jax.sharding import PartitionSpec as P

HD = 64
BAND = 30
EPSILON = 1e-05
MESH = pl.DeviceIdType.MESH
F32 = jnp.float32
BF16 = jnp.bfloat16
GROUP = 16
TILE = 128
PAD = 32
WINDOW = TILE + 2 * PAD
TWINS = {"acc_t": "acc", "gm_t": "normed"}
STEP = 2
ROWS = 512
GELU_C = 0.7978845608028654
GELU_A = 0.044715
GAIN, SHIFT, BQKV, BLEND, BIN, OBIAS, VROWS = 0, 2, 4, 7, 10, 14, 16
VECTOR_ROWS = (GAIN, SHIFT, BQKV, BLEND, BIN, OBIAS)


def nn(a, b):
    return jnp.dot(a, b, preferred_element_type=F32)


def nt(a, b):
    return lax.dot_general(a, b, (((1,), (1,)), ((), ())), preferred_element_type=F32)


def split(a):
    high = a.astype(BF16)
    return high, (a - high.astype(F32)).astype(BF16)


def row_index(shape):
    return lax.broadcasted_iota(jnp.int32, shape, 0)


def col_index(shape):
    return lax.broadcasted_iota(jnp.int32, shape, 1)


def head_diag(a):
    return jnp.where((row_index(a.shape) < HD) == (col_index(a.shape) < HD), a, 0.0)


def spread(tile):
    top, bottom = tile[:HD], tile[HD:]
    zero = jnp.zeros_like(top)
    return jnp.concatenate(
        [jnp.concatenate([top, zero], axis=1), jnp.concatenate([zero, bottom], axis=1)], axis=0
    )


def fold(wide):
    half = wide.shape[1] // 2
    return jnp.concatenate([wide[:HD, :half], wide[HD:, half:]], axis=0)


def col_sum(a):
    return jnp.sum(a, axis=0, keepdims=True)


GBLEND = 64


def group_shape(width, hidden):
    first = hidden // width
    return (first, width // GROUP // first // 4, 2, 2)


class Net:
    def __init__(self, layers, seq, width, hidden, length, r):
        self.layers, self.seq, self.width, self.hidden = layers, seq, width, hidden
        self.pairs = width // (2 * HD)
        self.tiles = seq // TILE
        self.length = length
        self.padded = seq + TILE
        self.ff_blocks = hidden // width
        self.groups = group_shape(width, hidden)
        self.__dict__.update(r)
        for name, twin in TWINS.items():
            if name not in r:
                setattr(self, name, r[twin])

    @staticmethod
    def scratch(layers, seq, width, hidden):
        padded = seq + TILE
        pairs = width // (2 * HD)
        tiles = seq // TILE
        ff = hidden // width
        v = pltpu.VMEM
        arrays = dict(
            acc=v((seq, width), F32),
            acc_t=v((width, seq), F32),
            xhat=v((layers, 2, seq, width), BF16),
            rstd=v((seq, 128), F32),
            normed=v((seq, width), BF16),
            normed_t=v((layers, 2, width, seq), BF16),
            q_t=v((layers, width, seq), BF16),
            k_pad=v((layers, padded, width), BF16),
            v_pad=v((layers, padded, width), BF16),
            tr_pad=v((width, padded), BF16),
            probs=v((layers, pairs, tiles, WINDOW, 2 * TILE), BF16),
            near_t=v((layers, width, seq), BF16),
            tanh_t=v((layers, width, seq), BF16),
            s_one=v((layers, pairs, 2 * HD, 2 * HD), F32),
            s_two=v((layers, pairs, 2 * HD, 2 * HD), F32),
            rden=v((layers, pairs, 8, seq), F32),
            mixed_t=v((layers, width, seq), BF16),
            act_t=v((layers, ff, width, seq), BF16),
            dact=v((layers, ff, seq, width), BF16),
            band=v((tiles, WINDOW, 2 * TILE), BF16),
            cols=v((width, 128), F32),
            gm_t=v((width, seq), BF16),
            gk_pad=v((padded, width), F32),
            gv_pad=v((padded, width), F32),
            vecs=v((layers, VROWS, width), F32),
            vgrads=v((layers, VROWS, width), F32),
        )
        return {n: a for n, a in arrays.items() if seq != width or n not in TWINS}

    def w_rows(self, l, first):
        return self.packed[l, :, :, :, :, pl.ds(first, GROUP), :].reshape(self.width, self.width)

    def w_qkv(self, l, n):
        return self.w_rows(l, GROUP * n)

    def w_attn(self, l):
        return self.w_rows(l, 3 * GROUP)

    def w_in(self, l, j):
        return self.w_rows(l, pl.multiple_of(4 * GROUP + GROUP * j, GROUP))

    def out_at(self, j):
        per = self.hidden // (self.width // GROUP)
        return j, pl.ds((4 + self.ff_blocks) * GROUP, per)

    def w_out(self, l, j):
        groups, rows = self.out_at(j)
        return self.packed[l, groups, :, :, :, rows, :].reshape(self.width, self.width)

    def put_rows(self, l, first, value):
        self.grads[:, :, :, :, pl.ds(first, GROUP), :] = value.astype(BF16).reshape(
            self.groups + (GROUP, self.width)
        )

    def put_out(self, l, j, value):
        groups, rows = self.out_at(j)
        per = self.hidden // (self.width // GROUP)
        self.grads[groups, :, :, :, rows, :] = value.astype(BF16).reshape(
            self.groups[1:] + (per, self.width)
        )

    def vec(self, l, row):
        return self.vecs[l, pl.ds(row, 1), :]

    def keep(self, value):
        return jnp.where(row_index(value.shape) < self.length, value, 0.0)

    def setup(self):
        shape = (WINDOW, 2 * TILE)
        key, query = row_index(shape) - PAD, col_index(shape) % TILE
        for t in range(self.tiles):
            pos = key + t * TILE
            ok = (jnp.abs(key - query) <= BAND) & (pos >= 0)
            ok = ok & ((pos < self.length) | (key == query))
            self.band[t] = jnp.where(ok, 0.0, -1e30).astype(BF16)
        zero_head = jnp.zeros((PAD, self.width), BF16)
        zero_tail = jnp.zeros((self.padded - PAD - self.seq, self.width), BF16)
        for l in range(self.layers):
            for ref in (self.k_pad, self.v_pad):
                ref[l, :PAD] = zero_head
                ref[l, PAD + self.seq :] = zero_tail

    def setup_vecs(self):
        eye = (row_index((self.width, self.width)) == col_index((self.width, self.width))).astype(
            BF16
        )
        for l in range(self.layers):
            self.cols[:, VROWS * l : VROWS * (l + 1)] = nt(eye, self.vecs[l].astype(BF16))

    def rows(self, body):
        @pl.loop(0, self.seq // ROWS)
        def _(i):
            body(pl.ds(pl.multiple_of(i * ROWS, ROWS), ROWS))

    def norm(self, l, which, source):
        def body(at):
            value = source[at, :]
            centered = value - jnp.mean(value, axis=-1, keepdims=True)
            rstd = lax.rsqrt(jnp.mean(centered * centered, axis=-1, keepdims=True) + EPSILON)
            xhat = centered * rstd
            n = 2 * l + which
            self.rstd[at, n : n + 1] = rstd
            self.xhat[l, which, at, :] = xhat.astype(BF16)
            normed = xhat * self.vec(l, GAIN + which) + self.vec(l, SHIFT + which)
            self.normed[at, :] = normed.astype(BF16)

        self.rows(body)
        self.normed_t[l, which] = self.normed[...].T

    def pad_keep(self):
        row = row_index((self.padded, 2 * HD)) - PAD
        return (row >= 0) & (row < self.length)

    def fwd_qkv(self, l, n):
        out = (nn(self.normed[...], self.w_qkv(l, n)) + self.vec(l, BQKV + n)).astype(BF16)
        if n == 0:
            self.q_t[l] = out.T
        else:
            (self.k_pad, self.v_pad)[n - 1][l, PAD : PAD + self.seq] = out
        if n == 2:
            self.tr_pad[...] = self.v_pad[l].T

    def pair_at(self, p):
        return pl.ds(pl.multiple_of(p * 2 * HD, 2 * HD), 2 * HD)

    def fwd_near(self, l, p):
        at = self.pair_at(p)
        spans = [
            (slice(t * TILE, (t + 1) * TILE), slice(t * TILE, t * TILE + WINDOW))
            for t in range(self.tiles)
        ]
        scores = [nn(self.k_pad[l, window, at], spread(self.q_t[l, at, here])) for here, window in spans]
        for t, (here, window) in enumerate(spans):
            one = scores[t] * (HD**-0.5) + self.band[t].astype(F32)
            weights = jnp.exp(one - jnp.max(one, axis=0, keepdims=True))
            inverse = 1.0 / jnp.sum(weights, axis=0, keepdims=True)
            probs = (weights * inverse).astype(BF16)
            self.probs[l, p, t] = probs
        for t, (here, window) in enumerate(spans):
            near = fold(nn(self.tr_pad[at, window], self.probs[l, p, t]))
            self.near_t[l, at, here] = near.astype(BF16)

    def features(self, x):
        grown = jnp.exp(jnp.minimum(x, 0.0))
        return jnp.where(x > 0, x + 1.0, grown), grown, jnp.tanh(x)

    def key_features(self, l, at):
        phi, slope, tanh = self.features(self.k_pad[l, :, at].astype(F32))
        ok = self.pad_keep()
        return (
            jnp.where(ok, phi, 0.0).astype(BF16),
            slope,
            jnp.where(ok, tanh, 0.0).astype(BF16),
            tanh,
        )

    def coefficient(self):
        wide = jnp.full((1, 1), HD, F32) * self.length.astype(F32)
        return lax.rsqrt(wide)

    def heads_row(self, two, seq):
        return jnp.concatenate(
            [
                jnp.broadcast_to(two[0:1], (HD, seq)),
                jnp.broadcast_to(two[1:2], (HD, seq)),
            ],
            axis=0,
        )

    def fwd_far(self, l, p):
        at = self.pair_at(p)
        phk, _, tk, _ = self.key_features(l, at)
        values_t = self.tr_pad[at, :]
        s_one = head_diag(nn(values_t, phk))
        s_two = head_diag(nn(values_t, tk))
        total = col_sum(phk.astype(F32))
        self.s_one[l, p], self.s_two[l, p] = s_one, s_two
        phi, _, tanh = self.features(self.q_t[l, at, :].astype(F32))
        phq, tq = phi.astype(BF16), tanh.astype(BF16)
        shape = (8, 2 * HD)
        mine = (row_index(shape) == 0) == (col_index(shape) < HD)
        z_high, z_low = split(jnp.where(mine & (row_index(shape) < 2), total, 0.0))
        den = nn(z_high, phq) + nn(z_low, phq)
        rden = 1.0 / jnp.where(row_index(den.shape) < 2, den, 1.0)
        self.rden[l, p] = rden
        total_col = jnp.broadcast_to(total, (8, 2 * HD)).T
        n = VROWS * l
        self.cols[at, n : n + 1] = total_col[:, 0:1]
        high, low = split(s_one)
        far_elu = (nn(high, phq) + nn(low, phq)) * self.heads_row(rden, self.seq)
        high, low = split(s_two)
        far_tanh = (nn(high, tq) + nn(low, tq)) * self.coefficient()
        self.tanh_t[l, at, :] = far_tanh.astype(BF16)
        blend = self.cols[at, VROWS * l : VROWS * (l + 1)]
        self.mixed_t[l, at, :] = (
            blend[:, BLEND : BLEND + 1] * self.near_t[l, at, :].astype(F32)
            + blend[:, BLEND + 1 : BLEND + 2] * far_elu
            + blend[:, BLEND + 2 : BLEND + 3] * far_tanh
        ).astype(BF16)

    def fwd_attn(self, l):
        mixed = self.mixed_t[l].T
        out = nn(mixed, self.w_attn(l)) + self.vec(l, OBIAS)
        self.gk_pad[: self.seq] = self.h[...] + self.keep(out)
        self.norm(l, 1, self.gk_pad)

    def fwd_up(self, l, j):
        pre = nn(self.normed[...], self.w_in(l, j)) + self.vec(l, BIN + j)
        square = pre * pre
        th = jnp.tanh(GELU_C * pre * (1.0 + GELU_A * square))
        half = 0.5 * (1.0 + th)
        slope = half + (0.5 * GELU_C) * pre * (1.0 - th * th) * (1.0 + 3.0 * GELU_A * square)
        self.dact[l, j] = slope.astype(BF16)
        self.act_t[l, j] = (pre * half).astype(BF16).T

    def fwd_down(self, l):
        self.acc[...] = jnp.broadcast_to(self.vec(l, OBIAS + 1), self.acc.shape)

        @pl.loop(0, self.ff_blocks)
        def _(j):
            self.acc[...] += nn(self.act_t[l, j].T, self.w_out(l, j))

    def fwd_end(self, l):
        self.h[...] = self.gk_pad[: self.seq] + self.keep(self.acc[...])

    def put_vec(self, l, row, value):
        self.vgrads[l, pl.ds(row, 1), :] = value

    def bwd_start(self, l, source):
        gz = self.keep(source[...].astype(F32)).astype(BF16)
        self.normed[...] = gz
        self.put_vec(l, OBIAS + 1, col_sum(gz.astype(F32)))

    def bwd_out(self, l, j):
        self.put_out(l, j, nn(self.act_t[l, j], self.normed[...]))

    def bwd_up(self, l, j):
        grad = nt(self.normed[...], self.w_out(l, j))
        gpre = (grad * self.dact[l, j].astype(F32)).astype(BF16)
        self.put_vec(l, BIN + j, col_sum(gpre.astype(F32)))
        first = pl.multiple_of(4 * GROUP + GROUP * j, GROUP)
        self.put_rows(l, first, nn(self.normed_t[l, 1], gpre))
        self.acc[...] += nt(gpre, self.w_in(l, j))

    def norm_back(self, l, which):
        self.put_vec(l, GAIN + which, jnp.zeros((1, self.width), F32))
        self.put_vec(l, SHIFT + which, jnp.zeros((1, self.width), F32))

        def body(at):
            grad = self.acc[at, :]
            xhat = self.xhat[l, which, at, :].astype(F32)
            self.vgrads[l, pl.ds(GAIN + which, 1), :] += col_sum(grad * xhat)
            self.vgrads[l, pl.ds(SHIFT + which, 1), :] += col_sum(grad)
            grad = grad * self.vec(l, GAIN + which)
            mean = jnp.mean(grad, axis=-1, keepdims=True)
            slope = jnp.mean(grad * xhat, axis=-1, keepdims=True)
            n = 2 * l + which
            self.h[at, :] += self.rstd[at, n : n + 1] * (grad - mean - xhat * slope)

        self.rows(body)

    def bwd_attn(self, l):
        self.norm_back(l, 1)
        go = self.keep(self.h[...]).astype(BF16)
        self.put_vec(l, OBIAS, col_sum(go.astype(F32)))
        self.put_rows(l, 3 * GROUP, nn(self.mixed_t[l], go))
        self.gm_t[...] = nt(self.w_attn(l), go).astype(BF16)
        self.tr_pad[...] = self.k_pad[l].T
        self.gk_pad[...] = jnp.zeros_like(self.gk_pad)
        self.gv_pad[...] = jnp.zeros_like(self.gv_pad)

    def bwd_near(self, l, p):
        at = self.pair_at(p)
        blend = self.cols[at, VROWS * l : VROWS * (l + 1)]
        spans = [
            (slice(t * TILE, (t + 1) * TILE), slice(t * TILE, t * TILE + WINDOW))
            for t in range(self.tiles)
        ]
        grads = []
        for here, _ in spans:
            grad = blend[:, BLEND : BLEND + 1] * self.gm_t[at, here].astype(F32)
            grads.append(spread(grad.astype(BF16)))
        dprobs = [nn(self.v_pad[l, window, at], g) for g, (_, window) in zip(grads, spans)]
        terms = []
        for t in range(self.tiles):
            wide = self.probs[l, p, t].astype(F32)
            term = wide * dprobs[t]
            inner = jnp.sum(term, axis=0, keepdims=True)
            terms.append(((term - wide * inner) * (HD**-0.5)).astype(BF16))
        for gs, (here, window) in zip(terms, spans):
            self.acc_t[at, here] = fold(nn(self.tr_pad[at, window], gs))
        keys = [nt(gs, spread(self.q_t[l, at, here])) for gs, (here, _) in zip(terms, spans)]
        values = [nt(self.probs[l, p, t], grads[t]) for t in range(self.tiles)]
        for t, (_, window) in enumerate(spans):
            self.gk_pad[window, at] += keys[t]
            self.gv_pad[window, at] += values[t]

    def bwd_far(self, l, p):
        at = self.pair_at(p)
        seq = self.seq
        blend = self.cols[at, VROWS * l : VROWS * (l + 1)]
        gm = self.gm_t[at, :].astype(F32)
        q = self.q_t[l, at, :].astype(F32)
        phi_q, slope_q, tanh_q = self.features(q)
        phq, tq = phi_q.astype(BF16), tanh_q.astype(BF16)
        high, low = split(self.s_one[l, p])
        far_elu = (nn(high, phq) + nn(low, phq)) * self.heads_row(self.rden[l, p], seq)
        column = lambda a: jnp.sum(a, axis=1, keepdims=True)
        sums = [
            column(gm * self.near_t[l, at, :].astype(F32)),
            column(gm * far_elu),
            column(gm * self.tanh_t[l, at, :].astype(F32)),
        ]
        for n, one in enumerate(sums):
            self.cols[at, GBLEND + n : GBLEND + n + 1] = one
        phk, slope_k, tk, tanh_k = self.key_features(l, at)
        values = self.v_pad[l, :, at]
        gnum = (blend[:, BLEND + 1 : BLEND + 2] * gm * self.heads_row(self.rden[l, p], seq)).astype(
            BF16
        )
        prod = gnum.astype(F32) * far_elu
        gden_one = -col_sum(prod[:HD])
        gden_two = -col_sum(prod[HD:])
        gden = jnp.concatenate([gden_one, gden_two, jnp.zeros((6, seq), F32)], axis=0)
        s_one = self.s_one[l, p].T
        high, low = split(s_one)
        gphq = nn(high, gnum) + nn(low, gnum) + self.cols[at, VROWS * l : VROWS * l + 1] * self.heads_row(gden, seq)
        gs_one = head_diag(nt(phq, gnum))
        gs_high, gs_low = split(gs_one)
        gden_high, gden_low = split(gden)
        both = nt(gden_high, phq) + nt(gden_low, phq)
        gzz = jnp.where(col_index((1, 2 * HD)) < HD, both[0:1], both[1:2])
        gtanh = (blend[:, BLEND + 2 : BLEND + 3] * gm * self.coefficient()).astype(BF16)
        gtq = nn(self.s_two[l, p].T.astype(BF16), gtanh)
        gs_two = head_diag(nt(tq, gtanh)).astype(BF16)
        self.acc_t[at, :] += gphq * jnp.where(q > 0, 1.0, slope_q) + gtq * (1.0 - tanh_q * tanh_q)
        gphk = nt(values, gs_high) + nt(values, gs_low) + gzz
        gtk = nt(values, gs_two)
        grad_k = gphk * slope_k + gtk * (1.0 - tanh_k * tanh_k)
        self.gk_pad[:, at] += jnp.where(self.pad_keep(), grad_k, 0.0)
        self.gv_pad[:, at] += nn(phk, gs_high) + nn(tk, gs_two)

    def bwd_qkv(self, l, n):
        rows = slice(PAD, PAD + self.seq)
        if n == 0:
            grad = self.acc_t[...].T.astype(BF16)
        else:
            grad = (self.gk_pad, self.gv_pad)[n - 1][rows, :].astype(BF16)
        self.put_vec(l, BQKV + n, col_sum(grad.astype(F32)))
        self.put_rows(l, GROUP * n, nn(self.normed_t[l, 0], grad))
        total = self.gv_pad.at[rows]
        part = nt(grad, self.w_qkv(l, n))
        if n == 2:
            total[...] = part
        elif n == 1:
            total[...] += part
        else:
            self.acc[...] = total[...] + part

    def bwd_end(self, l):
        self.vgrads[l, pl.ds(BLEND, 3), :] = self.cols[...].T[GBLEND : GBLEND + 3]
        self.norm_back(l, 0)


class Comm:
    def __init__(self, depth, sems):
        self.sems = sems
        self.free = ([], [])
        self.made = [0, 0]
        self.clock = 0
        self.heard = {}
        dp, fsdp = lax.axis_index("dp"), lax.axis_index("fsdp")
        self.depth = depth
        self.at = {"z": dp // 2, "x": dp % 2, "y": fsdp // 2, "c": fsdp % 2}

    def device(self, **moved):
        at = dict(self.at, **moved)
        return (at["z"] * 2 + at["x"], at["y"] * 2 + at["c"])

    def steps(self, axis):
        return range(1, self.depth) if axis == "z" else range(1, 2)

    def other(self, axis, step=1):
        if axis == "z":
            return lax.rem(self.at["z"] + step, self.depth)
        return 1 - self.at[axis]

    def barrier(self):
        semaphore = pltpu.get_barrier_semaphore()
        peers = [
            self.device(**{axis: self.other(axis, k)}) for axis in "zxyc" for k in self.steps(axis)
        ]
        for peer in peers:
            pl.semaphore_signal(semaphore, inc=1, device_id=peer, device_id_type=MESH)
        pl.semaphore_wait(semaphore, len(peers))

    def take(self, side, before):
        for entry in self.free[side]:
            if entry[0] < before:
                self.free[side].remove(entry)
                return entry[1]
        self.made[side] += 1
        return self.made[side] - 1

    def copy(self, source, target, axis, step):
        self.clock += 1
        sent = self.take(0, self.clock)
        arrived = self.take(1, self.heard.get((axis, step), -1))
        made = pltpu.make_async_remote_copy(
            src_ref=source,
            dst_ref=target,
            send_sem=self.sems[0].at[sent],
            recv_sem=self.sems[1].at[arrived],
            device_id=self.device(**{axis: self.other(axis, step)}),
            device_id_type=MESH,
        )
        made.start()
        back = (axis, self.depth - step if axis == "z" else 1)
        return made, sent, arrived, back, self.clock

    def wait(self, copies):
        for made, sent, arrived, back, when in copies:
            made.wait()
            self.clock += 1
            self.free[0].append((self.clock, sent))
            self.free[1].append((self.clock, arrived))
            self.heard[back] = max(when, self.heard.get(back, -1))

    def index(self, whole, moved=None):
        at = dict(self.at, **(moved or {}))
        return tuple(slice(None) if axis in whole else at[axis] for axis in "zxyc")

    def gather(self, view, order):
        cores = []
        for stage in range(4):
            whole, started = order[:stage], []
            if stage < 3:
                axis = order[stage]
                block = view(self.index(whole))
                started = [self.copy(block, block, axis, k) for k in self.steps(axis)]
            if "z" in whole:
                axis = order[stage - 1]
                if axis == "z":
                    block = view(self.index(whole))
                else:
                    block = view(self.index(order[: stage - 1], {axis: self.other(axis)}))
                cores.append(self.copy(block, block, "c", 1))
            yield
            self.wait(started)
        self.wait(cores)

    @staticmethod
    def add(mine, others):
        @pl.loop(0, mine.shape[0])
        def _(n):
            for rest in itertools.product(*[range(m) for m in mine.shape[1:-2]]):
                at = (n,) + rest
                total = mine[at]
                for other in others:
                    total = total + other[at]
                mine[at] = total

    def scatter(self, view, slot, order, put):
        axes = "c" + order
        for stage, axis in enumerate(axes):
            whole = axes[stage + 1 :]
            started = []
            for k in self.steps(axis):
                block = view(self.index(whole, {axis: self.other(axis, k)}))
                started.append(self.copy(block, slot(stage, k - 1), axis, k))
            yield
            self.wait(started)
            mine = view(self.index(whole))
            arrived = [slot(stage, k - 1) for k in self.steps(axis)]
            if whole:
                self.add(mine, arrived)
            else:
                total = mine[...].astype(F32)
                for one in arrived:
                    total = total + one[...].astype(F32)
                put(total)


ORDERS = {
    ("gather", 0): (
        (2, "zyx"), (7, "zyx"), (5, "zxy"), (1, "zyx"),
        (8, "zxy"), (0, "zyx"), (4, "zyx"), (10, "zyx"),
        (3, "xzy"), (9, "zxy"), (11, "xzy"), (6, "zxy"),
    ),
    ("gather", 1): (
        (2, "zxy"), (6, "zyx"), (0, "yzx"), (1, "yzx"),
        (3, "xzy"), (7, "xzy"), (4, "yzx"), (5, "xzy"),
        (9, "zxy"), (10, "yzx"), (8, "zyx"), (11, "xzy"),
    ),
    ("scatter", 0): (
        (6, "xzy"), (9, "xzy"), (2, "xyz"), (8, "yxz"),
        (11, "yxz"), (10, "xzy"), (3, "yxz"), (5, "yxz"),
        (0, "xyz"), (4, "yxz"), (7, "yzx"), (1, "yxz"),
    ),
    ("scatter", 1): (
        (1, "xzy"), (0, "xzy"), (5, "yzx"), (7, "yxz"),
        (4, "yxz"), (9, "yxz"), (6, "xyz"), (10, "xzy"),
        (2, "yxz"), (3, "xzy"), (11, "yzx"), (8, "xzy"),
    ),
}
LINK, HOP = 0.0235, 2.0
CORE, CORE_HOP = 0.0027, 0.9
ISSUE, BACKLOG, AHEAD = 0.04, 5.0, 13


def plan(layers, segments, parts):
    size = {"z": 4, "x": 2, "y": 2, "c": 2}
    free = dict.fromkeys("zxyc", 0.0)
    clock, steps = 0.0, []
    stage = dict.fromkeys(parts, 0)
    ready = {n: 0.0 if not scatter else None for n, (_, _, scatter) in parts.items()}
    done = set()
    waiting = list(segments)

    def send(axis, blocks, rows):
        link, hop = (CORE, CORE_HOP) if axis == "c" else (LINK, HOP)
        load = blocks * rows * link * (size["z"] if axis == "z" else 1)
        free[axis] = max(free[axis], clock) + load
        return free[axis] + hop

    def count(axes):
        total = 1
        for axis in axes:
            total *= size[axis]
        return total

    def step(name):
        nonlocal clock
        rows, order, scatter = parts[name]
        now = stage[name]
        steps.append((name,))
        stage[name] += 1
        last = 4
        if scatter:
            axes = "c" + order
            if now > 0:
                clock += 0.02 + count(axes[now:]) * rows * 0.0002
            if now < last:
                arrives = send(axes[now], count(axes[now + 1 :]), rows)
                clock += ISSUE * (3 if axes[now] == "z" else 1)
        else:
            arrives = ready[name]
            if now < 3:
                arrives = send(order[now], count(order[:now]), rows)
                clock += ISSUE * (3 if order[now] == "z" else 1)
            if "z" in order[:now] and now < last:
                whole = order[:now] if order[now - 1] == "z" else order[: now - 1]
                core = send("c", count(whole), rows)
                clock += ISSUE
                if now == 3:
                    arrives = core
        if now == last:
            done.add(name)
            ready[name] = None
        else:
            ready[name] = arrives

    def startable(name):
        _, order, scatter = parts[name]
        first = "c" if scatter else order[0]
        return stage[name] > 0 or free[first] <= clock + BACKLOG

    while len(done) < len(parts) or waiting:
        left = [n for n in parts if n not in done][:AHEAD]
        able = [n for n in left if ready[n] is not None and ready[n] <= clock and startable(n)]
        if able:
            step(able[0])
            continue
        if waiting:
            name, layer, argument, cost, needs, makes = waiting[0]
            if all(n in done for n in needs):
                waiting.pop(0)
                steps.append((name, layer, argument))
                clock += cost
                for n in makes:
                    ready[n] = clock
                continue
        later = [ready[n] for n in left if ready[n] is not None and ready[n] > clock]
        later += [free[a] - BACKLOG for a in "zxyc" if free[a] - BACKLOG > clock]
        clock = min(later)
    return steps, clock


def make_plan(layers, pairs, ff, rows):
    units = rows // GROUP
    parts = {("gather", 0, "vectors"): (4, "zxy", False)}
    for l in range(layers):
        for u, order in ORDERS["gather", l]:
            parts["gather", l, u] = (GROUP, order, False)
    for l in reversed(range(layers)):
        for u, order in ORDERS["scatter", l]:
            parts["scatter", l, u] = (GROUP, order, True)
    parts["scatter", 0, "vectors"] = (8, "yxz", True)
    gathers = lambda l, us: [("gather", l, u) for u in us]
    scatters = lambda l, us: [("scatter", l, u) for u in us]
    downs = range(units - ff, units)
    segments = []
    add = lambda *s: segments.append(s)
    halves = [(0, pairs)]
    twos = [(j, min(j + STEP, ff)) for j in range(0, ff, STEP)]
    add("start", 0, None, 0.5, [], [])
    add("spread", 0, None, 0.5, [("gather", 0, "vectors")], [])
    for l in range(layers):
        add("norm", l, 0, 0.7, [], [])
        for n in range(3):
            add("fwd_qkv", l, n, 0.25, gathers(l, [n]), [])
        for half in halves:
            add("fwd_near", l, half, 2.6, [], [])
        for half in halves:
            add("fwd_far", l, half, 2.3, [], [])
        add("fwd_attn", l, None, 1.3, gathers(l, [3]), [])
        for j, end in twos:
            add("fwd_up", l, (j, end), 1.05 * (end - j), gathers(l, range(4 + j, 4 + end)), [])
        if l == layers - 1:
            add("bwd_start", l, None, 0.3, [], [])
            add("bwd_out", l, (0, ff), 0.43 * ff, [], scatters(l, downs))
        add("fwd_down", l, None, 1.9, gathers(l, downs), [])
    for l in reversed(range(layers)):
        again = lambda us: scatters(l + 1, us) if l < layers - 1 else []
        if l < layers - 1:
            add("bwd_start", l, None, 0.3, [], [])
            add("bwd_out", l, (0, ff), 0.43 * ff, again(downs), scatters(l, downs))
        for j, end in twos:
            units = range(4 + j, 4 + end)
            add("bwd_up", l, (j, end), 1.33 * (end - j), again(units), scatters(l, units))
        add("bwd_attn", l, None, 1.6, again([3]), scatters(l, [3]))
        for half in halves:
            add("bwd_near", l, half, 3.1, [], [])
        for half in halves:
            add("bwd_far", l, half, 3.8, [], [])
        for n in (2, 1, 0):
            add("bwd_qkv", l, n, 0.6, again([n]), scatters(l, [n]))
        add("bwd_end", l, None, 0.9, [], [])
    add("collect", 0, None, 0.5, [], scatters(0, ["vectors"]))
    return plan(layers, segments, parts), parts


class Vectors:
    def __init__(self, layers, width, hidden):
        self.layers, self.width = layers, width
        self.devices = width // GROUP
        self.long = [(BQKV, 3), (BIN, hidden // width)]

    def swap(self, tiles, back):
        lane = lax.broadcasted_iota(jnp.int32, tiles.shape, 2)
        result = tiles
        for l in range(self.layers):
            for row, count in self.long:
                first = l * VROWS + row
                columns = [tiles[:, :, first + n : first + n + 1] for n in range(count)]
                if back:
                    both = jnp.stack(columns, axis=1).reshape(count, self.devices, GROUP, 1)
                    columns = [both[n] for n in range(count)]
                else:
                    both = jnp.concatenate(columns, axis=0)
                    both = both.reshape(self.devices, count, GROUP, 1)
                    columns = [both[:, n] for n in range(count)]
                for n in range(count):
                    result = jnp.where(lane == first + n, columns[n], result)
        return result

    def spread(self, shares, vecs, cols):
        tiles = shares[...].reshape(self.devices, GROUP, 128).astype(F32)
        columns = self.swap(tiles, True).reshape(self.width, 128)
        cols[...] = columns
        vecs[...] = columns.T[: self.layers * VROWS].reshape(vecs.shape)

    def collect(self, vgrads, shares):
        rows = vgrads[...].reshape(self.layers * VROWS, self.width)
        rest = jnp.zeros((128 - self.layers * VROWS, self.width), F32)
        columns = jnp.concatenate([rows, rest], axis=0).T
        tiles = self.swap(columns.reshape(self.devices, GROUP, 128), False)
        shares[...] = tiles.reshape(shares.shape)

    def pack(self, refs, table):
        table[...] = jnp.zeros_like(table)
        for l in range(self.layers):
            for ref, row in zip(refs, VECTOR_ROWS):
                row += l * VROWS
                if len(ref.shape) == 3:
                    table[row : row + ref.shape[1], :GROUP] = ref[l].astype(F32)
                else:
                    value = ref[l : l + 1, :].astype(F32)
                    for n in range(ref.shape[1] // GROUP):
                        piece = value[:, n * GROUP : (n + 1) * GROUP]
                        table[row + n : row + n + 1, :GROUP] = piece
        return table[...].T[:GROUP]

    def unpack(self, tile, table, refs):
        rest = jnp.zeros((128 - GROUP, 128), F32)
        table[...] = jnp.concatenate([tile, rest], axis=0).T
        for l in range(self.layers):
            for ref, row in zip(refs, VECTOR_ROWS):
                row += l * VROWS
                if len(ref.shape) == 3:
                    ref[l] = table[row : row + ref.shape[1], :GROUP]
                else:
                    count = ref.shape[1] // GROUP
                    rows = [table[row + n : row + n + 1, :GROUP] for n in range(count)]
                    ref[l : l + 1, :] = jnp.concatenate(rows, axis=1)


class Program:
    def __init__(self, net, comm, vectors, r):
        self.net, self.comm, self.vectors = net, comm, vectors
        self.__dict__.update(r)

    def fill(self):
        own = self.comm.index(())
        width = self.net.width
        for l in range(self.net.layers):
            first = 0
            for ref in (self.w_qkv, self.w_attn, self.w_in):
                for n in range(ref.shape[2] // width):
                    rows = pl.ds(first, GROUP)
                    self.net.packed[(l,) + own + (rows,)] = ref[l, :, n * width : (n + 1) * width]
                    first += GROUP
            rows = pl.ds(first, self.w_out.shape[1])
            self.net.packed[(l,) + own + (rows,)] = self.w_out[l]
        refs = [getattr(self, name) for name in VECTORS]
        self.shares[own] = self.vectors.pack(refs, self.table).astype(BF16)

    def gather(self, l, unit, order):
        if unit == "vectors":
            return self.comm.gather(lambda index: self.shares.at[index], order)
        at = pl.ds(unit * GROUP, GROUP)
        return self.comm.gather(lambda index: self.net.packed.at[(l,) + index + (at,)], order)

    def scatter(self, l, unit, order):
        if unit == "vectors":
            arrivals, at, source = self.varrivals, (), self.vshares
        else:
            at = (pl.ds(unit * GROUP, GROUP),)
            arrivals, source = self.arrivals, self.net.grads
        depth = self.comm.depth
        every = slice(None)

        def slot(stage, k):
            if stage < 2:
                return arrivals[stage].at[(every,) * (3 - stage) + at]
            if stage == 2:
                span = slice(2 * k, 2 * k + 2) if order[1] == "z" else slice(0, depth)
                return arrivals[2].at[(span,) + at]
            return arrivals[2].at[(2 * (depth - 1) if order[1] == "z" else depth + k,) + at]

        put = functools.partial(self.put, l, unit)
        return self.comm.scatter(lambda index: source.at[index + at], slot, order, put)

    def put(self, l, unit, total):
        if unit == "vectors":
            self.gsmall[...] = total
            return
        width = self.net.width
        for ref in (self.gw_qkv, self.gw_attn, self.gw_in):
            count = ref.shape[2] // width
            if unit < count:
                ref[l, :, unit * width : (unit + 1) * width] = total
                return
            unit -= count
        self.gw_out[l, unit * GROUP : (unit + 1) * GROUP, :] = total

    def start(self, l, _):
        self.net.setup()
        self.net.h[...] = self.tokens[...].astype(F32)

    def spread(self, l, _):
        self.vectors.spread(self.shares, self.net.vecs, self.net.cols)

    def collect(self, l, _):
        self.vectors.collect(self.net.vgrads, self.vshares)

    def norm(self, l, _):
        self.net.norm(l, 0, self.net.h)

    def fwd_attn(self, l, _):
        self.net.fwd_attn(l)

    def fwd_down(self, l, _):
        self.net.fwd_down(l)
        self.net.fwd_end(l)
        if l == self.net.layers - 1:
            self.mixed_out[...] = self.net.h[...].astype(BF16)
            self.net.h[...] = self.cotangent[...].astype(F32)

    def bwd_up(self, l, span):
        if span[0] == 0:
            self.net.acc[...] = jnp.zeros_like(self.net.acc)
        self.over(self.net.bwd_up, l, span)

    def bwd_start(self, l, _):
        self.net.bwd_start(l, self.cotangent if l == self.net.layers - 1 else self.net.h)

    def bwd_attn(self, l, _):
        self.net.bwd_attn(l)

    def bwd_end(self, l, _):
        self.net.bwd_end(l)

    def over(self, body, l, span):
        @pl.loop(*span)
        def _(p):
            body(l, p)

    def run(self):
        net = self.net
        rows = net.packed.shape[-2]
        (steps, _), parts = make_plan(net.layers, net.pairs, net.ff_blocks, rows)
        running = {}
        for (kind, l, unit), (_, order, _) in parts.items():
            make = self.gather if kind == "gather" else self.scatter
            running[kind, l, unit] = make(l, unit, order)
        self.fill()
        self.comm.barrier()
        for name, *rest in steps:
            if not rest:
                next(running[name], None)
            elif hasattr(self, name):
                getattr(self, name)(*rest)
            elif isinstance(rest[1], tuple):
                self.over(getattr(net, name), *rest)
            else:
                getattr(net, name)(*rest)
        assert max(self.comm.made) <= SEMAPHORES


VECTORS = ("gains", "shifts", "b_qkv", "blends", "b_in", "biases")
WEIGHTS = ("w_qkv", "w_attn", "w_in", "w_out")
INPUTS = ("tokens", "cotangent") + VECTORS + WEIGHTS
OUTPUTS = ("mixed_out", "h", "gsmall", "gw_qkv", "gw_attn", "gw_in", "gw_out")
SEMAPHORES = 96


def fused_body(sizes, depth, names, length_ref, *refs):
    named = dict(zip(INPUTS + OUTPUTS + names, refs))
    arrivals = [named.pop("arrive%d" % n) for n in range(3)]
    varrivals = [named.pop("varrive%d" % n) for n in range(3)]
    sems = named.pop("send"), named.pop("recv")
    inner = {n: r for n, r in named.items() if n not in INPUTS}
    net = Net(*sizes, length_ref[0], inner)
    comm = Comm(depth, sems)
    vectors = Vectors(sizes[0], sizes[2], sizes[3])
    Program(net, comm, vectors, dict(named, arrivals=arrivals, varrivals=varrivals)).run()


def fused(lengths, tokens, cotangent, vectors, weights):
    layers, _, width = weights[1].shape
    hidden = weights[2].shape[2]
    seq = tokens.shape[0]
    sizes = (layers, seq, width, hidden)
    rows = sum(w.shape[1] * w.shape[2] for w in weights) // width
    groups = group_shape(width, hidden)
    tile = (GROUP, 128)
    vmem = pl.BlockSpec(memory_space=pltpu.VMEM)
    scratch = dict(Net.scratch(*sizes))
    scratch["packed"] = pltpu.VMEM((layers,) + groups + (rows, width), BF16)
    scratch["grads"] = pltpu.VMEM(groups + (rows, width), BF16)
    scratch["shares"] = pltpu.VMEM(groups + tile, BF16)
    scratch["vshares"] = pltpu.VMEM(groups + tile, F32)
    scratch["table"] = pltpu.VMEM((128, 128), F32)
    kept = (groups[:3], groups[:2], (2 * groups[0] - 1,))
    for n, lead in enumerate(kept):
        scratch["arrive%d" % n] = pltpu.VMEM(lead + (rows, width), BF16)
        scratch["varrive%d" % n] = pltpu.VMEM(lead + tile, F32)
    scratch["send"] = pltpu.SemaphoreType.DMA((SEMAPHORES,))
    scratch["recv"] = pltpu.SemaphoreType.DMA((SEMAPHORES,))
    return pl.pallas_call(
        functools.partial(fused_body, sizes, groups[0], tuple(scratch)),
        out_shape=(
            jax.ShapeDtypeStruct(tokens.shape, BF16),
            jax.ShapeDtypeStruct(tokens.shape, F32),
            jax.ShapeDtypeStruct(tile, F32),
        )
        + tuple(jax.ShapeDtypeStruct(w.shape, F32) for w in weights),
        in_specs=[pl.BlockSpec(memory_space=pltpu.SMEM)] + [vmem] * len(INPUTS),
        out_specs=(vmem,) * len(OUTPUTS),
        scratch_shapes=list(scratch.values()),
        compiler_params=pltpu.CompilerParams(
            collective_id=0, has_side_effects=True, vmem_limit_bytes=63 * 2**20
        ),
    )(lengths, tokens, cotangent, *vectors, *weights)


def finish_body(vectors, big, *refs):
    sources, tile, refs = refs[:big], refs[big], refs[big + 1 :]
    targets, outs, table, sems = refs[:big], refs[big : -big - 2], refs[-big - 2], refs[-big - 1]
    buffers = refs[-big:]
    loads = [
        pltpu.make_async_copy(source, buffer, sems.at[0, n])
        for n, (source, buffer) in enumerate(zip(sources, buffers))
    ]
    stores = [
        pltpu.make_async_copy(buffer, target, sems.at[1, n])
        for n, (buffer, target) in enumerate(zip(buffers, targets))
    ]
    for one in loads:
        one.start()
    vectors.unpack(tile[...], table, outs)
    for load, store in zip(loads, stores):
        load.wait()
        store.start()
    for one in stores:
        one.wait()


def finish(vectors, large, tile, shapes):
    anywhere, vmem = pl.BlockSpec(memory_space=pl.ANY), pl.BlockSpec(memory_space=pltpu.VMEM)
    outs = pl.pallas_call(
        functools.partial(finish_body, vectors, len(large)),
        out_shape=tuple(jax.ShapeDtypeStruct(a.shape, a.dtype) for a in large)
        + tuple(jax.ShapeDtypeStruct(shape, F32) for shape in shapes),
        in_specs=[anywhere] * len(large) + [vmem],
        out_specs=(anywhere,) * len(large) + (vmem,) * len(shapes),
        scratch_shapes=[
            pltpu.VMEM((128, 128), F32),
            pltpu.SemaphoreType.DMA((2, len(large))),
        ]
        + [pltpu.VMEM(a.shape, a.dtype) for a in large],
        compiler_params=pltpu.CompilerParams(vmem_limit_bytes=62 * 2**20),
    )(*large, tile)
    return outs[: len(large)], outs[len(large) :]


def plain_body(sizes, names, length_ref, *refs):
    names = ("tokens", "cotangent", "packed", "vecs", "mixed_out", "h", "grads_out", "vgrads") + names
    named = dict(zip(names, refs))
    net = Net(*sizes, length_ref[0], named)

    def over(body, l):
        @pl.loop(0, net.pairs)
        def _(p):
            body(l, p)

    net.setup()
    net.setup_vecs()
    net.h[...] = named["tokens"][...].astype(F32)
    for l in range(net.layers):
        net.norm(l, 0, net.h)
        for n in range(3):
            net.fwd_qkv(l, n)
        over(net.fwd_near, l)
        over(net.fwd_far, l)
        net.fwd_attn(l)
        for j in range(net.ff_blocks):
            net.fwd_up(l, j)
        net.fwd_down(l)
        net.fwd_end(l)
    named["mixed_out"][...] = net.h[...].astype(BF16)
    net.h[...] = named["cotangent"][...].astype(F32)
    for l in reversed(range(net.layers)):
        net.bwd_start(l, net.h)
        net.acc[...] = jnp.zeros_like(net.acc)
        for j in range(net.ff_blocks):
            net.bwd_out(l, j)
            net.bwd_up(l, j)
        net.bwd_attn(l)
        over(net.bwd_near, l)
        over(net.bwd_far, l)
        for n in (2, 1, 0):
            net.bwd_qkv(l, n)
        net.bwd_end(l)
        copy = pltpu.make_async_copy(named["grads"], named["grads_out"].at[l], named["sem"])
        copy.start()
        copy.wait()


def plain(lengths, tokens, cotangent, packed, vecs):
    layers, rows, width = packed.shape[0], packed.shape[-2], packed.shape[-1]
    seq = tokens.shape[0]
    hidden = (rows // GROUP - 4) // 2 * width
    sizes = (layers, seq, width, hidden)
    scratch = dict(Net.scratch(*sizes))
    del scratch["vecs"], scratch["vgrads"]
    scratch["grads"] = pltpu.VMEM(packed.shape[1:], BF16)
    scratch["sem"] = pltpu.SemaphoreType.DMA
    vmem = pl.BlockSpec(memory_space=pltpu.VMEM)
    return pl.pallas_call(
        functools.partial(plain_body, sizes, tuple(scratch)),
        out_shape=(
            jax.ShapeDtypeStruct((seq, width), BF16),
            jax.ShapeDtypeStruct((seq, width), F32),
            jax.ShapeDtypeStruct(packed.shape, BF16),
            jax.ShapeDtypeStruct((layers, VROWS, width), F32),
        ),
        in_specs=[pl.BlockSpec(memory_space=pltpu.SMEM)] + [vmem] * 4,
        out_specs=(vmem, vmem, pl.BlockSpec(memory_space=pl.ANY), vmem),
        scratch_shapes=list(scratch.values()),
        compiler_params=pltpu.CompilerParams(vmem_limit_bytes=63 * 2**20),
    )(lengths, tokens, cotangent, packed, vecs)


BOTH = ("dp", "fsdp")


def general(lengths, tokens, cotangent, vectors, weights):
    whole = lambda v, axis: lax.all_gather(v, BOTH, axis=axis, tiled=True)
    w_all = [whole(w, 1) for w in weights]
    v_all = [whole(v, v.ndim - 1) for v in vectors]
    layers, width, _ = w_all[1].shape
    groups = group_shape(width, w_all[2].shape[2])
    blocks = []
    for w in w_all[:3]:
        cut = w.reshape((layers,) + groups + (GROUP, -1, width))
        blocks.append(jnp.moveaxis(cut, -2, -3).reshape((layers,) + groups + (-1, width)))
    blocks.append(w_all[3].reshape((layers,) + groups + (-1, width)))
    vecs = jnp.concatenate([v.reshape(layers, -1, width) for v in v_all], axis=1).astype(F32)
    mixed, grad_tokens, grads, vgrads = plain(
        lengths, tokens, cotangent, jnp.concatenate(blocks, axis=-2), vecs
    )
    reduce = lambda g, axis: lax.psum_scatter(g, BOTH, scatter_dimension=axis, tiled=True)
    w_grads, first = [], 0
    for n, (w, block) in enumerate(zip(w_all, blocks)):
        part = grads[..., first : first + block.shape[-2], :].astype(F32)
        first += block.shape[-2]
        if n < 3:
            part = part.reshape((layers,) + groups + (-1, GROUP, width))
            part = jnp.moveaxis(part, -3, -2)
        w_grads.append(reduce(part.reshape(w.shape), 1))
    v_grads, first = [], 0
    for v in v_all:
        count = v.size // (layers * width)
        part = vgrads[:, first : first + count].reshape(v.shape)
        first += count
        v_grads.append(reduce(part, v.ndim - 1))
    return mixed, grad_tokens, v_grads, w_grads


def on_device(mesh, tokens, lengths, *rest):
    gains, shifts, w_qkv, b_qkv, w_attn, blends, w_in, b_in, w_out, biases, cotangent = rest
    vectors = (gains, shifts, b_qkv, blends, b_in, biases)
    weights = (w_qkv, w_attn, w_in, w_out)
    layers, _, width = w_attn.shape
    groups = group_shape(width, w_in.shape[2])
    if (mesh.shape["dp"], mesh.shape["fsdp"]) == (groups[0] * groups[1], groups[2] * groups[3]):
        mixed, grad_tokens, tile, *w_grads = fused(
            lengths, tokens, cotangent, vectors, weights
        )
        large, v_grads = finish(
            Vectors(layers, width, w_in.shape[2]),
            (mixed, grad_tokens, *w_grads),
            tile,
            [v.shape for v in vectors],
        )
        mixed, grad_tokens, *w_grads = large
    else:
        mixed, grad_tokens, v_grads, w_grads = general(
            lengths, tokens, cotangent, vectors, weights
        )
    d_gains, d_shifts, d_b_qkv, d_blends, d_b_in, d_biases = v_grads
    d_w_qkv, d_w_attn, d_w_in, d_w_out = w_grads
    return (
        mixed,
        grad_tokens,
        d_gains,
        d_shifts,
        d_w_qkv,
        d_b_qkv,
        d_w_attn,
        d_blends,
        d_w_in,
        d_b_in,
        d_w_out,
        d_biases,
    )


def solution(mesh):
    rows, vector = P(BOTH, None), P(None, None, BOTH)
    weight, bias = P(None, BOTH, None), P(None, BOTH)
    in_specs = (
        rows,
        P(BOTH),
        vector,
        vector,
        weight,
        bias,
        weight,
        vector,
        weight,
        bias,
        weight,
        vector,
        rows,
    )
    out_specs = (
        rows,
        rows,
        vector,
        vector,
        weight,
        bias,
        weight,
        vector,
        weight,
        bias,
        weight,
        vector,
    )
    return jax.shard_map(
        functools.partial(on_device, mesh),
        mesh=mesh,
        in_specs=in_specs,
        out_specs=out_specs,
        check_vma=False,
    )
```

```python
import functools
import itertools
import jax
import jax.numpy as jnp
from jax import lax
from jax.experimental import pallas as pl
from jax.experimental.pallas import tpu as pltpu
from jax.sharding import PartitionSpec as P

HD = 64
BAND = 30
EPSILON = 1e-05
MESH = pl.DeviceIdType.MESH
F32 = jnp.float32
BF16 = jnp.bfloat16
GROUP = 16
TILE = 128
PAD = 32
WINDOW = TILE + 2 * PAD
TWINS = {"acc_t": "acc", "gm_t": "normed"}
STEP = 2
ROWS = 512
GELU_C = 0.7978845608028654
GELU_A = 0.044715
GAIN, SHIFT, BQKV, BLEND, BIN, OBIAS, VROWS = 0, 2, 4, 7, 10, 14, 16
VECTOR_ROWS = (GAIN, SHIFT, BQKV, BLEND, BIN, OBIAS)


def nn(a, b):
    return jnp.dot(a, b, preferred_element_type=F32)


def nt(a, b):
    return lax.dot_general(a, b, (((1,), (1,)), ((), ())), preferred_element_type=F32)


def split(a):
    high = a.astype(BF16)
    return high, (a - high.astype(F32)).astype(BF16)


def row_index(shape):
    return lax.broadcasted_iota(jnp.int32, shape, 0)


def col_index(shape):
    return lax.broadcasted_iota(jnp.int32, shape, 1)


def head_diag(a):
    return jnp.where((row_index(a.shape) < HD) == (col_index(a.shape) < HD), a, 0.0)


def spread(tile):
    top, bottom = tile[:HD], tile[HD:]
    zero = jnp.zeros_like(top)
    return jnp.concatenate(
        [jnp.concatenate([top, zero], axis=1), jnp.concatenate([zero, bottom], axis=1)], axis=0
    )


def fold(wide):
    half = wide.shape[1] // 2
    return jnp.concatenate([wide[:HD, :half], wide[HD:, half:]], axis=0)


def col_sum(a):
    return jnp.sum(a, axis=0, keepdims=True)


GBLEND = 64


def group_shape(width, hidden):
    first = hidden // width
    return (first, width // GROUP // first // 4, 2, 2)


class Net:
    def __init__(self, layers, seq, width, hidden, length, r):
        self.layers, self.seq, self.width, self.hidden = layers, seq, width, hidden
        self.pairs = width // (2 * HD)
        self.tiles = seq // TILE
        self.length = length
        self.padded = seq + TILE
        self.ff_blocks = hidden // width
        self.groups = group_shape(width, hidden)
        self.__dict__.update(r)
        for name, twin in TWINS.items():
            if name not in r:
                setattr(self, name, r[twin])

    @staticmethod
    def scratch(layers, seq, width, hidden):
        padded = seq + TILE
        pairs = width // (2 * HD)
        tiles = seq // TILE
        ff = hidden // width
        v = pltpu.VMEM
        arrays = dict(
            acc=v((seq, width), F32),
            acc_t=v((width, seq), F32),
            xhat=v((layers, 2, seq, width), BF16),
            rstd=v((seq, 128), F32),
            normed=v((seq, width), BF16),
            normed_t=v((layers, 2, width, seq), BF16),
            q_t=v((layers, width, seq), BF16),
            k_pad=v((layers, padded, width), BF16),
            v_pad=v((layers, padded, width), BF16),
            tr_pad=v((width, padded), BF16),
            probs=v((layers, pairs, tiles, WINDOW, 2 * TILE), BF16),
            near_t=v((layers, width, seq), BF16),
            tanh_t=v((layers, width, seq), BF16),
            s_one=v((layers, pairs, 2 * HD, 2 * HD), F32),
            s_two=v((layers, pairs, 2 * HD, 2 * HD), F32),
            rden=v((layers, pairs, 8, seq), F32),
            mixed_t=v((layers, width, seq), BF16),
            act_t=v((layers, ff, width, seq), BF16),
            dact=v((layers, ff, seq, width), BF16),
            band=v((tiles, WINDOW, 2 * TILE), BF16),
            cols=v((width, 128), F32),
            gm_t=v((width, seq), BF16),
            gk_pad=v((padded, width), F32),
            gv_pad=v((padded, width), F32),
            vecs=v((layers, VROWS, width), F32),
            vgrads=v((layers, VROWS, width), F32),
        )
        return {n: a for n, a in arrays.items() if seq != width or n not in TWINS}

    def w_rows(self, l, first):
        return self.packed[l, :, :, :, :, pl.ds(first, GROUP), :].reshape(self.width, self.width)

    def w_qkv(self, l, n):
        return self.w_rows(l, GROUP * n)

    def w_attn(self, l):
        return self.w_rows(l, 3 * GROUP)

    def w_in(self, l, j):
        return self.w_rows(l, pl.multiple_of(4 * GROUP + GROUP * j, GROUP))

    def out_at(self, j):
        per = self.hidden // (self.width // GROUP)
        return j, pl.ds((4 + self.ff_blocks) * GROUP, per)

    def w_out(self, l, j):
        groups, rows = self.out_at(j)
        return self.packed[l, groups, :, :, :, rows, :].reshape(self.width, self.width)

    def put_rows(self, l, first, value):
        self.grads[:, :, :, :, pl.ds(first, GROUP), :] = value.astype(BF16).reshape(
            self.groups + (GROUP, self.width)
        )

    def put_out(self, l, j, value):
        groups, rows = self.out_at(j)
        per = self.hidden // (self.width // GROUP)
        self.grads[groups, :, :, :, rows, :] = value.astype(BF16).reshape(
            self.groups[1:] + (per, self.width)
        )

    def vec(self, l, row):
        return self.vecs[l, pl.ds(row, 1), :]

    def keep(self, value):
        return jnp.where(row_index(value.shape) < self.length, value, 0.0)

    def setup(self):
        shape = (WINDOW, 2 * TILE)
        key, query = row_index(shape) - PAD, col_index(shape) % TILE
        for t in range(self.tiles):
            pos = key + t * TILE
            ok = (jnp.abs(key - query) <= BAND) & (pos >= 0)
            ok = ok & ((pos < self.length) | (key == query))
            self.band[t] = jnp.where(ok, 0.0, -1e30).astype(BF16)
        zero_head = jnp.zeros((PAD, self.width), BF16)
        zero_tail = jnp.zeros((self.padded - PAD - self.seq, self.width), BF16)
        for l in range(self.layers):
            for ref in (self.k_pad, self.v_pad):
                ref[l, :PAD] = zero_head
                ref[l, PAD + self.seq :] = zero_tail

    def setup_vecs(self):
        eye = (row_index((self.width, self.width)) == col_index((self.width, self.width))).astype(
            BF16
        )
        for l in range(self.layers):
            self.cols[:, VROWS * l : VROWS * (l + 1)] = nt(eye, self.vecs[l].astype(BF16))

    def rows(self, body):
        @pl.loop(0, self.seq // ROWS)
        def _(i):
            body(pl.ds(pl.multiple_of(i * ROWS, ROWS), ROWS))

    def norm(self, l, which, source):
        def body(at):
            value = source[at, :]
            centered = value - jnp.mean(value, axis=-1, keepdims=True)
            rstd = lax.rsqrt(jnp.mean(centered * centered, axis=-1, keepdims=True) + EPSILON)
            xhat = centered * rstd
            n = 2 * l + which
            self.rstd[at, n : n + 1] = rstd
            self.xhat[l, which, at, :] = xhat.astype(BF16)
            normed = xhat * self.vec(l, GAIN + which) + self.vec(l, SHIFT + which)
            self.normed[at, :] = normed.astype(BF16)

        self.rows(body)
        self.normed_t[l, which] = self.normed[...].T

    def pad_keep(self):
        row = row_index((self.padded, 2 * HD)) - PAD
        return (row >= 0) & (row < self.length)

    def fwd_qkv(self, l, n):
        out = (nn(self.normed[...], self.w_qkv(l, n)) + self.vec(l, BQKV + n)).astype(BF16)
        if n == 0:
            self.q_t[l] = out.T
        else:
            (self.k_pad, self.v_pad)[n - 1][l, PAD : PAD + self.seq] = out
        if n == 2:
            self.tr_pad[...] = self.v_pad[l].T

    def pair_at(self, p):
        return pl.ds(pl.multiple_of(p * 2 * HD, 2 * HD), 2 * HD)

    def fwd_near(self, l, p):
        at = self.pair_at(p)
        spans = [
            (slice(t * TILE, (t + 1) * TILE), slice(t * TILE, t * TILE + WINDOW))
            for t in range(self.tiles)
        ]
        scores = [nn(self.k_pad[l, window, at], spread(self.q_t[l, at, here])) for here, window in spans]
        for t, (here, window) in enumerate(spans):
            one = scores[t] * (HD**-0.5) + self.band[t].astype(F32)
            weights = jnp.exp(one - jnp.max(one, axis=0, keepdims=True))
            inverse = 1.0 / jnp.sum(weights, axis=0, keepdims=True)
            probs = (weights * inverse).astype(BF16)
            self.probs[l, p, t] = probs
        for t, (here, window) in enumerate(spans):
            near = fold(nn(self.tr_pad[at, window], self.probs[l, p, t]))
            self.near_t[l, at, here] = near.astype(BF16)

    def features(self, x):
        grown = jnp.exp(jnp.minimum(x, 0.0))
        return jnp.where(x > 0, x + 1.0, grown), grown, jnp.tanh(x)

    def key_features(self, l, at):
        phi, slope, tanh = self.features(self.k_pad[l, :, at].astype(F32))
        ok = self.pad_keep()
        return (
            jnp.where(ok, phi, 0.0).astype(BF16),
            slope,
            jnp.where(ok, tanh, 0.0).astype(BF16),
            tanh,
        )

    def coefficient(self):
        wide = jnp.full((1, 1), HD, F32) * self.length.astype(F32)
        return lax.rsqrt(wide)

    def heads_row(self, two, seq):
        return jnp.concatenate(
            [
                jnp.broadcast_to(two[0:1], (HD, seq)),
                jnp.broadcast_to(two[1:2], (HD, seq)),
            ],
            axis=0,
        )

    def fwd_far(self, l, p):
        at = self.pair_at(p)
        phk, _, tk, _ = self.key_features(l, at)
        values_t = self.tr_pad[at, :]
        s_one = head_diag(nn(values_t, phk))
        s_two = head_diag(nn(values_t, tk))
        total = col_sum(phk.astype(F32))
        self.s_one[l, p], self.s_two[l, p] = s_one, s_two
        phi, _, tanh = self.features(self.q_t[l, at, :].astype(F32))
        phq, tq = phi.astype(BF16), tanh.astype(BF16)
        shape = (8, 2 * HD)
        mine = (row_index(shape) == 0) == (col_index(shape) < HD)
        z_high, z_low = split(jnp.where(mine & (row_index(shape) < 2), total, 0.0))
        den = nn(z_high, phq) + nn(z_low, phq)
        rden = 1.0 / jnp.where(row_index(den.shape) < 2, den, 1.0)
        self.rden[l, p] = rden
        total_col = jnp.broadcast_to(total, (8, 2 * HD)).T
        n = VROWS * l
        self.cols[at, n : n + 1] = total_col[:, 0:1]
        high, low = split(s_one)
        far_elu = (nn(high, phq) + nn(low, phq)) * self.heads_row(rden, self.seq)
        high, low = split(s_two)
        far_tanh = (nn(high, tq) + nn(low, tq)) * self.coefficient()
        self.tanh_t[l, at, :] = far_tanh.astype(BF16)
        blend = self.cols[at, VROWS * l : VROWS * (l + 1)]
        self.mixed_t[l, at, :] = (
            blend[:, BLEND : BLEND + 1] * self.near_t[l, at, :].astype(F32)
            + blend[:, BLEND + 1 : BLEND + 2] * far_elu
            + blend[:, BLEND + 2 : BLEND + 3] * far_tanh
        ).astype(BF16)

    def fwd_attn(self, l):
        mixed = self.mixed_t[l].T
        out = nn(mixed, self.w_attn(l)) + self.vec(l, OBIAS)
        self.gk_pad[: self.seq] = self.h[...] + self.keep(out)
        self.norm(l, 1, self.gk_pad)

    def fwd_up(self, l, j):
        pre = nn(self.normed[...], self.w_in(l, j)) + self.vec(l, BIN + j)
        square = pre * pre
        th = jnp.tanh(GELU_C * pre * (1.0 + GELU_A * square))
        half = 0.5 * (1.0 + th)
        slope = half + (0.5 * GELU_C) * pre * (1.0 - th * th) * (1.0 + 3.0 * GELU_A * square)
        self.dact[l, j] = slope.astype(BF16)
        self.act_t[l, j] = (pre * half).astype(BF16).T

    def fwd_down(self, l):
        self.acc[...] = jnp.broadcast_to(self.vec(l, OBIAS + 1), self.acc.shape)

        @pl.loop(0, self.ff_blocks)
        def _(j):
            self.acc[...] += nn(self.act_t[l, j].T, self.w_out(l, j))

    def fwd_end(self, l):
        self.h[...] = self.gk_pad[: self.seq] + self.keep(self.acc[...])

    def put_vec(self, l, row, value):
        self.vgrads[l, pl.ds(row, 1), :] = value

    def bwd_start(self, l, source):
        gz = self.keep(source[...].astype(F32)).astype(BF16)
        self.normed[...] = gz
        self.put_vec(l, OBIAS + 1, col_sum(gz.astype(F32)))

    def bwd_out(self, l, j):
        self.put_out(l, j, nn(self.act_t[l, j], self.normed[...]))

    def bwd_up(self, l, j):
        grad = nt(self.normed[...], self.w_out(l, j))
        gpre = (grad * self.dact[l, j].astype(F32)).astype(BF16)
        self.put_vec(l, BIN + j, col_sum(gpre.astype(F32)))
        first = pl.multiple_of(4 * GROUP + GROUP * j, GROUP)
        self.put_rows(l, first, nn(self.normed_t[l, 1], gpre))
        self.acc[...] += nt(gpre, self.w_in(l, j))

    def norm_back(self, l, which):
        self.put_vec(l, GAIN + which, jnp.zeros((1, self.width), F32))
        self.put_vec(l, SHIFT + which, jnp.zeros((1, self.width), F32))

        def body(at):
            grad = self.acc[at, :]
            xhat = self.xhat[l, which, at, :].astype(F32)
            self.vgrads[l, pl.ds(GAIN + which, 1), :] += col_sum(grad * xhat)
            self.vgrads[l, pl.ds(SHIFT + which, 1), :] += col_sum(grad)
            grad = grad * self.vec(l, GAIN + which)
            mean = jnp.mean(grad, axis=-1, keepdims=True)
            slope = jnp.mean(grad * xhat, axis=-1, keepdims=True)
            n = 2 * l + which
            self.h[at, :] += self.rstd[at, n : n + 1] * (grad - mean - xhat * slope)

        self.rows(body)

    def bwd_attn(self, l):
        self.norm_back(l, 1)
        go = self.keep(self.h[...]).astype(BF16)
        self.put_vec(l, OBIAS, col_sum(go.astype(F32)))
        self.put_rows(l, 3 * GROUP, nn(self.mixed_t[l], go))
        self.gm_t[...] = nt(self.w_attn(l), go).astype(BF16)
        self.tr_pad[...] = self.k_pad[l].T
        self.gk_pad[...] = jnp.zeros_like(self.gk_pad)
        self.gv_pad[...] = jnp.zeros_like(self.gv_pad)

    def bwd_near(self, l, p):
        at = self.pair_at(p)
        blend = self.cols[at, VROWS * l : VROWS * (l + 1)]
        spans = [
            (slice(t * TILE, (t + 1) * TILE), slice(t * TILE, t * TILE + WINDOW))
            for t in range(self.tiles)
        ]
        grads = []
        for here, _ in spans:
            grad = blend[:, BLEND : BLEND + 1] * self.gm_t[at, here].astype(F32)
            grads.append(spread(grad.astype(BF16)))
        dprobs = [nn(self.v_pad[l, window, at], g) for g, (_, window) in zip(grads, spans)]
        terms = []
        for t in range(self.tiles):
            wide = self.probs[l, p, t].astype(F32)
            term = wide * dprobs[t]
            inner = jnp.sum(term, axis=0, keepdims=True)
            terms.append(((term - wide * inner) * (HD**-0.5)).astype(BF16))
        for gs, (here, window) in zip(terms, spans):
            self.acc_t[at, here] = fold(nn(self.tr_pad[at, window], gs))
        keys = [nt(gs, spread(self.q_t[l, at, here])) for gs, (here, _) in zip(terms, spans)]
        values = [nt(self.probs[l, p, t], grads[t]) for t in range(self.tiles)]
        for t, (_, window) in enumerate(spans):
            self.gk_pad[window, at] += keys[t]
            self.gv_pad[window, at] += values[t]

    def bwd_far(self, l, p):
        at = self.pair_at(p)
        seq = self.seq
        blend = self.cols[at, VROWS * l : VROWS * (l + 1)]
        gm = self.gm_t[at, :].astype(F32)
        q = self.q_t[l, at, :].astype(F32)
        phi_q, slope_q, tanh_q = self.features(q)
        phq, tq = phi_q.astype(BF16), tanh_q.astype(BF16)
        high, low = split(self.s_one[l, p])
        far_elu = (nn(high, phq) + nn(low, phq)) * self.heads_row(self.rden[l, p], seq)
        column = lambda a: jnp.sum(a, axis=1, keepdims=True)
        sums = [
            column(gm * self.near_t[l, at, :].astype(F32)),
            column(gm * far_elu),
            column(gm * self.tanh_t[l, at, :].astype(F32)),
        ]
        for n, one in enumerate(sums):
            self.cols[at, GBLEND + n : GBLEND + n + 1] = one
        phk, slope_k, tk, tanh_k = self.key_features(l, at)
        values = self.v_pad[l, :, at]
        gnum = (blend[:, BLEND + 1 : BLEND + 2] * gm * self.heads_row(self.rden[l, p], seq)).astype(
            BF16
        )
        prod = gnum.astype(F32) * far_elu
        gden_one = -col_sum(prod[:HD])
        gden_two = -col_sum(prod[HD:])
        gden = jnp.concatenate([gden_one, gden_two, jnp.zeros((6, seq), F32)], axis=0)
        s_one = self.s_one[l, p].T
        high, low = split(s_one)
        gphq = nn(high, gnum) + nn(low, gnum) + self.cols[at, VROWS * l : VROWS * l + 1] * self.heads_row(gden, seq)
        gs_one = head_diag(nt(phq, gnum))
        gs_high, gs_low = split(gs_one)
        gden_high, gden_low = split(gden)
        both = nt(gden_high, phq) + nt(gden_low, phq)
        gzz = jnp.where(col_index((1, 2 * HD)) < HD, both[0:1], both[1:2])
        gtanh = (blend[:, BLEND + 2 : BLEND + 3] * gm * self.coefficient()).astype(BF16)
        gtq = nn(self.s_two[l, p].T.astype(BF16), gtanh)
        gs_two = head_diag(nt(tq, gtanh)).astype(BF16)
        self.acc_t[at, :] += gphq * jnp.where(q > 0, 1.0, slope_q) + gtq * (1.0 - tanh_q * tanh_q)
        gphk = nt(values, gs_high) + nt(values, gs_low) + gzz
        gtk = nt(values, gs_two)
        grad_k = gphk * slope_k + gtk * (1.0 - tanh_k * tanh_k)
        self.gk_pad[:, at] += jnp.where(self.pad_keep(), grad_k, 0.0)
        self.gv_pad[:, at] += nn(phk, gs_high) + nn(tk, gs_two)

    def bwd_qkv(self, l, n):
        rows = slice(PAD, PAD + self.seq)
        if n == 0:
            grad = self.acc_t[...].T.astype(BF16)
        else:
            grad = (self.gk_pad, self.gv_pad)[n - 1][rows, :].astype(BF16)
        self.put_vec(l, BQKV + n, col_sum(grad.astype(F32)))
        self.put_rows(l, GROUP * n, nn(self.normed_t[l, 0], grad))
        total = self.gv_pad.at[rows]
        part = nt(grad, self.w_qkv(l, n))
        if n == 2:
            total[...] = part
        elif n == 1:
            total[...] += part
        else:
            self.acc[...] = total[...] + part

    def bwd_end(self, l):
        self.vgrads[l, pl.ds(BLEND, 3), :] = self.cols[...].T[GBLEND : GBLEND + 3]
        self.norm_back(l, 0)


class Comm:
    def __init__(self, depth, sems):
        self.sems = sems
        self.free = ([], [])
        self.made = [0, 0]
        self.clock = 0
        self.heard = {}
        dp, fsdp = lax.axis_index("dp"), lax.axis_index("fsdp")
        self.depth = depth
        self.at = {"z": dp // 2, "x": dp % 2, "y": fsdp // 2, "c": fsdp % 2}

    def device(self, **moved):
        at = dict(self.at, **moved)
        return (at["z"] * 2 + at["x"], at["y"] * 2 + at["c"])

    def steps(self, axis):
        return range(1, self.depth) if axis == "z" else range(1, 2)

    def other(self, axis, step=1):
        if axis == "z":
            return lax.rem(self.at["z"] + step, self.depth)
        return 1 - self.at[axis]

    def barrier(self):
        semaphore = pltpu.get_barrier_semaphore()
        peers = [
            self.device(**{axis: self.other(axis, k)}) for axis in "zxyc" for k in self.steps(axis)
        ]
        for peer in peers:
            pl.semaphore_signal(semaphore, inc=1, device_id=peer, device_id_type=MESH)
        pl.semaphore_wait(semaphore, len(peers))

    def take(self, side, before):
        for entry in self.free[side]:
            if entry[0] < before:
                self.free[side].remove(entry)
                return entry[1]
        self.made[side] += 1
        return self.made[side] - 1

    def copy(self, source, target, axis, step):
        self.clock += 1
        sent = self.take(0, self.clock)
        arrived = self.take(1, self.heard.get((axis, step), -1))
        made = pltpu.make_async_remote_copy(
            src_ref=source,
            dst_ref=target,
            send_sem=self.sems[0].at[sent],
            recv_sem=self.sems[1].at[arrived],
            device_id=self.device(**{axis: self.other(axis, step)}),
            device_id_type=MESH,
        )
        made.start()
        back = (axis, self.depth - step if axis == "z" else 1)
        return made, sent, arrived, back, self.clock

    def wait(self, copies):
        for made, sent, arrived, back, when in copies:
            made.wait()
            self.clock += 1
            self.free[0].append((self.clock, sent))
            self.free[1].append((self.clock, arrived))
            self.heard[back] = max(when, self.heard.get(back, -1))

    def index(self, whole, moved=None):
        at = dict(self.at, **(moved or {}))
        return tuple(slice(None) if axis in whole else at[axis] for axis in "zxyc")

    def gather(self, view, order):
        cores = []
        for stage in range(4):
            whole, started = order[:stage], []
            if stage < 3:
                axis = order[stage]
                block = view(self.index(whole))
                started = [self.copy(block, block, axis, k) for k in self.steps(axis)]
            if "z" in whole:
                axis = order[stage - 1]
                if axis == "z":
                    block = view(self.index(whole))
                else:
                    block = view(self.index(order[: stage - 1], {axis: self.other(axis)}))
                cores.append(self.copy(block, block, "c", 1))
            yield
            self.wait(started)
        self.wait(cores)

    @staticmethod
    def add(mine, others):
        @pl.loop(0, mine.shape[0])
        def _(n):
            for rest in itertools.product(*[range(m) for m in mine.shape[1:-2]]):
                at = (n,) + rest
                total = mine[at]
                for other in others:
                    total = total + other[at]
                mine[at] = total

    def scatter(self, view, slot, order, put):
        axes = "c" + order
        for stage, axis in enumerate(axes):
            whole = axes[stage + 1 :]
            started = []
            for k in self.steps(axis):
                block = view(self.index(whole, {axis: self.other(axis, k)}))
                started.append(self.copy(block, slot(stage, k - 1), axis, k))
            yield
            self.wait(started)
            mine = view(self.index(whole))
            arrived = [slot(stage, k - 1) for k in self.steps(axis)]
            if whole:
                self.add(mine, arrived)
            else:
                total = mine[...].astype(F32)
                for one in arrived:
                    total = total + one[...].astype(F32)
                put(total)


ORDERS = {
    ("gather", 0): (
        (2, "zyx"), (7, "zyx"), (5, "zxy"), (1, "zyx"),
        (8, "zxy"), (0, "zyx"), (4, "zyx"), (10, "zyx"),
        (3, "xzy"), (9, "zxy"), (11, "xzy"), (6, "zxy"),
    ),
    ("gather", 1): (
        (2, "zxy"), (6, "zyx"), (0, "yzx"), (1, "yzx"),
        (3, "xzy"), (7, "xzy"), (4, "yzx"), (5, "xzy"),
        (9, "zxy"), (10, "yzx"), (8, "zyx"), (11, "xzy"),
    ),
    ("scatter", 0): (
        (6, "xzy"), (9, "xzy"), (2, "xyz"), (8, "yxz"),
        (11, "yxz"), (10, "xzy"), (3, "yxz"), (5, "yxz"),
        (0, "xyz"), (4, "yxz"), (7, "yzx"), (1, "yxz"),
    ),
    ("scatter", 1): (
        (1, "xzy"), (0, "xzy"), (5, "yzx"), (7, "yxz"),
        (4, "yxz"), (9, "yxz"), (6, "xyz"), (10, "xzy"),
        (2, "yxz"), (3, "xzy"), (11, "yzx"), (8, "xzy"),
    ),
}
LINK, HOP = 0.0235, 2.0
CORE, CORE_HOP = 0.0027, 0.9
ISSUE, BACKLOG, AHEAD = 0.04, 5.0, 13


def plan(layers, segments, parts):
    size = {"z": 4, "x": 2, "y": 2, "c": 2}
    free = dict.fromkeys("zxyc", 0.0)
    clock, steps = 0.0, []
    stage = dict.fromkeys(parts, 0)
    ready = {n: 0.0 if not scatter else None for n, (_, _, scatter) in parts.items()}
    done = set()
    waiting = list(segments)

    def send(axis, blocks, rows):
        link, hop = (CORE, CORE_HOP) if axis == "c" else (LINK, HOP)
        load = blocks * rows * link * (size["z"] if axis == "z" else 1)
        free[axis] = max(free[axis], clock) + load
        return free[axis] + hop

    def count(axes):
        total = 1
        for axis in axes:
            total *= size[axis]
        return total

    def step(name):
        nonlocal clock
        rows, order, scatter = parts[name]
        now = stage[name]
        steps.append((name,))
        stage[name] += 1
        last = 4
        if scatter:
            axes = "c" + order
            if now > 0:
                clock += 0.02 + count(axes[now:]) * rows * 0.0002
            if now < last:
                arrives = send(axes[now], count(axes[now + 1 :]), rows)
                clock += ISSUE * (3 if axes[now] == "z" else 1)
        else:
            arrives = ready[name]
            if now < 3:
                arrives = send(order[now], count(order[:now]), rows)
                clock += ISSUE * (3 if order[now] == "z" else 1)
            if "z" in order[:now] and now < last:
                whole = order[:now] if order[now - 1] == "z" else order[: now - 1]
                core = send("c", count(whole), rows)
                clock += ISSUE
                if now == 3:
                    arrives = core
        if now == last:
            done.add(name)
            ready[name] = None
        else:
            ready[name] = arrives

    def startable(name):
        _, order, scatter = parts[name]
        first = "c" if scatter else order[0]
        return stage[name] > 0 or free[first] <= clock + BACKLOG

    while len(done) < len(parts) or waiting:
        left = [n for n in parts if n not in done][:AHEAD]
        able = [n for n in left if ready[n] is not None and ready[n] <= clock and startable(n)]
        if able:
            step(able[0])
            continue
        if waiting:
            name, layer, argument, cost, needs, makes = waiting[0]
            if all(n in done for n in needs):
                waiting.pop(0)
                steps.append((name, layer, argument))
                clock += cost
                for n in makes:
                    ready[n] = clock
                continue
        later = [ready[n] for n in left if ready[n] is not None and ready[n] > clock]
        later += [free[a] - BACKLOG for a in "zxyc" if free[a] - BACKLOG > clock]
        clock = min(later)
    return steps, clock


def make_plan(layers, pairs, ff, rows):
    units = rows // GROUP
    parts = {("gather", 0, "vectors"): (4, "zxy", False)}
    for l in range(layers):
        for u, order in ORDERS["gather", l]:
            parts["gather", l, u] = (GROUP, order, False)
    for l in reversed(range(layers)):
        for u, order in ORDERS["scatter", l]:
            parts["scatter", l, u] = (GROUP, order, True)
    parts["scatter", 0, "vectors"] = (8, "yxz", True)
    gathers = lambda l, us: [("gather", l, u) for u in us]
    scatters = lambda l, us: [("scatter", l, u) for u in us]
    downs = range(units - ff, units)
    segments = []
    add = lambda *s: segments.append(s)
    halves = [(0, pairs)]
    twos = [(j, min(j + STEP, ff)) for j in range(0, ff, STEP)]
    add("start", 0, None, 0.5, [], [])
    add("spread", 0, None, 0.5, [("gather", 0, "vectors")], [])
    for l in range(layers):
        add("norm", l, 0, 0.7, [], [])
        for n in range(3):
            add("fwd_qkv", l, n, 0.25, gathers(l, [n]), [])
        for half in halves:
            add("fwd_near", l, half, 2.6, [], [])
        for half in halves:
            add("fwd_far", l, half, 2.3, [], [])
        add("fwd_attn", l, None, 1.3, gathers(l, [3]), [])
        for j, end in twos:
            add("fwd_up", l, (j, end), 1.05 * (end - j), gathers(l, range(4 + j, 4 + end)), [])
        if l == layers - 1:
            add("bwd_start", l, None, 0.3, [], [])
            add("bwd_out", l, (0, ff), 0.43 * ff, [], scatters(l, downs))
        add("fwd_down", l, None, 1.9, gathers(l, downs), [])
    for l in reversed(range(layers)):
        again = lambda us: scatters(l + 1, us) if l < layers - 1 else []
        if l < layers - 1:
            add("bwd_start", l, None, 0.3, [], [])
            add("bwd_out", l, (0, ff), 0.43 * ff, again(downs), scatters(l, downs))
        for j, end in twos:
            units = range(4 + j, 4 + end)
            add("bwd_up", l, (j, end), 1.33 * (end - j), again(units), scatters(l, units))
        add("bwd_attn", l, None, 1.6, again([3]), scatters(l, [3]))
        for half in halves:
            add("bwd_near", l, half, 3.1, [], [])
        for half in halves:
            add("bwd_far", l, half, 3.8, [], [])
        for n in (2, 1, 0):
            add("bwd_qkv", l, n, 0.6, again([n]), scatters(l, [n]))
        add("bwd_end", l, None, 0.9, [], [])
    add("collect", 0, None, 0.5, [], scatters(0, ["vectors"]))
    return plan(layers, segments, parts), parts


class Vectors:
    def __init__(self, layers, width, hidden):
        self.layers, self.width = layers, width
        self.devices = width // GROUP
        self.long = [(BQKV, 3), (BIN, hidden // width)]

    def swap(self, tiles, back):
        lane = lax.broadcasted_iota(jnp.int32, tiles.shape, 2)
        result = tiles
        for l in range(self.layers):
            for row, count in self.long:
                first = l * VROWS + row
                columns = [tiles[:, :, first + n : first + n + 1] for n in range(count)]
                if back:
                    both = jnp.stack(columns, axis=1).reshape(count, self.devices, GROUP, 1)
                    columns = [both[n] for n in range(count)]
                else:
                    both = jnp.concatenate(columns, axis=0)
                    both = both.reshape(self.devices, count, GROUP, 1)
                    columns = [both[:, n] for n in range(count)]
                for n in range(count):
                    result = jnp.where(lane == first + n, columns[n], result)
        return result

    def spread(self, shares, vecs, cols):
        tiles = shares[...].reshape(self.devices, GROUP, 128).astype(F32)
        columns = self.swap(tiles, True).reshape(self.width, 128)
        cols[...] = columns
        vecs[...] = columns.T[: self.layers * VROWS].reshape(vecs.shape)

    def collect(self, vgrads, shares):
        rows = vgrads[...].reshape(self.layers * VROWS, self.width)
        rest = jnp.zeros((128 - self.layers * VROWS, self.width), F32)
        columns = jnp.concatenate([rows, rest], axis=0).T
        tiles = self.swap(columns.reshape(self.devices, GROUP, 128), False)
        shares[...] = tiles.reshape(shares.shape)

    def pack(self, refs, table):
        table[...] = jnp.zeros_like(table)
        for l in range(self.layers):
            for ref, row in zip(refs, VECTOR_ROWS):
                turned = row == BLEND
                row += l * VROWS
                if turned:
                    for n in range(ref.shape[0]):
                        table[row + n : row + n + 1, :GROUP] = ref[n, l : l + 1, :].astype(F32)
                elif len(ref.shape) == 3:
                    table[row : row + ref.shape[1], :GROUP] = ref[l].astype(F32)
                else:
                    value = ref[l : l + 1, :].astype(F32)
                    for n in range(ref.shape[1] // GROUP):
                        piece = value[:, n * GROUP : (n + 1) * GROUP]
                        table[row + n : row + n + 1, :GROUP] = piece
        return table[...].T[:GROUP]

    def unpack(self, tile, table, refs):
        rest = jnp.zeros((128 - GROUP, 128), F32)
        table[...] = jnp.concatenate([tile, rest], axis=0).T
        for l in range(self.layers):
            for ref, row in zip(refs, VECTOR_ROWS):
                turned = row == BLEND
                row += l * VROWS
                if turned:
                    for n in range(ref.shape[0]):
                        ref[n, l : l + 1, :] = table[row + n : row + n + 1, :GROUP]
                elif len(ref.shape) == 3:
                    ref[l] = table[row : row + ref.shape[1], :GROUP]
                else:
                    count = ref.shape[1] // GROUP
                    rows = [table[row + n : row + n + 1, :GROUP] for n in range(count)]
                    ref[l : l + 1, :] = jnp.concatenate(rows, axis=1)


class Program:
    def __init__(self, net, comm, vectors, r):
        self.net, self.comm, self.vectors = net, comm, vectors
        self.__dict__.update(r)

    def fill(self):
        own = self.comm.index(())
        width = self.net.width
        for l in range(self.net.layers):
            first = 0
            for ref in (self.w_qkv, self.w_attn, self.w_in):
                for n in range(ref.shape[2] // width):
                    rows = pl.ds(first, GROUP)
                    self.net.packed[(l,) + own + (rows,)] = ref[l, :, n * width : (n + 1) * width]
                    first += GROUP
            rows = pl.ds(first, self.w_out.shape[1])
            self.net.packed[(l,) + own + (rows,)] = self.w_out[l]
        refs = [getattr(self, name) for name in VECTORS]
        self.shares[own] = self.vectors.pack(refs, self.table).astype(BF16)

    def gather(self, l, unit, order):
        if unit == "vectors":
            return self.comm.gather(lambda index: self.shares.at[index], order)
        at = pl.ds(unit * GROUP, GROUP)
        return self.comm.gather(lambda index: self.net.packed.at[(l,) + index + (at,)], order)

    def scatter(self, l, unit, order):
        if unit == "vectors":
            arrivals, at, source = self.varrivals, (), self.vshares
        else:
            at = (pl.ds(unit * GROUP, GROUP),)
            arrivals, source = self.arrivals, self.net.grads
        depth = self.comm.depth
        every = slice(None)

        def slot(stage, k):
            if stage < 2:
                return arrivals[stage].at[(every,) * (3 - stage) + at]
            if stage == 2:
                span = slice(2 * k, 2 * k + 2) if order[1] == "z" else slice(0, depth)
                return arrivals[2].at[(span,) + at]
            return arrivals[2].at[(2 * (depth - 1) if order[1] == "z" else depth + k,) + at]

        put = functools.partial(self.put, l, unit)
        return self.comm.scatter(lambda index: source.at[index + at], slot, order, put)

    def put(self, l, unit, total):
        if unit == "vectors":
            self.gsmall[...] = total
            return
        width = self.net.width
        for ref in (self.gw_qkv, self.gw_attn, self.gw_in):
            count = ref.shape[2] // width
            if unit < count:
                ref[l, :, unit * width : (unit + 1) * width] = total
                return
            unit -= count
        self.gw_out[l, unit * GROUP : (unit + 1) * GROUP, :] = total

    def start(self, l, _):
        self.net.setup()
        self.net.h[...] = self.tokens[...].astype(F32)

    def spread(self, l, _):
        self.vectors.spread(self.shares, self.net.vecs, self.net.cols)

    def collect(self, l, _):
        self.vectors.collect(self.net.vgrads, self.vshares)

    def norm(self, l, _):
        self.net.norm(l, 0, self.net.h)

    def fwd_attn(self, l, _):
        self.net.fwd_attn(l)

    def fwd_down(self, l, _):
        self.net.fwd_down(l)
        self.net.fwd_end(l)
        if l == self.net.layers - 1:
            self.mixed_out[...] = self.net.h[...].astype(BF16)
            self.net.h[...] = self.cotangent[...].astype(F32)

    def bwd_up(self, l, span):
        if span[0] == 0:
            self.net.acc[...] = jnp.zeros_like(self.net.acc)
        self.over(self.net.bwd_up, l, span)

    def bwd_start(self, l, _):
        self.net.bwd_start(l, self.cotangent if l == self.net.layers - 1 else self.net.h)

    def bwd_attn(self, l, _):
        self.net.bwd_attn(l)

    def bwd_end(self, l, _):
        self.net.bwd_end(l)

    def over(self, body, l, span):
        @pl.loop(*span)
        def _(p):
            body(l, p)

    def run(self):
        net = self.net
        rows = net.packed.shape[-2]
        (steps, _), parts = make_plan(net.layers, net.pairs, net.ff_blocks, rows)
        running = {}
        for (kind, l, unit), (_, order, _) in parts.items():
            make = self.gather if kind == "gather" else self.scatter
            running[kind, l, unit] = make(l, unit, order)
        self.fill()
        self.comm.barrier()
        for name, *rest in steps:
            if not rest:
                next(running[name], None)
            elif hasattr(self, name):
                getattr(self, name)(*rest)
            elif isinstance(rest[1], tuple):
                self.over(getattr(net, name), *rest)
            else:
                getattr(net, name)(*rest)
        assert max(self.comm.made) <= SEMAPHORES


VECTORS = ("gains", "shifts", "b_qkv", "blends", "b_in", "biases")
WEIGHTS = ("w_qkv", "w_attn", "w_in", "w_out")
INPUTS = ("tokens", "cotangent") + VECTORS + WEIGHTS
OUTPUTS = ("mixed_out", "h", "gsmall", "gw_qkv", "gw_attn", "gw_in", "gw_out")
SEMAPHORES = 96


def fused_body(sizes, depth, names, length_ref, *refs):
    named = dict(zip(INPUTS + OUTPUTS + names, refs))
    arrivals = [named.pop("arrive%d" % n) for n in range(3)]
    varrivals = [named.pop("varrive%d" % n) for n in range(3)]
    sems = named.pop("send"), named.pop("recv")
    inner = {n: r for n, r in named.items() if n not in INPUTS}
    net = Net(*sizes, length_ref[0], inner)
    comm = Comm(depth, sems)
    vectors = Vectors(sizes[0], sizes[2], sizes[3])
    Program(net, comm, vectors, dict(named, arrivals=arrivals, varrivals=varrivals)).run()


def fused(lengths, tokens, cotangent, vectors, weights):
    layers, _, width = weights[1].shape
    hidden = weights[2].shape[2]
    seq = tokens.shape[0]
    sizes = (layers, seq, width, hidden)
    rows = sum(w.shape[1] * w.shape[2] for w in weights) // width
    groups = group_shape(width, hidden)
    tile = (GROUP, 128)
    vmem = pl.BlockSpec(memory_space=pltpu.VMEM)
    scratch = dict(Net.scratch(*sizes))
    scratch["packed"] = pltpu.VMEM((layers,) + groups + (rows, width), BF16)
    scratch["grads"] = pltpu.VMEM(groups + (rows, width), BF16)
    scratch["shares"] = pltpu.VMEM(groups + tile, BF16)
    scratch["vshares"] = pltpu.VMEM(groups + tile, F32)
    scratch["table"] = pltpu.VMEM((128, 128), F32)
    kept = (groups[:3], groups[:2], (2 * groups[0] - 1,))
    for n, lead in enumerate(kept):
        scratch["arrive%d" % n] = pltpu.VMEM(lead + (rows, width), BF16)
        scratch["varrive%d" % n] = pltpu.VMEM(lead + tile, F32)
    scratch["send"] = pltpu.SemaphoreType.DMA((SEMAPHORES,))
    scratch["recv"] = pltpu.SemaphoreType.DMA((SEMAPHORES,))
    return pl.pallas_call(
        functools.partial(fused_body, sizes, groups[0], tuple(scratch)),
        out_shape=(
            jax.ShapeDtypeStruct(tokens.shape, BF16),
            jax.ShapeDtypeStruct(tokens.shape, F32),
            jax.ShapeDtypeStruct(tile, F32),
        )
        + tuple(jax.ShapeDtypeStruct(w.shape, F32) for w in weights),
        in_specs=[pl.BlockSpec(memory_space=pltpu.SMEM)] + [vmem] * len(INPUTS),
        out_specs=(vmem,) * len(OUTPUTS),
        scratch_shapes=list(scratch.values()),
        compiler_params=pltpu.CompilerParams(
            collective_id=0, has_side_effects=True, vmem_limit_bytes=63 * 2**20
        ),
    )(lengths, tokens, cotangent, *vectors, *weights)


def finish_body(vectors, big, *refs):
    sources, tile, refs = refs[:big], refs[big], refs[big + 1 :]
    targets, outs, table, sems = refs[:big], refs[big : -big - 2], refs[-big - 2], refs[-big - 1]
    buffers = refs[-big:]
    loads = [
        pltpu.make_async_copy(source, buffer, sems.at[0, n])
        for n, (source, buffer) in enumerate(zip(sources, buffers))
    ]
    stores = [
        pltpu.make_async_copy(buffer, target, sems.at[1, n])
        for n, (buffer, target) in enumerate(zip(buffers, targets))
    ]
    for one in loads:
        one.start()
    vectors.unpack(tile[...], table, outs)
    for load, store in zip(loads, stores):
        load.wait()
        store.start()
    for one in stores:
        one.wait()


def finish(vectors, large, tile, shapes):
    anywhere, vmem = pl.BlockSpec(memory_space=pl.ANY), pl.BlockSpec(memory_space=pltpu.VMEM)
    outs = pl.pallas_call(
        functools.partial(finish_body, vectors, len(large)),
        out_shape=tuple(jax.ShapeDtypeStruct(a.shape, a.dtype) for a in large)
        + tuple(jax.ShapeDtypeStruct(shape, F32) for shape in shapes),
        in_specs=[anywhere] * len(large) + [vmem],
        out_specs=(anywhere,) * len(large) + (vmem,) * len(shapes),
        scratch_shapes=[
            pltpu.VMEM((128, 128), F32),
            pltpu.SemaphoreType.DMA((2, len(large))),
        ]
        + [pltpu.VMEM(a.shape, a.dtype) for a in large],
        compiler_params=pltpu.CompilerParams(vmem_limit_bytes=62 * 2**20),
    )(*large, tile)
    return outs[: len(large)], outs[len(large) :]


def plain_body(sizes, names, length_ref, *refs):
    names = ("tokens", "cotangent", "packed", "vecs", "mixed_out", "h", "grads_out", "vgrads") + names
    named = dict(zip(names, refs))
    net = Net(*sizes, length_ref[0], named)

    def over(body, l):
        @pl.loop(0, net.pairs)
        def _(p):
            body(l, p)

    net.setup()
    net.setup_vecs()
    net.h[...] = named["tokens"][...].astype(F32)
    for l in range(net.layers):
        net.norm(l, 0, net.h)
        for n in range(3):
            net.fwd_qkv(l, n)
        over(net.fwd_near, l)
        over(net.fwd_far, l)
        net.fwd_attn(l)
        for j in range(net.ff_blocks):
            net.fwd_up(l, j)
        net.fwd_down(l)
        net.fwd_end(l)
    named["mixed_out"][...] = net.h[...].astype(BF16)
    net.h[...] = named["cotangent"][...].astype(F32)
    for l in reversed(range(net.layers)):
        net.bwd_start(l, net.h)
        net.acc[...] = jnp.zeros_like(net.acc)
        for j in range(net.ff_blocks):
            net.bwd_out(l, j)
            net.bwd_up(l, j)
        net.bwd_attn(l)
        over(net.bwd_near, l)
        over(net.bwd_far, l)
        for n in (2, 1, 0):
            net.bwd_qkv(l, n)
        net.bwd_end(l)
        copy = pltpu.make_async_copy(named["grads"], named["grads_out"].at[l], named["sem"])
        copy.start()
        copy.wait()


def plain(lengths, tokens, cotangent, packed, vecs):
    layers, rows, width = packed.shape[0], packed.shape[-2], packed.shape[-1]
    seq = tokens.shape[0]
    hidden = (rows // GROUP - 4) // 2 * width
    sizes = (layers, seq, width, hidden)
    scratch = dict(Net.scratch(*sizes))
    del scratch["vecs"], scratch["vgrads"]
    scratch["grads"] = pltpu.VMEM(packed.shape[1:], BF16)
    scratch["sem"] = pltpu.SemaphoreType.DMA
    vmem = pl.BlockSpec(memory_space=pltpu.VMEM)
    return pl.pallas_call(
        functools.partial(plain_body, sizes, tuple(scratch)),
        out_shape=(
            jax.ShapeDtypeStruct((seq, width), BF16),
            jax.ShapeDtypeStruct((seq, width), F32),
            jax.ShapeDtypeStruct(packed.shape, BF16),
            jax.ShapeDtypeStruct((layers, VROWS, width), F32),
        ),
        in_specs=[pl.BlockSpec(memory_space=pltpu.SMEM)] + [vmem] * 4,
        out_specs=(vmem, vmem, pl.BlockSpec(memory_space=pl.ANY), vmem),
        scratch_shapes=list(scratch.values()),
        compiler_params=pltpu.CompilerParams(vmem_limit_bytes=63 * 2**20),
    )(lengths, tokens, cotangent, packed, vecs)


BOTH = ("dp", "fsdp")


def general(lengths, tokens, cotangent, vectors, weights):
    whole = lambda v, axis: lax.all_gather(v, BOTH, axis=axis, tiled=True)
    w_all = [whole(w, 1) for w in weights]
    v_all = [whole(v, v.ndim - 1) for v in vectors]
    layers, width, _ = w_all[1].shape
    groups = group_shape(width, w_all[2].shape[2])
    blocks = []
    for w in w_all[:3]:
        cut = w.reshape((layers,) + groups + (GROUP, -1, width))
        blocks.append(jnp.moveaxis(cut, -2, -3).reshape((layers,) + groups + (-1, width)))
    blocks.append(w_all[3].reshape((layers,) + groups + (-1, width)))
    vecs = jnp.concatenate([v.reshape(layers, -1, width) for v in v_all], axis=1).astype(F32)
    mixed, grad_tokens, grads, vgrads = plain(
        lengths, tokens, cotangent, jnp.concatenate(blocks, axis=-2), vecs
    )
    reduce = lambda g, axis: lax.psum_scatter(g, BOTH, scatter_dimension=axis, tiled=True)
    w_grads, first = [], 0
    for n, (w, block) in enumerate(zip(w_all, blocks)):
        part = grads[..., first : first + block.shape[-2], :].astype(F32)
        first += block.shape[-2]
        if n < 3:
            part = part.reshape((layers,) + groups + (-1, GROUP, width))
            part = jnp.moveaxis(part, -3, -2)
        w_grads.append(reduce(part.reshape(w.shape), 1))
    v_grads, first = [], 0
    for v in v_all:
        count = v.size // (layers * width)
        part = vgrads[:, first : first + count].reshape(v.shape)
        first += count
        v_grads.append(reduce(part, v.ndim - 1))
    return mixed, grad_tokens, v_grads, w_grads


def on_device(mesh, tokens, lengths, *rest):
    gains, shifts, w_qkv, b_qkv, w_attn, blends, w_in, b_in, w_out, biases, cotangent = rest
    vectors = (gains, shifts, b_qkv, blends, b_in, biases)
    weights = (w_qkv, w_attn, w_in, w_out)
    layers, _, width = w_attn.shape
    groups = group_shape(width, w_in.shape[2])
    if (mesh.shape["dp"], mesh.shape["fsdp"]) == (groups[0] * groups[1], groups[2] * groups[3]):
        turn = lambda vs: [v.transpose(1, 0, 2) if n == 3 else v for n, v in enumerate(vs)]
        vectors = turn(vectors)
        mixed, grad_tokens, tile, *w_grads = fused(
            lengths, tokens, cotangent, vectors, weights
        )
        large, v_grads = finish(
            Vectors(layers, width, w_in.shape[2]),
            (mixed, grad_tokens, *w_grads),
            tile,
            [v.shape for v in vectors],
        )
        mixed, grad_tokens, *w_grads = large
        v_grads = turn(v_grads)
    else:
        mixed, grad_tokens, v_grads, w_grads = general(
            lengths, tokens, cotangent, vectors, weights
        )
    d_gains, d_shifts, d_b_qkv, d_blends, d_b_in, d_biases = v_grads
    d_w_qkv, d_w_attn, d_w_in, d_w_out = w_grads
    return (
        mixed,
        grad_tokens,
        d_gains,
        d_shifts,
        d_w_qkv,
        d_b_qkv,
        d_w_attn,
        d_blends,
        d_w_in,
        d_b_in,
        d_w_out,
        d_biases,
    )


def solution(mesh):
    rows, vector = P(BOTH, None), P(None, None, BOTH)
    weight, bias = P(None, BOTH, None), P(None, BOTH)
    in_specs = (
        rows,
        P(BOTH),
        vector,
        vector,
        weight,
        bias,
        weight,
        vector,
        weight,
        bias,
        weight,
        vector,
        rows,
    )
    out_specs = (
        rows,
        rows,
        vector,
        vector,
        weight,
        bias,
        weight,
        vector,
        weight,
        bias,
        weight,
        vector,
    )
    return jax.shard_map(
        functools.partial(on_device, mesh),
        mesh=mesh,
        in_specs=in_specs,
        out_specs=out_specs,
        check_vma=False,
    )
```
